32 devices in a mesh: shard: 2 (over y), ctx: 4 (over x, core), tp: 4 (over z).
Axes of the slice: x: 2, y: 2, z: 4, core: 2. Of those that a mesh axis runs over, the one named last changes fastest.
Arguments:
- inputs: bfloat16 [2, 4096, 1024], P('shard', 'ctx'), may hold values from -6 to 6
- cotangent: bfloat16 [2, 4096, 1024], P('shard', 'ctx'), may hold values from -6 to 6
- segments: int32 [2, 4096], P('shard'), may hold values from 0 to 4095, as said below
- adapter_index: int32 [2], P('shard'), may hold values from 0 to 7
- query_weight: bfloat16 [1024, 1024], P('shard', 'tp'), may hold values from -0.1875 to 0.1875
- key_value_weight: bfloat16 [2, 1024, 512], P(None, 'shard', 'tp'), may hold values from -0.1875 to 0.1875
- output_weight: bfloat16 [1024, 1024], P('tp', 'shard'), may hold values from -1 to 1
- gate_up_weight: bfloat16 [2, 1024, 4608], P(None, 'shard', 'tp'), may hold values from -0.1875 to 0.1875
- down_weight: bfloat16 [4608, 1024], P('tp', 'shard'), may hold values from -0.09375 to 0.09375
- norm_attn: float32 [1024], replicated, may hold values from 0.5 to 1.5
- norm_ffn: float32 [1024], replicated, may hold values from 0.5 to 1.5
- q_gain: float32 [64], replicated, may hold values from 0.8 to 2
- k_gain: float32 [64], replicated, may hold values from 0.8 to 2
- input_adapter_lower: bfloat16 [8, 1024, 80], replicated, may hold values from -0.1875 to 0.1875
- query_adapter_upper: bfloat16 [8, 16, 1024], P(None, None, 'tp'), may hold values from -0.75 to 0.75
- key_value_adapter_upper: bfloat16 [8, 2, 16, 512], P(None, None, None, 'tp'), may hold values from -0.75 to 0.75
- gate_up_adapter_upper: bfloat16 [8, 2, 16, 4608], P(None, None, None, 'tp'), may hold values from -0.75 to 0.75
- output_adapter_lower: bfloat16 [8, 1024, 16], P(None, 'tp'), may hold values from -1 to 1
- output_adapter_upper: bfloat16 [8, 16, 1024], replicated, may hold values from -0.75 to 0.75
- down_adapter_lower: bfloat16 [8, 4608, 16], P(None, 'tp'), may hold values from -0.09375 to 0.09375
- down_adapter_upper: bfloat16 [8, 16, 1024], replicated, may hold values from -0.75 to 0.75
Outputs:
- outputs: bfloat16 [2, 4096, 1024], P('shard', 'ctx')
- grad_inputs: float32 [2, 4096, 1024], P('shard', 'ctx')
- grad_adapt_in: float32 [8, 1024, 80], P(None, ('shard', 'ctx'))
- grad_b_query: float32 [8, 16, 1024], P(None, None, 'tp')
- grad_b_keyval: float32 [8, 2, 16, 512], P(None, None, None, 'tp')
- grad_b_gateup: float32 [8, 2, 16, 4608], P(None, None, None, 'tp')
- grad_a_out: float32 [8, 1024, 16], P(None, 'tp')
- grad_b_out: float32 [8, 16, 1024], replicated
- grad_a_down: float32 [8, 4608, 16], P(None, 'tp')
- grad_b_down: float32 [8, 16, 1024], replicated
The draws below stay inside these ranges and needn't reach their ends.
Inputs may be any that keep to these rules, and one draw needn't show every extreme that they name: `segments`: A token's segment number is the position in its packed sequence where its document starts, so numbers never fall along a sequence and begin at 0; the last token is a document of its own; in every sequence one document starts among the first 1024 positions and ends among the last 1024.
All inputs are finite; a program needn't handle non-finite values.
Results may differ from the reference program's by a relative error of at most 0.024.
Values may be sent and summed in bfloat16 or wider, within the bound.
No kernel may reach another device: no remote copies, remote signals or barrier semaphores. Data moves between devices by JAX's collectives and lax.ppermute only.
A program may use at most 192 MiB of HBM per device.

```python
import jax
import jax.numpy as jnp
from jax import lax

D = 1024
HEADS = 16
KVH = 8
HD = 64
FF = 4608
ADAPTER_RANK = 16
ADAPT = 8
TOK_DEV = 1024
SEQS = 2
LEN = 4096


def draw_segments(key, part):
    key = jax.random.fold_in(key, 11)
    first, second, third, fourth = jax.random.split(key, 4)
    start = jax.random.randint(first, (SEQS, 1), 1, TOK_DEV)
    stop = jax.random.randint(second, (SEQS, 1), LEN - TOK_DEV + 1, LEN)
    spacing = jax.random.randint(third, (SEQS, 1), 4, 64)
    random_bits = jax.random.randint(fourth, (SEQS, LEN), 0, 1048576)
    places = jnp.arange(LEN, dtype=jnp.int32)[None, :]
    outside = (places < start) | (places > stop)
    breaks = (random_bits % spacing == 0) & outside | (places == start) | (places == stop) | (places == LEN - 1)
    breaks = breaks & (places > 0)
    marks = jnp.where(breaks, places, 0).astype(jnp.int32)
    return lax.cummax(marks, axis=1).astype(jnp.int32)


def levels(own_key, dims, shards, least, top_value):
    factor_of = 1.0
    for dim, shards_of in shards:
        steps = jax.random.uniform(jax.random.fold_in(jax.random.fold_in(own_key, 6), dim), (shards_of,), jnp.float32, least / len(shards), top_value / len(shards))
        factor_of = factor_of * jnp.repeat(jnp.exp(steps), dims[dim] // shards_of).reshape((-1,) + (1,) * (len(dims) - 1 - dim))
    return factor_of


def noise(stream_key, shape, spread, most, cuts=(), kind=jnp.bfloat16):
    level = levels(stream_key, shape, cuts, -0.22, 0.18) if cuts else 1.0
    entries = jax.random.normal(stream_key, shape, jnp.float32) * spread * level
    return jnp.minimum(jnp.maximum(entries, -most), most).astype(kind)


def setup_inputs(seed: int = 0) -> dict:
    key_of = jax.random.split(jax.random.key(seed), 22)
    inputs = noise(key_of[0], (SEQS, LEN, D), 1.0, 6.0, ((0, 2), (1, 4)))
    cotangent = noise(key_of[1], (SEQS, LEN, D), 1.0, 6.0, ((0, 2), (1, 4)))
    segments = draw_segments(jax.random.fold_in(key_of[21], 71), 0)
    adapter_index = jax.random.randint(key_of[3], (SEQS,), 0, ADAPT).astype(jnp.int32)
    query_weight = noise(key_of[4], (D, HEADS * HD), D ** -0.5, 0.1875, ((0, 2), (1, 4)))
    key_value_weight = noise(key_of[5], (2, D, KVH * HD), D ** -0.5, 0.1875, ((1, 2), (2, 4)))
    output_weight = noise(key_of[6], (HEADS * HD, D), (HEADS * HD // 32) ** -0.5, 1.0, ((0, 4), (1, 2)))
    gate_up_weight = noise(key_of[7], (2, D, FF), D ** -0.5, 0.1875, ((1, 2), (2, 4)))
    down_weight = noise(key_of[8], (FF, D), FF ** -0.5, 0.09375, ((0, 4), (1, 2)))
    norm_attn = jnp.clip(1.0 + 0.1 * jax.random.normal(key_of[9], (D,), jnp.float32), 0.5, 1.5)
    norm_ffn = jnp.clip(1.0 + 0.1 * jax.random.normal(key_of[10], (D,), jnp.float32), 0.5, 1.5)
    q_gain = jnp.clip(jax.random.uniform(key_of[11], (HD,), jnp.float32, 0.8, 2.0), 0.8, 2.0)
    k_gain = jnp.clip(jax.random.uniform(key_of[12], (HD,), jnp.float32, 0.8, 2.0), 0.8, 2.0)
    input_adapter_lower = noise(key_of[13], (ADAPT, D, 5 * ADAPTER_RANK), D ** -0.5, 0.1875)
    query_adapter_upper = noise(key_of[14], (ADAPT, ADAPTER_RANK, HEADS * HD), (4 * ADAPTER_RANK) ** -0.5, 0.75, ((2, 4),))
    key_value_adapter_upper = noise(key_of[15], (ADAPT, 2, ADAPTER_RANK, KVH * HD), (4 * ADAPTER_RANK) ** -0.5, 0.75, ((3, 4),))
    gate_up_adapter_upper = noise(key_of[16], (ADAPT, 2, ADAPTER_RANK, FF), (4 * ADAPTER_RANK) ** -0.5, 0.75, ((3, 4),))
    output_adapter_lower = noise(key_of[17], (ADAPT, HEADS * HD, ADAPTER_RANK), (HEADS * HD // 32) ** -0.5, 1.0, ((1, 4),))
    output_adapter_upper = noise(key_of[18], (ADAPT, ADAPTER_RANK, D), (4 * ADAPTER_RANK) ** -0.5, 0.75)
    down_adapter_lower = noise(key_of[19], (ADAPT, FF, ADAPTER_RANK), FF ** -0.5, 0.09375, ((1, 4),))
    down_adapter_upper = noise(key_of[20], (ADAPT, ADAPTER_RANK, D), (4 * ADAPTER_RANK) ** -0.5, 0.75)
    return {"inputs": inputs, "cotangent": cotangent, "segments": segments, "adapter_index": adapter_index, "query_weight": query_weight, "key_value_weight": key_value_weight, "output_weight": output_weight, "gate_up_weight": gate_up_weight, "down_weight": down_weight, "norm_attn": norm_attn, "norm_ffn": norm_ffn, "q_gain": q_gain, "k_gain": k_gain, "input_adapter_lower": input_adapter_lower, "query_adapter_upper": query_adapter_upper, "key_value_adapter_upper": key_value_adapter_upper, "gate_up_adapter_upper": gate_up_adapter_upper, "output_adapter_lower": output_adapter_lower, "output_adapter_upper": output_adapter_upper, "down_adapter_lower": down_adapter_lower, "down_adapter_upper": down_adapter_upper}


EPS = 1e-05
ADAPTER_SCALING = 2.0
THETA = 1000000.0
NEG = -1e+30

@jax.custom_vjp
def low(v):
    return lax.optimization_barrier(v.astype(jnp.bfloat16)).astype(jnp.float32)

@jax.custom_vjp
def narrow_reverse(v):
    return v

def low_keep(v):
    return (low(v), None)

def low_pass(kept, grad):
    return (grad,)

def back_keep(v):
    return (v, None)

def back_low(kept, grad):
    return (low(grad),)
low.defvjp(low_keep, low_pass)
narrow_reverse.defvjp(back_keep, back_low)

def multiply_fn(left, right):
    return jnp.dot(left, right, precision=lax.Precision.HIGHEST)

def rmsnorm(value, gain):
    return value * lax.rsqrt(lax.optimization_barrier(jnp.mean(value * value, axis=-1, keepdims=True)) + EPS) * gain

def rotate(value, cosines, sines):
    half_dim = value.shape[-1] // 2
    first = value[..., :half_dim]
    second = value[..., half_dim:]
    return jnp.concatenate([first * cosines - second * sines, second * cosines + first * sines], axis=-1)

def attention(queries, keys, values, segment):
    length = queries.shape[0]
    block = min(512, length)
    group = HEADS // KVH
    scale = HD ** (-0.5)
    places = jnp.arange(length, dtype=jnp.int32)

    def one_block(item):
        query_block, start = item
        grouped = query_block.reshape(block, KVH, group, HD)
        scores = jnp.einsum('tkgd,skd->kgts', grouped, keys, precision=lax.Precision.HIGHEST) * scale
        scores = narrow_reverse(scores)
        query_place = start + jnp.arange(block, dtype=jnp.int32)
        query_segment = lax.dynamic_slice_in_dim(segment, start, block)
        allowed = (places[None, :] <= query_place[:, None]) & (segment[None, :] == query_segment[:, None])
        scores = jnp.where(allowed, scores, NEG)
        log_total = jax.nn.logsumexp(scores, axis=-1, keepdims=True)
        probs = jnp.exp(scores - log_total)
        final_output = jnp.einsum('kgts,skd->tkgd', low(probs), values, precision=lax.Precision.HIGHEST)
        return final_output.reshape(block, HEADS * HD)
    blocks = queries.reshape(length // block, block, HEADS, HD)
    starts = (jnp.arange(length // block, dtype=jnp.int32) * block).astype(jnp.int32)
    final_output = lax.map(jax.checkpoint(one_block), (blocks, starts))
    return final_output.reshape(length, HEADS * HD)

def layer(inputs, segment, adapters, weights, gains):
    input_adapter_lower, query_adapter_upper, key_value_adapter_upper, gate_up_adapter_upper, output_adapter_lower, output_adapter_upper, down_adapter_lower, down_adapter_upper = adapters
    query_weight, key_value_weight, output_weight, gate_up_weight, down_weight = weights
    norm_attn, norm_ffn, q_gain, k_gain = gains
    length = inputs.shape[0]
    half_dim = HD // 2
    inverse = THETA ** (-(jnp.arange(half_dim, dtype=jnp.float32) * 2.0 / HD))
    angles = jnp.arange(length, dtype=jnp.float32)[:, None] * inverse[None, :]
    cosines = jnp.cos(angles)[:, None, :]
    sines = jnp.sin(angles)[:, None, :]
    normalized = low(rmsnorm(inputs, norm_attn))
    narrow_product = low(multiply_fn(normalized, input_adapter_lower[:, :3 * ADAPTER_RANK]))
    query_projected = narrow_reverse(multiply_fn(normalized, query_weight) + ADAPTER_SCALING * multiply_fn(narrow_product[:, :ADAPTER_RANK], query_adapter_upper))
    key_projected = narrow_reverse(multiply_fn(normalized, key_value_weight[0]) + ADAPTER_SCALING * multiply_fn(narrow_product[:, ADAPTER_RANK:2 * ADAPTER_RANK], key_value_adapter_upper[0]))
    value_projected = narrow_reverse(multiply_fn(normalized, key_value_weight[1]) + ADAPTER_SCALING * multiply_fn(narrow_product[:, 2 * ADAPTER_RANK:3 * ADAPTER_RANK], key_value_adapter_upper[1]))
    queries = narrow_reverse(low(rotate(rmsnorm(query_projected.reshape(length, HEADS, HD), q_gain), cosines, sines)))
    keys = narrow_reverse(low(rotate(rmsnorm(key_projected.reshape(length, KVH, HD), k_gain), cosines, sines)))
    values = low(value_projected).reshape(length, KVH, HD)
    attention_mixed = low(narrow_reverse(attention(queries, keys, values, segment)))
    compressed = low(multiply_fn(attention_mixed, output_adapter_lower))
    hidden_state = inputs + narrow_reverse(multiply_fn(attention_mixed, output_weight) + ADAPTER_SCALING * multiply_fn(compressed, output_adapter_upper))
    normalized_second = low(rmsnorm(hidden_state, norm_ffn))
    narrow_product_second = low(multiply_fn(normalized_second, input_adapter_lower[:, 3 * ADAPTER_RANK:]))
    gate_values = narrow_reverse(multiply_fn(normalized_second, gate_up_weight[0]) + ADAPTER_SCALING * multiply_fn(narrow_product_second[:, :ADAPTER_RANK], gate_up_adapter_upper[0]))
    up_projected = narrow_reverse(multiply_fn(normalized_second, gate_up_weight[1]) + ADAPTER_SCALING * multiply_fn(narrow_product_second[:, ADAPTER_RANK:], gate_up_adapter_upper[1]))
    active_slots = low(jax.nn.silu(gate_values) * up_projected)
    compressed_second = low(multiply_fn(active_slots, down_adapter_lower))
    return hidden_state + narrow_reverse(multiply_fn(active_slots, down_weight) + ADAPTER_SCALING * multiply_fn(compressed_second, down_adapter_upper))

def select_adapter(table, adapter_slot):
    return lax.dynamic_index_in_dim(table, adapter_slot, 0, keepdims=False)

def reference(inputs, cotangent, segments, adapter_index, query_weight, key_value_weight, output_weight, gate_up_weight, down_weight, norm_attn, norm_ffn, q_gain, k_gain, input_adapter_lower, query_adapter_upper, key_value_adapter_upper, gate_up_adapter_upper, output_adapter_lower, output_adapter_upper, down_adapter_lower, down_adapter_upper):
    weights = tuple((weight.astype(jnp.float32) for weight in (query_weight, key_value_weight, output_weight, gate_up_weight, down_weight)))
    gains = (norm_attn, norm_ffn, q_gain, k_gain)
    adapters = tuple((table.astype(jnp.float32) for table in (input_adapter_lower, query_adapter_upper, key_value_adapter_upper, gate_up_adapter_upper, output_adapter_lower, output_adapter_upper, down_adapter_lower, down_adapter_upper)))

    def one_sequence(carry, item):
        seq_inputs, seq_cotangent, segment, adapter_slot = item

        def forward(layer_inputs, tables):
            chosen = tuple((select_adapter(table, adapter_slot) for table in tables))
            return layer(layer_inputs, segment, chosen, weights, gains)
        final_output, pullback = jax.vjp(forward, seq_inputs.astype(jnp.float32), adapters)
        grad_layer, grad_tables = pullback(seq_cotangent.astype(jnp.float32))
        carry = jax.tree.map(jnp.add, carry, grad_tables)
        return (carry, (final_output.astype(jnp.bfloat16), grad_layer))
    zeros = tuple((jnp.zeros(table.shape, jnp.float32) for table in adapters))
    sums, (outputs, grad_inputs) = lax.scan(one_sequence, zeros, (inputs, cotangent, segments, adapter_index))
    return (outputs, grad_inputs, sums[0], sums[1], sums[2], sums[3], sums[4], sums[5], sums[6], sums[7])
```

```python
import functools

import jax
import jax.numpy as jnp
from jax import lax
from jax.experimental import pallas as pl
from jax.experimental.pallas import tpu as pltpu
from jax.sharding import PartitionSpec as P

HD = 64
RANK = 16
ADAPT = 8
EPS = 1e-05
ADAPTER_SCALING = 2.0
THETA = 1000000.0
LOG2E = 1.4426950408889634
SCALE = HD**-0.5
F32 = jnp.float32
BF16 = jnp.bfloat16
VMEM_LIMIT = 40 * 1024 * 1024

CORE = [(i, i ^ 1) for i in range(4)]
XSIDE = [(i, i ^ 2) for i in range(4)]
Z_XOR = {d: [(i, i ^ d) for i in range(4)] for d in (1, 2, 3)}
CT = ("ctx", "tp")
SCT = ("shard", "ctx", "tp")
COLUMN = [[(2 * x + k) * 4 + z for k in range(2) for z in range(4)] for x in range(2)]


def nn(left, right):
    return lax.dot_general(left, right, (((1,), (0,)), ((), ())), preferred_element_type=F32)


def nt(left, right):
    return lax.dot_general(left, right, (((1,), (1,)), ((), ())), preferred_element_type=F32)


def tn(left, right):
    return lax.dot_general(left, right, (((0,), (0,)), ((), ())), preferred_element_type=F32)


def rmsnorm(value, gain):
    return value * lax.rsqrt(jnp.mean(value * value, axis=-1, keepdims=True) + EPS) * gain


def order2(own, other, bit, axis=0):
    return jnp.concatenate(
        [jnp.where(bit == 0, own, other), jnp.where(bit == 0, other, own)], axis=axis
    )


def rows_at(value, block, size, axis=0):
    return lax.dynamic_slice_in_dim(value, block * size, size, axis)


def block_ranges(segment, first_query, query_block, key_base, key_block, key_blocks, queries):
    starts = first_query + jnp.arange(queries // query_block, dtype=jnp.int32) * query_block
    seg_first = segment[starts]
    seg_last = segment[starts + query_block - 1]
    low = jnp.clip((seg_first - key_base) // key_block, 0, key_blocks)
    high = jnp.clip(
        (starts + query_block - key_base + key_block - 1) // key_block, 0, key_blocks
    )
    free_low = jnp.clip((seg_last - key_base + key_block - 1) // key_block, 0, key_blocks)
    free_high = jnp.clip((starts + 1 - key_base) // key_block, 0, key_blocks)
    low = jnp.minimum(low, high)
    free_low = jnp.clip(free_low, low, high)
    free_high = jnp.clip(free_high, free_low, high)
    return jnp.stack([low, free_low, free_high, high]).astype(jnp.int32)


def key_loops(info, i, step, acc):
    low, free_low, free_high, high = info[0, i], info[1, i], info[2, i], info[3, i]
    ahead = free_low - low

    def masked(t, carry):
        j = jnp.where(t < ahead, low + t, free_high + t - ahead)
        return step(j, carry, True)

    acc = lax.fori_loop(0, ahead + high - free_high, masked, acc)
    return lax.fori_loop(free_low, free_high, lambda j, carry: step(j, carry, False), acc)


def fwd_kernel(bq, bk, last, info, base, q_ref, kv_ref, seg_ref, *rest):
    if last:
        acc_in, mixed_ref, low_ref, lse_ref, vx = rest
    else:
        acc_ref, vx = rest
    i = pl.program_id(0)
    keys = kv_ref.shape[0]

    @pl.when(i == 0)
    def _():
        col = lax.broadcasted_iota(jnp.int32, (keys, 2 * HD), 1)
        kv = kv_ref[...]
        swapped = jnp.concatenate([kv[:, HD:], kv[:, :HD]], axis=1)
        ones = jnp.where(col == HD, 1.0, 0.0).astype(BF16)
        vx[...] = jnp.where(col < HD, swapped, ones)

    q = q_ref[...]
    both = jnp.concatenate([q[:, :HD], q[:, HD:]], axis=0)
    q_base, k_base = base[0], base[1]

    def step(j, acc, masked):
        off = pl.multiple_of(j * bk, bk)
        scores = nt(both, kv_ref[pl.ds(off, bk), :HD])
        probs = jnp.exp2(scores * (SCALE * LOG2E))
        if masked:
            qi = q_base + i * bq + lax.broadcasted_iota(jnp.int32, (bq, bk), 0)
            ki = k_base + off + lax.broadcasted_iota(jnp.int32, (bq, bk), 1)
            allowed = (ki <= qi) & (ki >= seg_ref[...])
            probs = jnp.where(jnp.concatenate([allowed, allowed], axis=0), probs, 0.0)
        return acc + nn(probs.astype(BF16), vx[pl.ds(off, bk), :])

    if last:
        acc = jnp.concatenate([acc_in[0], acc_in[1]], axis=0)
    else:
        acc = jnp.zeros((2 * bq, 2 * HD), F32)
    acc = key_loops(info, i, step, acc)
    if last:
        total = acc[:, HD : HD + 1]
        out = acc[:, :HD] / total
        out = jnp.concatenate([out[:bq], out[bq:]], axis=1)
        mixed_ref[...] = out
        low_ref[...] = out.astype(BF16)
        lse = jnp.log2(total)
        lse_ref[...] = jnp.concatenate([lse[:bq], lse[bq:]], axis=1)
    else:
        acc_ref[0] = acc[:bq]
        acc_ref[1] = acc[bq:]


def attention_forward(q, kv, seg, info, base, acc_in=None, bq=256, bk=1024):
    rows, keys = q.shape[0], kv.shape[0]
    last = acc_in is not None
    row = lambda i, *_: (i, 0)
    whole = lambda i, *_: (0, 0)
    heads = lambda i, *_: (0, i, 0)
    in_specs = [
        pl.BlockSpec((bq, 2 * HD), row),
        pl.BlockSpec((keys, 2 * HD), whole),
        pl.BlockSpec((bq, 1), row),
    ]
    args = [q, kv, seg]
    if last:
        in_specs.append(pl.BlockSpec((2, bq, 2 * HD), heads))
        args.append(acc_in)
        out_specs = [
            pl.BlockSpec((bq, 2 * HD), row),
            pl.BlockSpec((bq, 2 * HD), row),
            pl.BlockSpec((bq, 2), row),
        ]
        out_shape = [
            jax.ShapeDtypeStruct((rows, 2 * HD), F32),
            jax.ShapeDtypeStruct((rows, 2 * HD), BF16),
            jax.ShapeDtypeStruct((rows, 2), F32),
        ]
    else:
        out_specs = pl.BlockSpec((2, bq, 2 * HD), heads)
        out_shape = jax.ShapeDtypeStruct((2, rows, 2 * HD), F32)
    area = rows * keys // (1 if last else 2)
    return pl.pallas_call(
        functools.partial(fwd_kernel, bq, bk, last),
        grid_spec=pltpu.PrefetchScalarGridSpec(
            num_scalar_prefetch=2,
            grid=(rows // bq,),
            in_specs=in_specs,
            out_specs=out_specs,
            scratch_shapes=[pltpu.VMEM((keys, 2 * HD), BF16)],
        ),
        out_shape=out_shape,
        compiler_params=pltpu.CompilerParams(vmem_limit_bytes=VMEM_LIMIT),
        cost_estimate=pl.CostEstimate(
            flops=2 * 2 * 2 * 128 * area * 2, bytes_accessed=8 << 20, transcendentals=2 * area
        ),
        name="attn_fwd_last" if last else "attn_fwd_first",
    )(info, base, *args)


def bwd_kernel(bq, bk, first, info, base, q_ref, kv_ref, seg_ref, do_ref, lse_ref, del_ref, *rest):
    if first:
        dq_ref, dkv_ref, dk, dv = rest
    else:
        dq_in, dq_ref, dkv_ref, dk, dv = rest
    i = pl.program_id(0)

    @pl.when(i == 0)
    def _():
        dk[...] = jnp.zeros_like(dk)
        dv[...] = jnp.zeros_like(dv)

    q = q_ref[...]
    do = do_ref[...]
    both = jnp.concatenate([q[:, :HD], q[:, HD:]], axis=0)
    both_do = jnp.concatenate([do[:, :HD], do[:, HD:]], axis=0)
    lse = lse_ref[0]
    delta = del_ref[0]
    q_base, k_base = base[0], base[1]

    def step(j, acc, masked):
        off = pl.multiple_of(j * bk, bk)
        kv = kv_ref[pl.ds(off, bk), :]
        k, v = kv[:, :HD], kv[:, HD:]
        probs = jnp.exp2(nt(k, both) * (SCALE * LOG2E) - lse)
        if masked:
            ki = k_base + off + lax.broadcasted_iota(jnp.int32, (bk, bq), 0)
            qi = q_base + i * bq + lax.broadcasted_iota(jnp.int32, (bk, bq), 1)
            allowed = (ki <= qi) & (ki >= seg_ref[0])
            probs = jnp.where(jnp.concatenate([allowed, allowed], axis=1), probs, 0.0)
        dscores = (probs * (nt(v, both_do) - delta)).astype(BF16)
        dv[pl.ds(off, bk), :] += nn(probs.astype(BF16), both_do)
        dk[pl.ds(off, bk), :] += nn(dscores, both)
        return acc + tn(dscores, k)

    acc = key_loops(info, i, step, jnp.zeros((2 * bq, HD), F32))
    acc = jnp.concatenate([acc[:bq], acc[bq:]], axis=1) * SCALE
    dq_ref[...] = acc if first else dq_in[...] + acc

    @pl.when(i == pl.num_programs(0) - 1)
    def _():
        dkv_ref[...] = jnp.concatenate([dk[...] * SCALE, dv[...]], axis=1).astype(dkv_ref.dtype)


def attention_backward(q, kv, seg, do, lse, delta, info, base, dq_in=None, bq=256, bk=512):
    rows, keys = q.shape[0], kv.shape[0]
    first = dq_in is None
    row = lambda i, *_: (i, 0)
    whole = lambda i, *_: (0, 0)
    flat = lambda i, *_: (i, 0, 0)
    in_specs = [
        pl.BlockSpec((bq, 2 * HD), row),
        pl.BlockSpec((keys, 2 * HD), whole),
        pl.BlockSpec((1, 1, bq), flat),
        pl.BlockSpec((bq, 2 * HD), row),
        pl.BlockSpec((1, 1, 2 * bq), flat),
        pl.BlockSpec((1, 1, 2 * bq), flat),
    ]
    args = [q, kv, seg, do, lse, delta]
    if not first:
        in_specs.append(pl.BlockSpec((bq, 2 * HD), row))
        args.append(dq_in)
    area = rows * keys // (1 if first else 2)
    return pl.pallas_call(
        functools.partial(bwd_kernel, bq, bk, first),
        grid_spec=pltpu.PrefetchScalarGridSpec(
            num_scalar_prefetch=2,
            grid=(rows // bq,),
            in_specs=in_specs,
            out_specs=[pl.BlockSpec((bq, 2 * HD), row), pl.BlockSpec((keys, 2 * HD), whole)],
            scratch_shapes=[pltpu.VMEM((keys, HD), F32), pltpu.VMEM((keys, HD), F32)],
        ),
        out_shape=[
            jax.ShapeDtypeStruct((rows, 2 * HD), F32),
            jax.ShapeDtypeStruct((keys, 2 * HD), BF16 if first else F32),
        ],
        compiler_params=pltpu.CompilerParams(vmem_limit_bytes=VMEM_LIMIT),
        cost_estimate=pl.CostEstimate(
            flops=2 * 5 * 2 * 128 * area * 2, bytes_accessed=8 << 20, transcendentals=2 * area
        ),
        name="attn_bwd_first" if first else "attn_bwd_last",
    )(info, base, *args)


def after(value, *others):
    return lax.optimization_barrier((value, others))[0]


def heads_tokens(value):
    return lax.all_to_all(value, CT, 0, 0, axis_index_groups=COLUMN, tiled=True)


def z_gather(own, z):
    up = {}
    down = {}
    ahead = back = own
    for d in (1, 2, 3):
        ahead = lax.ppermute(ahead, "tp", [(i, i + 1) for i in range(3)])
        back = lax.ppermute(back, "tp", [(i + 1, i) for i in range(3)])
        up[d], down[d] = ahead, back
    out = []
    for place in range(4):
        value = own
        for here in range(4):
            if here < place:
                value = jnp.where(z == here, down[place - here], value)
            elif here > place:
                value = jnp.where(z == here, up[here - place], value)
        out.append(value)
    return out


def body(
    shards,
    inputs,
    cotangent,
    segments,
    adapter_index,
    query_weight,
    key_value_weight,
    output_weight,
    gate_up_weight,
    down_weight,
    norm_attn,
    norm_ffn,
    q_gain,
    k_gain,
    input_adapter_lower,
    query_adapter_upper,
    key_value_adapter_upper,
    gate_up_adapter_upper,
    output_adapter_lower,
    output_adapter_upper,
    down_adapter_lower,
    down_adapter_upper,
):
    ctx = lax.axis_index("ctx")
    x, k = ctx // 2, ctx % 2
    z = lax.axis_index("tp")
    y = lax.axis_index("shard")
    tok = inputs.shape[1]
    half = 2 * tok
    sub = tok // 4
    width = inputs.shape[2]
    slot = adapter_index[0]
    segment = segments[0]
    pair = shards == 2
    swap_y = [(0, 1), (1, 0)]

    def chosen(table):
        return lax.dynamic_index_in_dim(table, slot, 0, keepdims=False)

    def shard_rows(piece, axis):
        if pair:
            return order2(piece, lax.ppermute(piece, "shard", swap_y), y, axis)
        return lax.all_gather(piece, "shard", axis=axis, tiled=True)

    head_q = rows_at(query_weight, k, 2 * HD, 1)
    head_kv = rows_at(key_value_weight, k, HD, 2)
    dense_qkv = shard_rows(jnp.concatenate([head_q, head_kv[0], head_kv[1]], axis=1), 0)
    tokens_other = lax.ppermute(inputs[0], "ctx", CORE)
    out_rows = shard_rows(rows_at(output_weight, k, 2 * HD, 0), 1)
    adapter_in = chosen(input_adapter_lower)
    up_q = rows_at(chosen(query_adapter_upper), k, 2 * HD, 1)
    up_kv = rows_at(chosen(key_value_adapter_upper), k, HD, 2)
    lower_down = chosen(down_adapter_lower)
    upper_down = chosen(down_adapter_upper)
    lower_out = rows_at(chosen(output_adapter_lower), k, 2 * HD, 0)
    upper_out = chosen(output_adapter_upper)
    merged_qkv = (
        dense_qkv.astype(F32)
        + ADAPTER_SCALING
        * jnp.concatenate(
            [
                nn(adapter_in[:, :RANK], up_q),
                nn(adapter_in[:, RANK : 2 * RANK], up_kv[0]),
                nn(adapter_in[:, 2 * RANK : 3 * RANK], up_kv[1]),
            ],
            axis=1,
        )
    ).astype(BF16)

    def quarter(weight):
        if not pair:
            full = lax.all_gather(weight, "shard", axis=1, tiled=True)
            return jnp.where(k == 0, full, lax.ppermute(full, "tp", Z_XOR[2]))

        def over_y(cores):
            return [
                ((s * 4 + c) * 4 + t, ((s ^ 1) * 4 + c) * 4 + t)
                for s in range(2)
                for c in cores
                for t in range(4)
            ]

        piece = rows_at(weight, x, weight.shape[1] // 2, 1)
        piece = lax.ppermute(
            piece, CT, [(c * 4 + t, c * 4 + (t ^ 2)) for c in (1, 3) for t in range(4)]
        )
        mine = lax.ppermute(after(weight, dense_qkv), SCT, over_y((0, 2)))
        piece_x = lax.ppermute(piece, "ctx", [(1, 3), (3, 1)])
        far = order2(piece, piece_x, x, 1)
        far_y = lax.ppermute(far, SCT, over_y((1, 3)))
        return order2(jnp.where(k == 0, weight, far), jnp.where(k == 0, mine, far_y), y, 1)

    frozen = jnp.concatenate([gate_up_weight, down_weight.T[None]], axis=0)
    dense_ffn = quarter(after(frozen, tokens_other))
    small_ffn = jnp.concatenate([chosen(gate_up_adapter_upper), lower_down.T[None]], axis=0)
    small_far = lax.ppermute(after(small_ffn, dense_qkv), "tp", Z_XOR[2])
    small_ffn = jnp.where(k == 0, small_ffn, small_far)
    lower_gate_up = adapter_in[:, 3 * RANK :]
    merged_gate, merged_up, merged_down = (
        (dense_ffn[i].astype(F32) + ADAPTER_SCALING * term).astype(BF16)
        for i, term in enumerate(
            (
                nn(lower_gate_up[:, :RANK], small_ffn[0]),
                nn(lower_gate_up[:, RANK:], small_ffn[1]),
                tn(upper_down, small_ffn[2]),
            )
        )
    )

    out_rows = (out_rows.astype(F32) + ADAPTER_SCALING * nn(lower_out, upper_out)).astype(BF16)
    small_rows = lower_out.reshape(-1, width)
    out_rows = jnp.concatenate(
        [out_rows, small_rows, jnp.zeros((16 - small_rows.shape[0], width), BF16)], axis=0
    )
    out_own = lax.all_gather(out_rows, "tp", axis=0)
    out_own = order2(out_own, lax.ppermute(out_own, "ctx", CORE), k)
    merged_out = out_own[:, : 2 * HD].reshape(-1, width)
    lower_whole = out_own[:, 2 * HD : 2 * HD + small_rows.shape[0]].reshape(-1, RANK)

    tokens = order2(inputs[0], tokens_other, k)
    normalized = rmsnorm(tokens.astype(F32), norm_attn).astype(BF16)
    narrow = nn(normalized, adapter_in[:, : 3 * RANK]).astype(BF16)
    projected = nn(normalized, merged_qkv)
    first_query = x * half
    half_dim = HD // 2
    inverse = THETA ** (-(jnp.arange(half_dim, dtype=F32) * 2.0 / HD))
    places = first_query + jnp.arange(half, dtype=jnp.int32)
    angles = places.astype(F32)[:, None] * inverse[None, :]
    cosines, sines = jnp.cos(angles), jnp.sin(angles)

    def shape_head(value, gain):
        value = rmsnorm(value, gain)
        first, second = value[:, :half_dim], value[:, half_dim:]
        return jnp.concatenate(
            [first * cosines - second * sines, second * cosines + first * sines], axis=1
        )

    def shape_heads(q0, q1, key):
        return shape_head(q0, q_gain), shape_head(q1, q_gain), shape_head(key, k_gain)

    raw = (projected[:, :HD], projected[:, HD : 2 * HD], projected[:, 2 * HD : 3 * HD])
    heads, heads_back = jax.vjp(shape_heads, *raw)
    queries = jnp.concatenate([heads[0], heads[1]], axis=1).astype(BF16)
    keyvals = jnp.concatenate([heads[2], projected[:, 3 * HD :]], axis=1).astype(BF16)
    keyvals_before = lax.ppermute(keyvals, "ctx", [(0, 2), (1, 3)])

    fq, fk, bq, bk = 256, 1024, 256, 512
    base_here = jnp.stack([first_query, first_query]).astype(jnp.int32)
    base_before = jnp.stack([first_query, first_query - half]).astype(jnp.int32)
    segment_here = lax.dynamic_slice_in_dim(segment, first_query, half)

    def info_of(size_q, size_k, key_base):
        return block_ranges(segment, first_query, size_q, key_base, size_k, half // size_k, half)

    seg_col = segment_here[:, None]
    acc = attention_forward(
        queries, keyvals, seg_col, info_of(fq, fk, first_query), base_here, None, fq, fk
    )
    mixed, mixed_low, lse = attention_forward(
        queries,
        keyvals_before,
        seg_col,
        info_of(fq, fk, first_query - half),
        base_before,
        acc,
        fq,
        fk,
    )

    def to_tokens(value):
        arrived = heads_tokens(value.reshape(8, sub, value.shape[1]))
        return jnp.concatenate([arrived[i] for i in range(8)], axis=1)

    mixed_all = to_tokens(mixed_low)
    tokens_own = rows_at(inputs[0], z, sub).astype(F32)
    hidden_state = tokens_own + nn(mixed_all, merged_out)
    normalized_second = rmsnorm(hidden_state, norm_ffn).astype(BF16)

    zbit = z % 2
    second_pair = order2(normalized_second, lax.ppermute(normalized_second, "tp", Z_XOR[1]), zbit)
    second_all = order2(second_pair, lax.ppermute(second_pair, "ctx", CORE), k)
    grad_pair = rows_at(cotangent[0], z // 2, 2 * sub)
    grad_all = order2(grad_pair, lax.ppermute(after(grad_pair, dense_qkv), "ctx", CORE), k)
    gate = nn(second_all, merged_gate)
    up = nn(second_all, merged_up)
    sig = 1.0 / (1.0 + jnp.exp(-gate))
    silu = gate * sig
    active = (silu * up).astype(BF16)
    grad_active = nn(grad_all, merged_down)
    grad_gate = (grad_active * up * (sig + silu * (1.0 - sig))).astype(BF16)
    grad_up = (grad_active * silu).astype(BF16)
    ffn_part = (nt(grad_gate, merged_gate) + nt(grad_up, merged_up)).astype(BF16)

    def summed_to_owner(part):
        mine = rows_at(part, k, 2 * sub).astype(F32)
        arrived = lax.ppermute(rows_at(part, 1 - k, 2 * sub), "ctx", CORE)
        mine = mine + arrived.astype(F32)
        give = rows_at(mine, 1 - zbit, sub).astype(BF16)
        return rows_at(mine, zbit, sub) + lax.ppermute(give, "tp", Z_XOR[1]).astype(F32)

    grad_normalized_second = summed_to_owner(ffn_part)

    grad_own = rows_at(cotangent[0], z, sub).astype(F32)
    unused, norm_two_back = jax.vjp(lambda value: rmsnorm(value, norm_ffn), hidden_state)
    grad_hidden = grad_own + norm_two_back(grad_normalized_second)[0]
    grad_hidden_low = grad_hidden.astype(BF16)
    grad_mixed_all = nt(grad_hidden_low, merged_out).astype(BF16)
    cols = 2 * HD
    grad_mixed = heads_tokens(
        jnp.stack([grad_mixed_all[:, i * cols : (i + 1) * cols] for i in range(8)])
    ).reshape(half, cols)

    active_later, second_later = after((active, second_all), grad_mixed_all)
    down_part = nt(active_later, merged_down).astype(BF16)
    down_sum = summed_to_owner(down_part)
    result = lax.all_gather((hidden_state + down_sum).astype(BF16), "tp", axis=0, tiled=True)
    narrow_second = nn(second_later, lower_gate_up).astype(BF16)
    du2 = ADAPTER_SCALING * jnp.concatenate(
        [nt(grad_gate, small_ffn[0]), nt(grad_up, small_ffn[1])], axis=1
    )
    zd = nt(active_later, small_ffn[2]).astype(BF16)
    dzd = (ADAPTER_SCALING * nt(grad_all, upper_down)).astype(BF16)
    zo = nn(mixed_all, lower_whole).astype(BF16)
    dzo = (ADAPTER_SCALING * nt(grad_hidden_low, upper_out)).astype(BF16)
    wide_grads = jnp.concatenate(
        [
            ADAPTER_SCALING * tn(zo, grad_hidden_low),
            ADAPTER_SCALING * tn(zd, grad_all),
            tn(dzo, mixed_all),
            tn(du2.astype(BF16), second_later),
        ],
        axis=0,
    ).astype(BF16)
    quarter_grads = jnp.concatenate(
        [
            ADAPTER_SCALING * tn(narrow_second[:, :RANK], grad_gate),
            ADAPTER_SCALING * tn(narrow_second[:, RANK:], grad_up),
            tn(dzd, active_later),
        ],
        axis=0,
    ).astype(BF16)

    slots = jnp.arange(ADAPT, dtype=jnp.int32)
    if pair:
        slot_other = lax.ppermute(after(adapter_index, dense_qkv), "shard", swap_y)[0]
        shard_slots = [jnp.where(y == 0, slot, slot_other), jnp.where(y == 0, slot_other, slot)]
    else:
        shard_slots = list(lax.all_gather(adapter_index[0], "shard"))
    kept = min(shards, ADAPT)

    def placed(grads):
        if shards > ADAPT:
            return grads.astype(F32)
        out = 0.0
        for i in range(shards):
            mask = (slots == shard_slots[i]).astype(F32).reshape((ADAPT,) + (1,) * (grads.ndim - 1))
            out = out + mask * grads[i].astype(F32)[None]
        return out

    def by_shard(arrived):
        sums = jnp.sum(
            arrived.astype(F32).reshape((shards, -1) + arrived.shape[1:]), axis=1
        )
        if shards <= ADAPT:
            return sums
        out = 0.0
        for i in range(shards):
            mask = (slots == shard_slots[i]).astype(F32).reshape((ADAPT,) + (1,) * (sums.ndim - 1))
            out = out + mask * sums[i][None]
        return out

    def split_columns(value, parts):
        return jnp.moveaxis(value.reshape(value.shape[0], parts, -1), 1, 0)

    def to_all(value, axes, parts):
        return lax.all_to_all(
            jnp.broadcast_to(value[None], (parts,) + value.shape), axes, 0, 0, tiled=True
        )

    def joined(value):
        value = jnp.moveaxis(value, 0, 2)
        return value.reshape(value.shape[:2] + (-1,))

    devices = shards * 16
    rows_axes = ("shard", "ctx")
    wide_grads, quarter_grads = after((wide_grads, quarter_grads), grad_mixed)
    wide_parts = lax.all_to_all(split_columns(wide_grads, devices), SCT, 0, 0, tiled=True)
    quarter_far = lax.ppermute(quarter_grads, "tp", Z_XOR[2])
    quarter_grads = jnp.where(k == 0, quarter_grads, quarter_far)

    product = grad_mixed.astype(F32) * mixed
    delta = jnp.stack([jnp.sum(product[:, :HD], 1), jnp.sum(product[:, HD:], 1)], axis=1)

    def lanes(value):
        blocks = value.reshape(half // bq, bq, 2).transpose(0, 2, 1)
        return blocks.reshape(half // bq, 1, 2 * bq)

    lse_rows, delta_rows = lanes(lse), lanes(delta)
    seg_rows = segment_here.reshape(half // bq, 1, bq)
    dq_before, dkv_before = attention_backward(
        queries,
        keyvals_before,
        seg_rows,
        grad_mixed,
        lse_rows,
        delta_rows,
        info_of(bq, bk, first_query - half),
        base_before,
        None,
        bq,
        bk,
    )
    dkv_after = lax.ppermute(dkv_before, "ctx", [(2, 0), (3, 1)])
    wide_parts, quarter_grads = after((wide_parts, quarter_grads), dq_before)
    wide_sums = by_shard(wide_parts).astype(BF16)
    wide_all = to_all(wide_sums, SCT, devices)
    quarter_parts = lax.all_to_all(
        split_columns(quarter_grads, shards * 4), rows_axes, 0, 0, tiled=True
    )
    dq, dkv = attention_backward(
        queries,
        keyvals,
        seg_rows,
        grad_mixed,
        lse_rows,
        delta_rows,
        info_of(bq, bk, first_query),
        base_here,
        dq_before,
        bq,
        bk,
    )
    dkv = (dkv + dkv_after.astype(F32)).astype(BF16)
    dq = dq.astype(BF16).astype(F32)
    d_raw = heads_back((dq[:, :HD], dq[:, HD:], dkv[:, :HD].astype(F32)))
    d_projected = jnp.concatenate(
        [d_raw[0].astype(BF16), d_raw[1].astype(BF16), d_raw[2].astype(BF16), dkv[:, HD:]], axis=1
    )

    qkv_own = lax.all_gather(after(merged_qkv, normalized_second).T, "tp", axis=0)
    qkv_all = order2(qkv_own, lax.ppermute(qkv_own, "ctx", CORE), k).reshape(-1, width)
    grad_normalized = nn(to_tokens(d_projected), qkv_all)
    unused, norm_back = jax.vjp(lambda value: rmsnorm(value, norm_attn), tokens_own)
    grad_tokens = (grad_hidden + norm_back(grad_normalized)[0]).astype(BF16)
    grad_inputs = jnp.concatenate(z_gather(grad_tokens, z), axis=0).astype(F32)

    wide_all, quarter_parts = after((wide_all, quarter_parts), d_projected)
    quarter_all = to_all(by_shard(quarter_parts).astype(BF16), rows_axes, shards * 4)
    grad_b_qkv = ADAPTER_SCALING * jnp.concatenate(
        [
            tn(narrow[:, :RANK], d_projected[:, : 2 * HD]),
            tn(narrow[:, RANK : 2 * RANK], d_projected[:, 2 * HD : 3 * HD]),
            tn(narrow[:, 2 * RANK :], d_projected[:, 3 * HD :]),
        ],
        axis=1,
    )
    du1 = ADAPTER_SCALING * jnp.concatenate(
        [
            nt(d_projected[:, : 2 * HD], up_q),
            nt(d_projected[:, 2 * HD : 3 * HD], up_kv[0]),
            nt(d_projected[:, 3 * HD :], up_kv[1]),
        ],
        axis=1,
    )
    in_attn = tn(du1.astype(BF16), normalized).astype(BF16)
    in_parts = lax.all_to_all(split_columns(in_attn, devices), SCT, 0, 0, tiled=True)
    in_all = joined(to_all(by_shard(in_parts).astype(BF16), "tp", 4))
    qkv_parts = to_all(grad_b_qkv.astype(BF16), rows_axes, shards * 4)
    qkv_parts = qkv_parts.reshape(shards, 2, 2, RANK, 4 * HD).astype(F32)
    qkv_sums = jnp.moveaxis(jnp.sum(qkv_parts, axis=1), 0, 1).reshape(2 * shards, RANK, 4 * HD)
    qkv_sums = [by_shard(qkv_sums[i * shards : (i + 1) * shards]) for i in range(2)]
    grad_b_query = jnp.concatenate([part[..., : 2 * HD] for part in qkv_sums], axis=-1)
    grad_b_keyval = jnp.stack(
        [
            jnp.concatenate([part[..., c * HD : (c + 1) * HD] for part in qkv_sums], axis=-1)
            for c in (2, 3)
        ],
        axis=1,
    )
    wide_all = joined(wide_all)
    grad_b_out = wide_all[:, :RANK]
    grad_b_down = wide_all[:, RANK : 2 * RANK]
    grad_a_out = wide_all[:, 2 * RANK : 3 * RANK]
    grad_a_out = jnp.concatenate(
        [rows_at(grad_a_out, z, cols, 2), rows_at(grad_a_out, 4 + z, cols, 2)], axis=2
    )
    own_width = width // (shards * 4)
    in_ffn = rows_at(wide_all[:, 3 * RANK :], y * 4 + ctx, own_width, 2)
    grad_adapt_in = jnp.concatenate([in_all, in_ffn], axis=1)
    quarter_all = joined(quarter_all)
    grad_b_gate_up = quarter_all[:, : 2 * RANK].reshape(kept, 2, RANK, -1)
    grad_a_down = quarter_all[:, 2 * RANK :]
    return (
        result[None],
        grad_inputs[None],
        jnp.swapaxes(placed(grad_adapt_in), 1, 2),
        placed(grad_b_query),
        placed(grad_b_keyval),
        placed(grad_b_gate_up),
        jnp.swapaxes(placed(grad_a_out), 1, 2),
        placed(grad_b_out),
        jnp.swapaxes(placed(grad_a_down), 1, 2),
        placed(grad_b_down),
    )


def solution(mesh):
    return jax.shard_map(
        functools.partial(body, mesh.shape["shard"]),
        mesh=mesh,
        in_specs=(
            P("shard", "ctx", None),
            P("shard", "ctx", None),
            P("shard", None),
            P("shard"),
            P("shard", "tp"),
            P(None, "shard", "tp"),
            P("tp", "shard"),
            P(None, "shard", "tp"),
            P("tp", "shard"),
            P(),
            P(),
            P(),
            P(),
            P(),
            P(None, None, "tp"),
            P(None, None, None, "tp"),
            P(None, None, None, "tp"),
            P(None, "tp", None),
            P(),
            P(None, "tp", None),
            P(),
        ),
        out_specs=(
            P("shard", "ctx", None),
            P("shard", "ctx", None),
            P(None, ("shard", "ctx"), None),
            P(None, None, "tp"),
            P(None, None, None, "tp"),
            P(None, None, None, "tp"),
            P(None, "tp", None),
            P(),
            P(None, "tp", None),
            P(),
        ),
        check_vma=False,
    )
```

```python
import functools

import jax
import jax.numpy as jnp
from jax import lax
from jax.experimental import pallas as pl
from jax.experimental.pallas import tpu as pltpu
from jax.sharding import PartitionSpec as P

HD = 64
RANK = 16
ADAPT = 8
EPS = 1e-05
ADAPTER_SCALING = 2.0
THETA = 1000000.0
LOG2E = 1.4426950408889634
SCALE = HD**-0.5
F32 = jnp.float32
BF16 = jnp.bfloat16
VMEM_LIMIT = 62 * 1024 * 1024

CORE = [(i, i ^ 1) for i in range(4)]
XSIDE = [(i, i ^ 2) for i in range(4)]
Z_XOR = {d: [(i, i ^ d) for i in range(4)] for d in (1, 2, 3)}
CT = ("ctx", "tp")
SCT = ("shard", "ctx", "tp")
COLUMN = [[(2 * x + k) * 4 + z for k in range(2) for z in range(4)] for x in range(2)]

COST = pl.CostEstimate(flops=1 << 20, bytes_accessed=1 << 16, transcendentals=0)
LONG = pl.CostEstimate(flops=30 << 30, bytes_accessed=16 << 20, transcendentals=0)
HIGHEST = lax.Precision.HIGHEST


def nn(left, right):
    return lax.dot_general(left, right, (((1,), (0,)), ((), ())), preferred_element_type=F32)


def nt(left, right):
    return lax.dot_general(left, right, (((1,), (1,)), ((), ())), preferred_element_type=F32)


def tn(left, right):
    return lax.dot_general(left, right, (((0,), (0,)), ((), ())), preferred_element_type=F32)


def rmsnorm(value, gain):
    return value * lax.rsqrt(jnp.mean(value * value, axis=-1, keepdims=True) + EPS) * gain


def order2(own, other, bit, axis=0):
    return jnp.concatenate(
        [jnp.where(bit == 0, own, other), jnp.where(bit == 0, other, own)], axis=axis
    )


def rows_at(value, block, size, axis=0):
    return lax.dynamic_slice_in_dim(value, block * size, size, axis)


def key_loops(segment, base, i, bq, bk, keys, step, acc):
    blocks = keys // bk
    first, key_base = base[0] + i * bq, base[1]
    low = jnp.minimum(jnp.maximum(segment[first] - key_base, 0) // bk, blocks)
    high = jnp.clip((first + bq - key_base + bk - 1) // bk, 0, blocks)
    low = jnp.minimum(low, high)
    free_low = (jnp.maximum(segment[first + bq - 1] - key_base, 0) + bk - 1) // bk
    free_low = jnp.clip(free_low, low, high)
    free_high = jnp.clip(jnp.maximum(first + 1 - key_base, 0) // bk, free_low, high)
    ahead = free_low - low

    def masked(t, carry):
        j = jnp.where(t < ahead, low + t, free_high + t - ahead)
        return step(j, carry, True)

    acc = lax.fori_loop(0, ahead + high - free_high, masked, acc)
    return lax.fori_loop(free_low, free_high, lambda j, carry: step(j, carry, False), acc)


def row_sums(weights, value):
    return lax.dot_general(
        weights, value, (((1,), (1,)), ((), ())), precision=HIGHEST, preferred_element_type=F32
    )


def fwd_kernel(bq, bk, last, segment, base, q_ref, kv_ref, seg_ref, *rest):
    if last:
        acc_in, mixed_ref, low_ref, lse_ref, vx = rest
    else:
        acc_ref, vx = rest
    i = pl.program_id(0)
    keys = kv_ref.shape[0]

    @pl.when(i == 0)
    def _():
        col = lax.broadcasted_iota(jnp.int32, (keys, 2 * HD), 1)
        kv = kv_ref[...]
        swapped = jnp.concatenate([kv[:, HD:], kv[:, :HD]], axis=1)
        ones = jnp.where(col == HD, 1.0, 0.0).astype(BF16)
        vx[...] = jnp.where(col < HD, swapped, ones)

    q = q_ref[...]
    both = jnp.concatenate([q[:, :HD], q[:, HD:]], axis=0)
    q_base, k_base = base[0], base[1]
    seg_col = jnp.broadcast_to(seg_ref[0].astype(F32), (8, bq))
    seg_col = jnp.transpose(seg_col)[:, :1].astype(jnp.int32)

    def step(j, acc, masked):
        off = pl.multiple_of(j * bk, bk)
        scores = nt(both, kv_ref[pl.ds(off, bk), :HD])
        probs = jnp.exp2(scores * (SCALE * LOG2E))
        if masked:
            qi = q_base + i * bq + lax.broadcasted_iota(jnp.int32, (bq, bk), 0)
            ki = k_base + off + lax.broadcasted_iota(jnp.int32, (bq, bk), 1)
            allowed = (ki <= qi) & (ki >= seg_col)
            probs = jnp.where(jnp.concatenate([allowed, allowed], axis=0), probs, 0.0)
        return acc + nn(probs.astype(BF16), vx[pl.ds(off, bk), :])

    if last:
        acc = jnp.concatenate([acc_in[0], acc_in[1]], axis=0)
    else:
        acc = jnp.zeros((2 * bq, 2 * HD), F32)
    acc = key_loops(segment, base, i, bq, bk, keys, step, acc)
    if last:
        total = acc[:, HD : HD + 1]
        out = acc[:, :HD] / total
        out = jnp.concatenate([out[:bq], out[bq:]], axis=1)
        mixed_ref[...] = out
        low_ref[...] = out.astype(BF16)
        pick = jnp.where(lax.broadcasted_iota(jnp.int32, (8, 2 * HD), 1) == HD, 1.0, 0.0)
        lse_ref[0] = jnp.log2(row_sums(pick, acc)[:1])
    else:
        acc_ref[0] = acc[:bq]
        acc_ref[1] = acc[bq:]


def attention_forward(q, kv, seg, segment, base, bq, bk, acc_in=None):
    rows, keys = q.shape[0], kv.shape[0]
    last = acc_in is not None
    row = lambda i, *_: (i, 0)
    everything = lambda i, *_: (0, 0)
    heads = lambda i, *_: (0, i, 0)
    in_specs = [
        pl.BlockSpec((bq, 2 * HD), row),
        pl.BlockSpec((keys, 2 * HD), everything),
        pl.BlockSpec((1, 1, bq), lambda i, *_: (i, 0, 0)),
    ]
    args = [q, kv, seg]
    if last:
        in_specs.append(pl.BlockSpec((2, bq, 2 * HD), heads))
        args.append(acc_in)
        out_specs = [
            pl.BlockSpec((bq, 2 * HD), row),
            pl.BlockSpec((bq, 2 * HD), row),
            pl.BlockSpec((1, 1, 2 * bq), lambda i, *_: (i, 0, 0)),
        ]
        out_shape = [
            jax.ShapeDtypeStruct((rows, 2 * HD), F32),
            jax.ShapeDtypeStruct((rows, 2 * HD), BF16),
            jax.ShapeDtypeStruct((rows // bq, 1, 2 * bq), F32),
        ]
    else:
        out_specs = pl.BlockSpec((2, bq, 2 * HD), heads)
        out_shape = jax.ShapeDtypeStruct((2, rows, 2 * HD), F32)
    return pl.pallas_call(
        functools.partial(fwd_kernel, bq, bk, last),
        grid_spec=pltpu.PrefetchScalarGridSpec(
            num_scalar_prefetch=2,
            grid=(rows // bq,),
            in_specs=in_specs,
            out_specs=out_specs,
            scratch_shapes=[pltpu.VMEM((keys, 2 * HD), BF16)],
        ),
        out_shape=out_shape,
        compiler_params=pltpu.CompilerParams(vmem_limit_bytes=VMEM_LIMIT),
        cost_estimate=LONG,
        name="attn_fwd_last" if last else "attn_fwd_first",
    )(segment, base, *args)


def bwd_kernel(
    bq, bk, first, segment, base, q_ref, kv_ref, seg_ref, do_ref, out_ref, lse_ref, *rest
):
    if first:
        dq_ref, dkv_ref, dk, dv = rest
    else:
        dq_in, dq_ref, dkv_ref, dk, dv = rest
    i = pl.program_id(0)

    @pl.when(i == 0)
    def _():
        dk[...] = jnp.zeros_like(dk)
        dv[...] = jnp.zeros_like(dv)

    q = q_ref[...]
    do = do_ref[...]
    both = jnp.concatenate([q[:, :HD], q[:, HD:]], axis=0)
    both_do = jnp.concatenate([do[:, :HD], do[:, HD:]], axis=0)
    lse = lse_ref[0]
    lane = lax.broadcasted_iota(jnp.int32, (8, 2 * HD), 1)
    row = lax.broadcasted_iota(jnp.int32, (8, 2 * HD), 0)
    pick = jnp.where(lane // HD == row, 1.0, 0.0)
    deltas = row_sums(pick, do.astype(F32) * out_ref[...])
    delta = jnp.concatenate([deltas[:1], deltas[1:2]], axis=1)
    q_base, k_base = base[0], base[1]

    def step(j, acc, masked):
        off = pl.multiple_of(j * bk, bk)
        kv = kv_ref[pl.ds(off, bk), :]
        k, v = kv[:, :HD], kv[:, HD:]
        probs = jnp.exp2(nt(k, both) * (SCALE * LOG2E) - lse)
        if masked:
            ki = k_base + off + lax.broadcasted_iota(jnp.int32, (bk, bq), 0)
            qi = q_base + i * bq + lax.broadcasted_iota(jnp.int32, (bk, bq), 1)
            allowed = (ki <= qi) & (ki >= seg_ref[0])
            probs = jnp.where(jnp.concatenate([allowed, allowed], axis=1), probs, 0.0)
        dscores = (probs * (nt(v, both_do) - delta)).astype(BF16)
        dv[pl.ds(off, bk), :] += nn(probs.astype(BF16), both_do)
        dk[pl.ds(off, bk), :] += nn(dscores, both)
        return acc + tn(k, dscores)

    acc = key_loops(
        segment, base, i, bq, bk, kv_ref.shape[0], step, jnp.zeros((HD, 2 * bq), F32)
    )
    acc = jnp.transpose(acc) * SCALE
    acc = jnp.concatenate([acc[:bq], acc[bq:]], axis=1)
    dq_ref[...] = acc if first else dq_in[...] + acc

    @pl.when(i == pl.num_programs(0) - 1)
    def _():
        dkv_ref[...] = jnp.concatenate([dk[...] * SCALE, dv[...]], axis=1).astype(dkv_ref.dtype)


def attention_backward(q, kv, seg, do, out, lse, segment, base, bq, bk, dq_in=None):
    rows, keys = q.shape[0], kv.shape[0]
    first = dq_in is None
    row = lambda i, *_: (i, 0)
    everything = lambda i, *_: (0, 0)
    flat = lambda i, *_: (i, 0, 0)
    in_specs = [
        pl.BlockSpec((bq, 2 * HD), row),
        pl.BlockSpec((keys, 2 * HD), everything),
        pl.BlockSpec((1, 1, bq), flat),
        pl.BlockSpec((bq, 2 * HD), row),
        pl.BlockSpec((bq, 2 * HD), row),
        pl.BlockSpec((1, 1, 2 * bq), flat),
    ]
    args = [q, kv, seg, do, out, lse]
    if not first:
        in_specs.append(pl.BlockSpec((bq, 2 * HD), row))
        args.append(dq_in)
    return pl.pallas_call(
        functools.partial(bwd_kernel, bq, bk, first),
        grid_spec=pltpu.PrefetchScalarGridSpec(
            num_scalar_prefetch=2,
            grid=(rows // bq,),
            in_specs=in_specs,
            out_specs=[pl.BlockSpec((bq, 2 * HD), row), pl.BlockSpec((keys, 2 * HD), everything)],
            scratch_shapes=[pltpu.VMEM((keys, HD), F32), pltpu.VMEM((keys, HD), F32)],
        ),
        out_shape=[
            jax.ShapeDtypeStruct((rows, 2 * HD), F32),
            jax.ShapeDtypeStruct((keys, 2 * HD), BF16 if first else F32),
        ],
        compiler_params=pltpu.CompilerParams(vmem_limit_bytes=VMEM_LIMIT),
        cost_estimate=LONG,
        name="attn_bwd_first" if first else "attn_bwd_last",
    )(segment, base, *args)


def run(kernel, name, grid, scalars, inputs, outputs, scratch=(), cost=COST):
    return pl.pallas_call(
        kernel,
        grid_spec=pltpu.PrefetchScalarGridSpec(
            num_scalar_prefetch=1,
            grid=grid,
            in_specs=[
                pl.BlockSpec(memory_space=pl.ANY) if block is None else pl.BlockSpec(block, index)
                for _, block, index in inputs
            ],
            out_specs=[
                pl.BlockSpec(memory_space=pl.ANY) if block is None else pl.BlockSpec(block, index)
                for _, _, block, index in outputs
            ],
            scratch_shapes=list(scratch),
        ),
        out_shape=[jax.ShapeDtypeStruct(shape, kind) for shape, kind, _, _ in outputs],
        compiler_params=pltpu.CompilerParams(vmem_limit_bytes=VMEM_LIMIT),
        cost_estimate=cost,
        name=name,
    )(scalars, *[array for array, _, _ in inputs])


def fixed(*index):
    return lambda i, s: index


def whole(array):
    return (array, array.shape, fixed(*(0,) * array.ndim))


def out_whole(shape, kind):
    return (shape, kind, shape, fixed(*(0,) * len(shape)))


def place_matrix(back):
    at_row = lax.broadcasted_iota(jnp.int32, (4 * HD, 4 * HD), 0)
    at_col = lax.broadcasted_iota(jnp.int32, (4 * HD, 4 * HD), 1)
    if back:
        at_row, at_col = at_col, at_row
    part = HD // 2
    moved = at_row // part % 2 * (2 * HD) + at_row // HD * part + at_row % part
    return jnp.where(moved == at_col, 1.0, 0.0).astype(BF16)


def head_means(value):
    at_row = lax.broadcasted_iota(jnp.int32, (2 * HD, 2 * HD), 0) // (HD // 2)
    at_col = lax.broadcasted_iota(jnp.int32, (2 * HD, 2 * HD), 1) // (HD // 2)
    same = jnp.where(at_row == at_col, 1.0 / HD, 0.0).astype(BF16)
    high = value.astype(BF16)
    rest = value - high.astype(F32)
    middle = rest.astype(BF16)
    return nn(high, same) + nn(middle, same) + nn((rest - middle.astype(F32)).astype(BF16), same)


def rotation(step, inner, outer):
    cos_in, sin_in = inner[0], inner[1]
    cos_out, sin_out = outer[0, pl.ds(step, 1)], outer[1, pl.ds(step, 1)]
    return cos_in * cos_out - sin_in * sin_out, sin_in * cos_out + cos_in * sin_out


def head_root(first, second):
    lane = lax.broadcasted_iota(jnp.int32, first.shape, 1)
    root = lax.rsqrt(head_means(first * first + second * second) + EPS)
    return jnp.where(lane < 3 * (HD // 2), root, 1.0), lane


def pieces_kernel(at, gate_up, down, gate_o, down_o):
    gate_o[...] = gate_up[0]
    down_o[...] = down[...]


def prepare_kernel(
    at, q, kv, out_w, up_gate_up, lower_down, up_q, up_kv, lower_out,
    qkv_o, rows_o, small_o, upper_o, low_o,
):
    k = at[0]
    value = kv[...].astype(F32)
    value = jnp.where(k == 0, value[:, :, :HD], value[:, :, HD:]).astype(BF16)
    value = jnp.concatenate([q[...], value[0], value[1]], axis=1)
    qkv_o[...] = nt(place_matrix(True), value).astype(BF16)
    rows_o[...] = out_w[...]
    small_o[:2] = up_gate_up[0]
    small_o[2] = lower_down[0]
    table = up_kv[0].astype(F32)
    table = jnp.where(k == 0, table[:, :, :HD], table[:, :, HD:]).astype(BF16)
    zero = jnp.zeros_like(table[0])
    wide = jnp.zeros((RANK, 2 * HD), BF16)
    rows = [
        jnp.concatenate([up_q[0], wide], axis=1),
        jnp.concatenate([wide, table[0], zero], axis=1),
        jnp.concatenate([wide, zero, table[1]], axis=1),
    ] + [jnp.concatenate([wide, wide], axis=1)] * 5
    upper_o[...] = nt(place_matrix(True), jnp.concatenate(rows, axis=0)).astype(BF16)
    table = jnp.transpose(lower_out[0].astype(F32))
    low_o[...] = jnp.concatenate(
        [table, jnp.zeros((table.shape[0], 2 * HD - RANK), F32)], axis=1
    ).astype(BF16)


def project_kernel(
    at, own, oth, gain, dense, lower, upper, inner, outer, gains,
    normal_o, narrow_o, q_o, kv_o, raw_o, weights,
):
    width = 4 * HD
    step = pl.program_id(0)
    steps = pl.num_programs(0)

    @pl.when(step == 0)
    def _():
        weights[:width] = dense[...]
        weights[width : width + 3 * RANK] = lower[0]
        weights[width + 3 * RANK :] = jnp.zeros(
            (weights.shape[0] - width - 3 * RANK, weights.shape[1]), BF16
        )

    value = jnp.where(step < steps // 2, own[...].astype(F32), oth[...].astype(F32))
    root = lax.rsqrt(jnp.mean(value * value, axis=1, keepdims=True) + EPS)
    normal = (value * root * gain[...]).astype(BF16)
    normal_o[...] = normal
    raw = nt(normal, weights[...])
    narrow = raw[:, width:].astype(BF16)
    narrow_o[...] = narrow[:, : 3 * RANK]
    raw = raw[:, :width] + ADAPTER_SCALING * nt(narrow, upper[...])
    raw_o[...] = raw
    first, second = raw[:, : 2 * HD], raw[:, 2 * HD :]
    root, _ = head_root(first, second)
    place = jnp.where(step < steps // 2, at[0] * (steps // 2) + step, (1 - at[0]) * (steps // 2) + step - steps // 2)
    cos, sin = rotation(place, inner, outer)
    first = first * root * gains[0:1]
    second = second * root * gains[1:2]
    turned = jnp.concatenate([first * cos - second * sin, second * cos + first * sin], axis=1)
    out = nn(turned.astype(BF16), place_matrix(True)).astype(BF16)
    q_o[...] = out[:, : 2 * HD]
    kv_o[...] = out[:, 2 * HD :]


def project_back_kernel(
    at, dq, dkv, dkv_after, raw, inner, outer, gains, narrow, normal, upper,
    out, wide_o, heads_o, wide, heads,
):
    step = pl.program_id(0)

    @pl.when(step == 0)
    def _():
        wide[...] = jnp.zeros_like(wide)
        heads[...] = jnp.zeros_like(heads)

    cos, sin = rotation(2 * step, inner, outer)
    grad_kv = (dkv[...] + dkv_after[...].astype(F32)).astype(BF16)
    grad = nn(jnp.concatenate([dq[...].astype(BF16), grad_kv], axis=1), place_matrix(False))
    first, second = raw[:, : 2 * HD], raw[:, 2 * HD :]
    root, lane = head_root(first, second)
    first, second = first * root, second * root
    back_first = grad[:, : 2 * HD] * cos + grad[:, 2 * HD :] * sin
    back_second = grad[:, 2 * HD :] * cos - grad[:, : 2 * HD] * sin
    back_first = back_first * gains[0:1]
    back_second = back_second * gains[1:2]
    mean = head_means(back_first * first + back_second * second)
    mean = jnp.where(lane < 3 * (HD // 2), mean, 0.0)
    back_first = (root * (back_first - first * mean)).astype(BF16)
    back_second = (root * (back_second - second * mean)).astype(BF16)
    grad = jnp.concatenate([back_first, back_second], axis=1)
    out[...] = grad
    inside = (ADAPTER_SCALING * nn(grad, upper[...])).astype(BF16)
    wide[...] += tn(inside[:, : 3 * RANK], normal[...])
    heads[...] += tn(narrow[...], grad)

    @pl.when(step == pl.num_programs(0) - 1)
    def _():
        wide_o[...] = wide[...].astype(BF16)
        total = (heads[...] * ADAPTER_SCALING).astype(BF16)
        total = nn(total, place_matrix(True))
        total = jnp.concatenate(
            [
                total[:RANK, : 2 * HD],
                total[RANK : 2 * RANK, 2 * HD : 3 * HD],
                total[2 * RANK :, 3 * HD :],
            ],
            axis=1,
        )
        zero = jnp.zeros_like(total)
        heads_o[:, : 4 * HD] = jnp.where(at[0] == 0, total, zero).astype(BF16)
        heads_o[:, 4 * HD :] = jnp.where(at[0] == 0, zero, total).astype(BF16)


def head_blocks(value, which):
    return jnp.concatenate([value[which * 4 + place] for place in range(4)], axis=1)


def mix_kernel(at, mixed, out_own, out_oth, upper, tokens, gain, hidden_o, normal_o, narrow_o):
    k = at[0]
    width = tokens.shape[2]
    total = nn(head_blocks(mixed, k), out_own[...]) + nn(head_blocks(mixed, 1 - k), out_oth[...])
    narrow = total[:, width : width + RANK].astype(BF16)
    narrow_o[...] = narrow
    total = tokens[0].astype(F32) + total[:, :width] + ADAPTER_SCALING * nn(narrow, upper[0])
    hidden_o[...] = total
    root = lax.rsqrt(jnp.mean(total * total, axis=1, keepdims=True) + EPS)
    normal_o[...] = (total * root * gain[...]).astype(BF16)


def norm_back(value, grad, gain):
    root = lax.rsqrt(jnp.mean(value * value, axis=1, keepdims=True) + EPS)
    unit = value * root
    grad = grad * gain
    return root * (grad - unit * jnp.mean(grad * unit, axis=1, keepdims=True))


def mix_back_kernel(
    at, hidden, cotangent, own, arrived, far, gain, out_own, out_oth, upper,
    grad_o, low_o, mixed_o, narrow_o,
):
    k = at[0]
    rows = hidden.shape[0]
    grad = own[:rows].astype(F32) + arrived[:rows].astype(F32) + far[...].astype(F32)
    grad = cotangent[0].astype(F32) + norm_back(hidden[...], grad, gain[...])
    grad_o[...] = grad
    low = grad.astype(BF16)
    low_o[...] = low
    table = jnp.transpose(upper[0].astype(F32))
    table = jnp.concatenate([table, jnp.zeros((table.shape[0], 2 * HD - RANK), F32)], axis=1)
    narrow = (ADAPTER_SCALING * nn(low, table.astype(BF16))).astype(BF16)
    narrow_o[...] = narrow[:, :RANK]
    low = jnp.concatenate([low, narrow], axis=1)
    for which, source in ((k, out_own), (1 - k, out_oth)):
        value = nt(low, source[...]).astype(BF16)
        for place in range(4):
            mixed_o[which * 4 + place] = value[:, place * 2 * HD : (place + 1) * 2 * HD]


def mix_grads_kernel(at, mixed, low, narrow, narrow_back, out_o):
    out_o[:RANK] = (ADAPTER_SCALING * tn(narrow[...], low[...])).astype(BF16)
    for i in range(8):
        value = tn(narrow_back[...], mixed[i])
        out_o[RANK:, i * 2 * HD : (i + 1) * 2 * HD] = value.astype(BF16)


def last_kernel(at, grads, own, own_x, oth, oth_x, lower, hidden, tokens, gain, out):
    k, x = at[0], at[1]
    width = hidden.shape[1]
    total = 0.0
    for which, side, source in ((k, x, own), (k, 1 - x, own_x), (1 - k, x, oth), (1 - k, 1 - x, oth_x)):
        lanes = pl.ds(pl.multiple_of(side * 2 * HD, 2 * HD), 2 * HD)
        value = [grads[which * 4 + place, :, lanes] for place in range(4)]
        total += nn(jnp.concatenate(value, axis=1), source[...])
    narrow = (ADAPTER_SCALING * total[:, width : width + 3 * RANK]).astype(BF16)
    total = total[:, :width] + nn(narrow, lower[0])
    value = tokens[0].astype(F32)
    out[...] = (hidden[...] + norm_back(value, total, gain[...])).astype(BF16)


def weight_copies(at, sources, dst, sem, down):
    k, x, y = at[0], at[1], at[2]

    def lanes(start, size):
        return pl.ds(pl.multiple_of(start, 2 * HD), size)

    def rows(start, size):
        return pl.ds(pl.multiple_of(start, 16), size)

    if down:
        height, width = dst.shape[0], sources[0].shape[1]
    else:
        height, width = sources[0].shape[1:]
    if len(sources) == 1:
        if down:
            pairs = [(sources[0], dst.at[:, pl.ds(0, width)])]
        else:
            pairs = [
                (sources[0].at[m], dst.at[pl.ds(0, height), pl.ds(m * width, width)])
                for m in range(2)
            ]
        return [
            (None, [pltpu.make_async_copy(a, b, sem.at[i]) for i, (a, b) in enumerate(pairs)])
        ]
    local, mine, *pieces = sources
    zero, one = [], []
    if down:
        part = height // 2
        for j, source in enumerate((local, mine)):
            zero.append((source, dst.at[:, lanes((y + j) % 2 * width, width)]))
        for j, source in enumerate(pieces):
            at_row = rows((x + j) % 2 * part, part)
            one.append((source, dst.at[at_row, lanes((y + j // 2) % 2 * width, width)]))
    else:
        for j, source in enumerate((local, mine)):
            for m in range(2):
                at_row = rows((y + j) % 2 * height, height)
                zero.append((source.at[m], dst.at[at_row, pl.ds(m * width, width)]))
        for j, source in enumerate(pieces):
            at_row = rows((y + j // 2) % 2 * height, height)
            one.append((source, dst.at[at_row, lanes((x + j) % 2 * width, width)]))
    return [
        (when, [pltpu.make_async_copy(a, b, sem.at[i]) for i, (a, b) in enumerate(pairs)])
        for when, pairs in ((k == 0, zero), (k == 1, one))
    ]


def for_copies(groups, what):
    for when, copies in groups:
        if when is None:
            for copy in copies:
                what(copy)
        else:

            @pl.when(when)
            def _():
                for copy in copies:
                    what(copy)


def put_down_lower(down, small):
    width = 2 * HD
    table = jnp.transpose(small[2].astype(F32))
    table = jnp.concatenate(
        [table, jnp.zeros((table.shape[0], width - table.shape[1]), F32)], axis=1
    )
    down[:, down.shape[1] - width :] = table.astype(BF16)


def both_tokens(step, own, far, own_oth, far_oth):
    here = jnp.concatenate([own[...], far[...]], axis=0).astype(F32)
    there = jnp.concatenate([own_oth[...], far_oth[...]], axis=0).astype(F32)
    return jnp.where(step == 0, here, there).astype(BF16)


def wide_table(table):
    table = jnp.transpose(table.astype(F32))
    return jnp.concatenate(
        [table, jnp.zeros((table.shape[0], 2 * HD - table.shape[1]), F32)], axis=1
    ).astype(BF16)


def ffn_kernel(many, at, own, far, own_oth, far_oth, cot, cot_far, cot_oth, cot_far_oth, *rest):
    lower, small, upper = rest[:3]
    sources, down_sources = rest[3 : 3 + many], rest[3 + many : 3 + 2 * many]
    part_own, part_oth, act_o, grad_o, narrow_o, back_o, weights, down, tables, sem = rest[
        3 + 2 * many :
    ]
    step = pl.program_id(0)
    units = small.shape[2]
    first = weight_copies(at, sources, weights, sem.at[0], False)
    second = weight_copies(at, down_sources, down, sem.at[1], True)

    @pl.when(step == 0)
    def _():
        for_copies(first, lambda copy: copy.start())
        for_copies(second, lambda copy: copy.start())
        put_down_lower(down, small)
        tables[0] = wide_table(lower[0][3 * RANK :])
        tables[1] = wide_table(upper[0])
        for_copies(first, lambda copy: copy.wait())
        for i in range(2):
            term = lower[0][(3 + i) * RANK : (4 + i) * RANK]
            at_lanes = slice(i * units, (i + 1) * units)
            merged = weights[:, at_lanes].astype(F32) + ADAPTER_SCALING * tn(term, small[i])
            weights[:, at_lanes] = merged.astype(BF16)
        for_copies(second, lambda copy: copy.wait())

    value = both_tokens(step, own, far, own_oth, far_oth)
    grad = both_tokens(step, cot.at[0], cot_far.at[0], cot_oth, cot_far_oth)
    narrow_o[0] = nn(value, tables[0]).astype(BF16)[:, : 2 * RANK]
    narrow = (ADAPTER_SCALING * nn(grad, tables[1])).astype(BF16)
    back_o[0] = narrow[:, :RANK]
    grad = jnp.concatenate([grad, narrow], axis=1)
    both = nn(value, weights[...])
    gate, up = both[:, :units], both[:, units:]
    grad_act = nt(grad, down[...])
    sig = 0.5 * jnp.tanh(0.5 * gate) + 0.5
    silu = gate * sig
    act_o[0] = (silu * up).astype(BF16)
    grad_gate = (grad_act * up * (sig + silu * (1.0 - sig))).astype(BF16)
    grad_up = (grad_act * silu).astype(BF16)
    grad_both = jnp.concatenate([grad_gate, grad_up], axis=1)
    grad_o[0] = grad_both
    part = nt(grad_both, weights[...]).astype(BF16)

    @pl.when(step == 0)
    def _():
        part_own[...] = part

    @pl.when(step == 1)
    def _():
        part_oth[...] = part


def ffn_down_kernel(many, at, act, small, upper, *rest):
    sources = rest[:many]
    part_own, part_oth, zd_o, down, sem = rest[many:]
    step = pl.program_id(0)
    width = upper.shape[2]
    copies = weight_copies(at, sources, down, sem.at[0], True)

    @pl.when(step == 0)
    def _():
        for_copies(copies, lambda copy: copy.start())
        put_down_lower(down, small)
        for_copies(copies, lambda copy: copy.wait())

    part = nn(act[0], down[...])
    zd = part[:, width : width + RANK].astype(BF16)
    zd_o[0] = zd
    part = (part[:, :width] + ADAPTER_SCALING * nn(zd, upper[0])).astype(BF16)

    @pl.when(step == 0)
    def _():
        part_own[...] = part

    @pl.when(step == 1)
    def _():
        part_oth[...] = part


def ffn_grads_kernel(at, own, far, own_oth, far_oth, cot, cot_far, cot_oth, cot_far_oth, *rest):
    act, grads, narrow, narrow_back, zd, small, wide_o, quarter_o, lanes, wide, quarter = rest
    step = pl.program_id(0)
    units = small.shape[2]

    @pl.when(step == 0)
    def _():
        wide[...] = jnp.zeros_like(wide)
        quarter[...] = jnp.zeros_like(quarter)
        lanes[...] = jnp.zeros_like(lanes)
        for i in range(2):
            table = jnp.transpose(small[i].astype(F32))
            zero = jnp.zeros_like(table)
            table = jnp.concatenate([table, zero] if i == 0 else [zero, table], axis=1)
            lanes[i * units : (i + 1) * units, : 2 * RANK] = table.astype(BF16)

    value = both_tokens(step, own, far, own_oth, far_oth)
    grad = both_tokens(step, cot.at[0], cot_far.at[0], cot_oth, cot_far_oth)
    inner = (ADAPTER_SCALING * nn(grads[0], lanes[...])).astype(BF16)[:, : 2 * RANK]
    wide[:RANK] += ADAPTER_SCALING * tn(zd[0], grad)
    wide[RANK:] += tn(inner, value)
    both = tn(narrow[0], grads[0])
    quarter[:RANK] += ADAPTER_SCALING * both[:RANK, :units]
    quarter[RANK : 2 * RANK] += ADAPTER_SCALING * both[RANK:, units:]
    quarter[2 * RANK :] += tn(narrow_back[0], act[0])

    @pl.when(step == 1)
    def _():
        wide_o[...] = wide[...].astype(BF16)
        quarter_o[...] = quarter[...].astype(BF16)


def assemble_kernel(at, own, *rest):
    z = at[4]
    up, down, out = rest[:3], rest[3:6], rest[6]
    place = pl.program_id(0)

    @pl.when(place == z)
    def _():
        out[0] = own[...].astype(out.dtype)

    for d in range(3):

        @pl.when(z - place == d + 1)
        def _():
            out[0] = up[d][...].astype(out.dtype)

        @pl.when(place - z == d + 1)
        def _():
            out[0] = down[d][...].astype(out.dtype)


def plus(here, there):
    return (here.astype(F32) + there.astype(F32)).astype(BF16)


def tie(*values):
    return lax.optimization_barrier(values)


def tie_all(values):
    return lax.optimization_barrier(values)


def heads_tokens(value):
    return lax.all_to_all(value, CT, 0, 0, axis_index_groups=COLUMN, tiled=True)


UP = [(i, i + 1) for i in range(3)]
DOWN = [(i + 1, i) for i in range(3)]


def body(
    shards,
    inputs,
    cotangent,
    segments,
    adapter_index,
    query_weight,
    key_value_weight,
    output_weight,
    gate_up_weight,
    down_weight,
    norm_attn,
    norm_ffn,
    q_gain,
    k_gain,
    input_adapter_lower,
    query_adapter_upper,
    key_value_adapter_upper,
    gate_up_adapter_upper,
    output_adapter_lower,
    output_adapter_upper,
    down_adapter_lower,
    down_adapter_upper,
):
    ctx = lax.axis_index("ctx")
    x, k = ctx // 2, ctx % 2
    z = lax.axis_index("tp")
    y = lax.axis_index("shard")
    tok = inputs.shape[1]
    half = 2 * tok
    sub = tok // 4
    width = inputs.shape[2]
    hidden_units = gate_up_weight.shape[2]
    slot = adapter_index[0]
    segment = segments[0]
    pair = shards == 2
    swap_y = [(0, 1), (1, 0)]
    cols = 2 * HD
    at = jnp.stack([k, x, y, slot, z]).astype(jnp.int32)
    K, X, Y, SLOT, Z = range(5)

    def shard_rows(piece, axis):
        if pair:
            return order2(piece, lax.ppermute(piece, "shard", swap_y), y, axis)
        return lax.all_gather(piece, "shard", axis=axis, tiled=True)

    def over_y(cores):
        return [
            ((s * 4 + c) * 4 + t, ((s ^ 1) * 4 + c) * 4 + t)
            for s in range(2)
            for c in cores
            for t in range(4)
        ]

    tokens_other = lax.ppermute(inputs[0], "ctx", CORE)
    by_slot = lambda i, s: (s[SLOT], 0, 0)
    prepared = run(
        prepare_kernel,
        "prepare",
        (1,),
        at,
        [
            (query_weight, (query_weight.shape[0], cols), lambda i, s: (0, s[K])),
            whole(key_value_weight),
            (output_weight, (cols, output_weight.shape[1]), lambda i, s: (s[K], 0)),
            (gate_up_adapter_upper, (1, 2, RANK, hidden_units), lambda i, s: (s[SLOT], 0, 0, 0)),
            (jnp.swapaxes(down_adapter_lower, 1, 2), (1, RANK, hidden_units), by_slot),
            (query_adapter_upper, (1, RANK, cols), lambda i, s: (s[SLOT], 0, s[K])),
            (key_value_adapter_upper, (1, 2, RANK, cols), lambda i, s: (s[SLOT], 0, 0, 0)),
            (
                jnp.swapaxes(output_adapter_lower, 1, 2),
                (1, RANK, cols),
                lambda i, s: (s[SLOT], 0, s[K]),
            ),
        ],
        [
            out_whole((2 * cols, query_weight.shape[0]), BF16),
            out_whole((cols, output_weight.shape[1]), BF16),
            out_whole((3, RANK, hidden_units), BF16),
            out_whole((2 * cols, cols), BF16),
            out_whole((cols, cols), BF16),
        ],
    )
    dense_piece, rows_piece, small_ffn, upper_qkv, low_rows = prepared
    dense_qkv = shard_rows(dense_piece, 1)
    rows_here = shard_rows(rows_piece, 1)

    far_z = [(c * 4 + t, c * 4 + (t ^ 2)) for c in (1, 3) for t in range(4)]
    far_x = [(1, 3), (3, 1)]
    if pair:
        piece_g, piece_d = run(
            pieces_kernel,
            "pieces",
            (1,),
            at,
            [
                (gate_up_weight, (1,) + gate_up_weight.shape[1:], lambda i, s: (s[X], 0, 0)),
                (down_weight, (hidden_units // 2, down_weight.shape[1]), lambda i, s: (s[X], 0)),
            ],
            [
                out_whole(gate_up_weight.shape[1:], BF16),
                out_whole((hidden_units // 2, down_weight.shape[1]), BF16),
            ],
        )
        piece_g = lax.ppermute(piece_g, CT, far_z)
        piece_d = lax.ppermute(piece_d, CT, far_z)

    block = tok // 4
    blocks = half // block
    half_dim = HD // 2
    first_query = x * half
    inverse = THETA ** (-(jnp.arange(half_dim, dtype=F32) * 2.0 / HD))
    inverse = jnp.concatenate([inverse] * 3 + [jnp.zeros_like(inverse)])

    def turns(places):
        angles = places.astype(F32)[:, None] * inverse[None, :]
        return jnp.stack([jnp.cos(angles), jnp.sin(angles)])

    inner = turns(jnp.arange(2 * block, dtype=jnp.int32))
    outer = turns(first_query + block * jnp.arange(blocks, dtype=jnp.int32))

    by_row = lambda i, s: (i, 0)
    by_step = lambda i, s: (i, 0, 0)
    lower_table = jnp.swapaxes(input_adapter_lower, 1, 2)
    lower_spec = (lower_table, (1, 5 * RANK, width), by_slot)
    ones = jnp.ones((half_dim,), F32)
    gains = jnp.stack(
        [
            jnp.concatenate([q_gain[part], q_gain[part], k_gain[part], ones])
            for part in (slice(0, half_dim), slice(half_dim, HD))
        ]
    )
    gain_attn, gain_ffn = norm_attn[None], norm_ffn[None]
    own_row = lambda i, s: (jnp.minimum(i, 3), 0)
    oth_row = lambda i, s: (jnp.maximum(i - 4, 0), 0)
    chip_row = lambda i, s: (jnp.where(i < 4, s[K] * 4 + i, (1 - s[K]) * 4 + i - 4), 0)
    normalized, narrow, queries, keyvals, raw = run(
        project_kernel,
        "project",
        (8,),
        at,
        [
            (inputs[0], (block, width), own_row),
            (tokens_other, (block, width), oth_row),
            whole(gain_attn),
            whole(dense_qkv),
            (lower_table, (1, 3 * RANK, width), by_slot),
            whole(upper_qkv),
            (inner, (2, block, cols), fixed(0, 0, 0)),
            whole(outer),
            whole(gains),
        ],
        [
            ((half, width), BF16, (block, width), chip_row),
            ((half, 3 * RANK), BF16, (block, 3 * RANK), chip_row),
            ((half, cols), BF16, (block, cols), chip_row),
            ((half, cols), BF16, (block, cols), chip_row),
            ((half, 2 * cols), F32, (block, 2 * cols), chip_row),
        ],
        [pltpu.VMEM((3 * cols, width), BF16)],
    )
    keyvals_before = lax.ppermute(keyvals, "ctx", [(0, 2), (1, 3)])

    base_here = jnp.stack([first_query, first_query]).astype(jnp.int32)
    base_before = jnp.stack([first_query, first_query - half]).astype(jnp.int32)
    segment_here = lax.dynamic_slice_in_dim(segment, first_query, half)
    size = half // 4
    seg_rows = segment_here.reshape(half // size, 1, size)
    keyvals, small_from = tie(keyvals, small_ffn)
    small_far = lax.ppermute(small_from, "tp", Z_XOR[2])
    if pair:
        keyvals, gate_up_from = tie(keyvals, gate_up_weight)
        mine_g = lax.ppermute(gate_up_from, SCT, over_y((0, 2)))
    acc = attention_forward(queries, keyvals, seg_rows, segment, base_here, size, size)
    acc, cot_here, out_rows = tie(acc, cotangent[0], jnp.concatenate([rows_here, low_rows], axis=1))
    out_own = lax.all_gather(out_rows, "tp", axis=0, tiled=True)
    cot_oth = lax.ppermute(cot_here, "ctx", CORE)
    if pair:
        acc, piece_g = tie(acc, piece_g)
        piece_gx = lax.ppermute(piece_g, "ctx", far_x)
        piece_gy = lax.ppermute(piece_g, SCT, over_y((1, 3)))
    mixed, mixed_low, lse = attention_forward(
        queries, keyvals_before, seg_rows, segment, base_before, size, 2 * size, acc
    )
    mixed_low, small_far = tie(mixed_low, small_far)
    small_ffn = jnp.where(k == 0, small_ffn, small_far)
    if pair:
        mixed_low, piece_d, piece_gx, piece_gy, down_from = tie(
            mixed_low, piece_d, piece_gx, piece_gy, down_weight
        )
        mine_d = lax.ppermute(down_from, SCT, over_y((0, 2)))
        piece_gxy = lax.ppermute(piece_gy, "ctx", far_x)
        piece_dx = lax.ppermute(piece_d, "ctx", far_x)
        piece_dy = lax.ppermute(piece_d, SCT, over_y((1, 3)))

    mixed_all = heads_tokens(mixed_low.reshape(8, sub, cols))
    qkv_rows = rows_at(jnp.concatenate([dense_qkv, upper_qkv], axis=1), x, cols)
    mixed_all, small_ffn, cot_oth, qkv_rows = tie(mixed_all, small_ffn, cot_oth, qkv_rows)
    out_oth = lax.ppermute(out_own, "ctx", CORE)
    if pair:
        mixed_all, mine_g, piece_gxy, piece_dx, piece_dy, out_own = tie(
            mixed_all, mine_g, piece_gxy, piece_dx, piece_dy, out_own
        )
        piece_dxy = lax.ppermute(piece_dy, "ctx", far_x)
        sources = [gate_up_weight, mine_g, piece_g, piece_gx, piece_gy, piece_gxy]
        down_sources = [down_weight, mine_d, piece_d, piece_dx, piece_dy, piece_dxy]
    else:
        full_g = lax.all_gather(gate_up_weight, "shard", axis=1, tiled=True)
        full_d = lax.all_gather(down_weight, "shard", axis=1, tiled=True)
        sources = [jnp.where(k == 0, full_g, lax.ppermute(full_g, "tp", Z_XOR[2]))]
        down_sources = [jnp.where(k == 0, full_d, lax.ppermute(full_d, "tp", Z_XOR[2]))]
    z_block = lambda i, s: (0, s[Z], 0)
    upper_out_spec = (output_adapter_upper, (1, RANK, width), lambda i, s: (s[SLOT], 0, 0))
    hidden_state, normalized_second, narrow_out = run(
        mix_kernel,
        "mix",
        (1,),
        at,
        [
            whole(mixed_all),
            whole(out_own),
            whole(out_oth),
            upper_out_spec,
            (inputs, (1, sub, width), z_block),
            whole(gain_ffn),
        ],
        [
            out_whole((sub, width), F32),
            out_whole((sub, width), BF16),
            out_whole((sub, RANK), BF16),
        ],
    )

    second = normalized_second
    second_oth = lax.ppermute(second, "ctx", CORE)
    second_far = lax.ppermute(second, "tp", Z_XOR[1])
    second_far_oth = lax.ppermute(second_far, "ctx", CORE)
    upper_down_spec = (down_adapter_upper, (1, RANK, width), by_slot)
    z_far = lambda i, s: (0, s[Z] ^ 1, 0)
    ffn_tokens = [
        whole(second),
        whole(second_far),
        whole(second_oth),
        whole(second_far_oth),
        (cotangent, (1, sub, width), z_block),
        (cotangent, (1, sub, width), z_far),
        (cot_oth, (sub, width), lambda i, s: (s[Z], 0)),
        (cot_oth, (sub, width), lambda i, s: (s[Z] ^ 1, 0)),
    ]
    tall = 2 * sub
    qkv_rows, second_far_oth = tie(qkv_rows, second_far_oth)
    qkv_own = lax.all_gather(qkv_rows, "tp", axis=0, tiled=True)
    ffn_tokens[3] = whole(second_far_oth)
    part_own, part_oth, active, grad_both, narrow_second, narrow_back_second = run(
        functools.partial(ffn_kernel, len(sources)),
        "ffn",
        (2,),
        at,
        ffn_tokens
        + [lower_spec, whole(small_ffn), upper_down_spec]
        + [(source, None, None) for source in sources + down_sources],
        [
            out_whole((tall, width), BF16),
            out_whole((tall, width), BF16),
            ((2, tall, hidden_units), BF16, (1, tall, hidden_units), by_step),
            ((2, tall, 2 * hidden_units), BF16, (1, tall, 2 * hidden_units), by_step),
            ((2, tall, 2 * RANK), BF16, (1, tall, 2 * RANK), by_step),
            ((2, tall, RANK), BF16, (1, tall, RANK), by_step),
        ],
        [
            pltpu.VMEM((width, 2 * hidden_units), BF16),
            pltpu.VMEM((hidden_units, width + cols), BF16),
            pltpu.VMEM((2, width, cols), BF16),
            pltpu.SemaphoreType.DMA((2, 4)),
        ],
        LONG,
    )
    part_arrived = lax.ppermute(part_oth, "ctx", CORE)
    part_give = (part_own[sub:].astype(F32) + part_arrived[sub:].astype(F32)).astype(BF16)
    part_give, active, qkv_own = tie(part_give, active, qkv_own)
    part_far = lax.ppermute(part_give, "tp", Z_XOR[1])
    qkv_own_x = lax.ppermute(qkv_own, "ctx", XSIDE)

    down_own, down_oth, zd = run(
        functools.partial(ffn_down_kernel, len(sources)),
        "ffn_down",
        (2,),
        at,
        [
            (active, (1, tall, hidden_units), by_step),
            whole(small_ffn),
            upper_down_spec,
        ]
        + [(source, None, None) for source in down_sources],
        [
            out_whole((tall, width), BF16),
            out_whole((tall, width), BF16),
            ((2, tall, RANK), BF16, (1, tall, RANK), by_step),
        ],
        [pltpu.VMEM((hidden_units, width + cols), BF16), pltpu.SemaphoreType.DMA((1, 4))],
        LONG,
    )
    hidden_back, down_own, down_oth, zd = tie(hidden_state, down_own, down_oth, zd)

    grad_hidden, grad_hidden_low, grad_mixed_all, narrow_back = run(
        mix_back_kernel,
        "mix_back",
        (1,),
        at,
        [
            whole(hidden_back),
            (cotangent, (1, sub, width), z_block),
            whole(part_own),
            whole(part_arrived),
            whole(part_far),
            whole(gain_ffn),
            whole(out_own),
            whole(out_oth),
            upper_out_spec,
        ],
        [
            out_whole((sub, width), F32),
            out_whole((sub, width), BF16),
            out_whole((8, sub, cols), BF16),
            out_whole((sub, RANK), BF16),
        ],
    )
    grad_mixed_all, grad_both, down_oth = tie(grad_mixed_all, grad_both, down_oth)
    grad_mixed = heads_tokens(grad_mixed_all).reshape(half, cols)
    down_arrived = lax.ppermute(down_oth, "ctx", CORE)
    down_give = (down_own[sub:].astype(F32) + down_arrived[sub:].astype(F32)).astype(BF16)
    down_far = lax.ppermute(down_give, "tp", Z_XOR[1])
    final = hidden_state + (
        down_own[:sub].astype(F32) + down_arrived[:sub].astype(F32) + down_far.astype(F32)
    )
    final = final.astype(BF16)
    wide_ffn, quarter_grads = run(
        ffn_grads_kernel,
        "ffn_grads",
        (2,),
        at,
        ffn_tokens
        + [
            (active, (1, tall, hidden_units), by_step),
            (grad_both, (1, tall, 2 * hidden_units), by_step),
            (narrow_second, (1, tall, 2 * RANK), by_step),
            (narrow_back_second, (1, tall, RANK), by_step),
            (zd, (1, tall, RANK), by_step),
            whole(small_ffn),
        ],
        [out_whole((3 * RANK, width), BF16), out_whole((3 * RANK, hidden_units), BF16)],
        [
            pltpu.VMEM((2 * hidden_units, cols), BF16),
            pltpu.VMEM((3 * RANK, width), F32),
            pltpu.VMEM((3 * RANK, hidden_units), F32),
        ],
        LONG,
    )
    (wide_mix,) = run(
        mix_grads_kernel,
        "mix_grads",
        (1,),
        at,
        [whole(mixed_all), whole(grad_hidden_low), whole(narrow_out), whole(narrow_back)],
        [out_whole((2 * RANK, width), BF16)],
    )
    wide_early = jnp.concatenate([wide_mix, wide_ffn], axis=0)
    grad_mixed, wide_early, final, qkv_own_x = tie(grad_mixed, wide_early, final, qkv_own_x)
    wide_near = lax.ppermute(wide_early, "tp", Z_XOR[1])
    out_up_1 = lax.ppermute(final, "tp", UP)
    out_down_1 = lax.ppermute(final, "tp", DOWN)
    if pair:
        slot_other = lax.ppermute(adapter_index, "shard", swap_y)[0]

    dq_before, dkv_before = attention_backward(
        queries,
        keyvals_before,
        seg_rows,
        grad_mixed,
        mixed,
        lse,
        segment,
        base_before,
        size,
        size,
    )
    dkv_after = lax.ppermute(dkv_before, "ctx", [(2, 0), (3, 1)])
    dq_before, wide_near, quarter_grads, qkv_own, qkv_own_x, out_up_1, out_down_1 = tie(
        dq_before, wide_near, quarter_grads, qkv_own, qkv_own_x, out_up_1, out_down_1
    )
    out_up_2 = lax.ppermute(out_up_1, "tp", UP)
    out_down_2 = lax.ppermute(out_down_1, "tp", DOWN)
    if pair:
        dq_before, slot_other = tie(dq_before, slot_other)
    qkv_oth = lax.ppermute(qkv_own, "ctx", CORE)
    qkv_oth_x = lax.ppermute(qkv_own_x, "ctx", CORE)
    wide_early = plus(wide_early, wide_near)
    wide_far = lax.ppermute(wide_early, "tp", Z_XOR[2])
    quarter_far = lax.ppermute(quarter_grads, "tp", Z_XOR[2])
    dq, dkv = attention_backward(
        queries,
        keyvals,
        seg_rows,
        grad_mixed,
        mixed,
        lse,
        segment,
        base_here,
        size,
        size,
        dq_before,
    )
    dq, wide_far, quarter_far, out_up_2, out_down_2 = tie(
        dq, wide_far, quarter_far, out_up_2, out_down_2
    )
    out_up_3 = lax.ppermute(out_up_2, "tp", UP)
    out_down_3 = lax.ppermute(out_down_2, "tp", DOWN)
    wide_early = plus(wide_early, wide_far)
    tall_blocks = blocks // 2
    d_projected, wide_attn, head_grads = run(
        project_back_kernel,
        "project_back",
        (tall_blocks,),
        at,
        [
            (dq, (2 * block, cols), by_row),
            (dkv, (2 * block, cols), by_row),
            (dkv_after, (2 * block, cols), by_row),
            (raw, (2 * block, 2 * cols), by_row),
            whole(inner),
            whole(outer),
            whole(gains),
            (narrow, (2 * block, 3 * RANK), by_row),
            (normalized, (2 * block, width), by_row),
            whole(upper_qkv),
        ],
        [
            ((half, 2 * cols), BF16, (2 * block, 2 * cols), by_row),
            out_whole((3 * RANK, width), BF16),
            out_whole((RANK, 4 * cols), BF16),
        ],
        [pltpu.VMEM((3 * RANK, width), F32), pltpu.VMEM((3 * RANK, 2 * cols), F32)],
        LONG,
    )
    d_projected, out_up_3, out_down_3 = tie(d_projected, out_up_3, out_down_3)

    d_all = heads_tokens(d_projected.reshape(8, sub, 2 * cols))
    def lanes_to(value, size):
        return jnp.pad(value, ((0, 0), (0, size - value.shape[1])))

    wide_count = 8 * RANK
    packed = jnp.concatenate(
        [
            lanes_to(jnp.concatenate([wide_early, wide_attn], axis=0), hidden_units),
            jnp.where(k == 0, quarter_grads, quarter_far),
            lanes_to(head_grads, hidden_units),
        ],
        axis=0,
    )

    packed = plus(packed, lax.ppermute(packed, "ctx", CORE))
    packed = plus(packed, lax.ppermute(packed, "ctx", XSIDE))
    slots = jnp.arange(ADAPT, dtype=jnp.int32)

    def placed(value, which):
        mask = (slots == which).astype(F32).reshape((ADAPT,) + (1,) * value.ndim)
        return mask * value.astype(F32)[None]

    if pair:
        both = jnp.stack([packed, lax.ppermute(packed, "shard", swap_y)])
    else:
        both = lax.psum(placed(packed, slot), "shard")
    (grad_tokens,) = run(
        last_kernel,
        "last",
        (1,),
        at,
        [
            whole(d_all),
            whole(qkv_own),
            whole(qkv_own_x),
            whole(qkv_oth),
            whole(qkv_oth_x),
            (lower_table, (1, 3 * RANK, width), by_slot),
            whole(grad_hidden),
            (inputs, (1, sub, width), z_block),
            whole(gain_attn),
        ],
        [out_whole((sub, width), BF16)],
    )
    up_1 = lax.ppermute(grad_tokens, "tp", UP)
    down_1 = lax.ppermute(grad_tokens, "tp", DOWN)
    own_width = width // (shards * 4)
    in_attn = rows_at(both[:, 5 * RANK : wide_count, :width], y * 4 + ctx, own_width, 2)
    in_attn = plus(in_attn, lax.ppermute(in_attn, "tp", Z_XOR[1]))
    up_1, down_1, in_attn, both = tie(up_1, down_1, in_attn, both)
    up_2 = lax.ppermute(up_1, "tp", UP)
    down_2 = lax.ppermute(down_1, "tp", DOWN)
    in_far = lax.ppermute(in_attn, "tp", Z_XOR[2])
    wide = both[:, : 5 * RANK, :width]
    in_ffn = rows_at(wide[:, 3 * RANK :], y * 4 + ctx, own_width, 2)
    rest = both[:, wide_count:]
    if pair:
        slots_here = (slot, slot_other)
        rest = sum(placed(rest[i], which) for i, which in enumerate(slots_here))
    quarter_sum, heads = rest[:, : 3 * RANK], rest[:, 3 * RANK :, : 4 * cols]
    grad_b_query = jnp.concatenate([heads[..., :cols], heads[..., 2 * cols : 3 * cols]], axis=-1)
    grad_b_keyval = jnp.stack(
        [
            jnp.concatenate(
                [heads[..., core * 2 * cols + c * HD :][..., :HD] for core in range(2)], axis=-1
            )
            for c in (2, 3)
        ],
        axis=1,
    )
    grad_b_gate_up = quarter_sum[:, : 2 * RANK].reshape(ADAPT, 2, RANK, -1)
    grad_a_down = jnp.swapaxes(quarter_sum[:, 2 * RANK :], 1, 2)
    in_all = jnp.concatenate([plus(in_attn, in_far), in_ffn], axis=1)
    if pair:
        wide = sum(placed(wide[i, : 3 * RANK], which) for i, which in enumerate(slots_here))
        in_all = sum(placed(in_all[i], which) for i, which in enumerate(slots_here))
    else:
        wide, in_all = wide.astype(F32), in_all.astype(F32)
    grad_b_out = wide[:, :RANK]
    grad_a_out = wide[:, RANK : 2 * RANK]
    grad_b_down = wide[:, 2 * RANK : 3 * RANK]
    grad_a_out = jnp.concatenate(
        [rows_at(grad_a_out, z, cols, 2), rows_at(grad_a_out, 4 + z, cols, 2)], axis=2
    )
    grad_a_out = jnp.swapaxes(grad_a_out, 1, 2)
    grad_adapt_in = jnp.swapaxes(in_all, 1, 2)
    up_2, down_2, final, grad_b_query, grad_b_keyval, grad_b_gate_up, grad_a_down = tie(
        up_2, down_2, final, grad_b_query, grad_b_keyval, grad_b_gate_up, grad_a_down
    )
    up_3 = lax.ppermute(up_2, "tp", UP)
    down_3 = lax.ppermute(down_2, "tp", DOWN)
    line = [grad_tokens, up_1, up_2, up_3, down_1, down_2, down_3]
    z_row = lambda i, s: (0, i, 0)
    (grad_inputs,) = run(
        assemble_kernel,
        "assemble",
        (4,),
        at,
        [whole(part) for part in line],
        [((1, tok, width), F32, (1, sub, width), z_row)],
    )
    line = [final, out_up_1, out_up_2, out_up_3, out_down_1, out_down_2, out_down_3]
    (result,) = run(
        assemble_kernel,
        "assemble_out",
        (4,),
        at,
        [whole(part) for part in line],
        [((1, tok, width), BF16, (1, sub, width), z_row)],
        cost=LONG,
    )
    return (
        result,
        grad_inputs,
        grad_adapt_in,
        grad_b_query,
        grad_b_keyval,
        grad_b_gate_up,
        grad_a_out,
        grad_b_out,
        grad_a_down,
        grad_b_down,
    )


def solution(mesh):
    return jax.shard_map(
        functools.partial(body, mesh.shape["shard"]),
        mesh=mesh,
        in_specs=(
            P("shard", "ctx", None),
            P("shard", "ctx", None),
            P("shard", None),
            P("shard"),
            P("shard", "tp"),
            P(None, "shard", "tp"),
            P("tp", "shard"),
            P(None, "shard", "tp"),
            P("tp", "shard"),
            P(),
            P(),
            P(),
            P(),
            P(),
            P(None, None, "tp"),
            P(None, None, None, "tp"),
            P(None, None, None, "tp"),
            P(None, "tp", None),
            P(),
            P(None, "tp", None),
            P(),
        ),
        out_specs=(
            P("shard", "ctx", None),
            P("shard", "ctx", None),
            P(None, ("shard", "ctx"), None),
            P(None, None, "tp"),
            P(None, None, None, "tp"),
            P(None, None, None, "tp"),
            P(None, "tp", None),
            P(),
            P(None, "tp", None),
            P(),
        ),
        check_vma=False,
    )
```

```python
import functools

import jax
import jax.numpy as jnp
from jax import lax
from jax.experimental import pallas as pl
from jax.experimental.pallas import tpu as pltpu
from jax.sharding import PartitionSpec as P

HD = 64
RANK = 16
ADAPT = 8
EPS = 1e-05
ADAPTER_SCALING = 2.0
THETA = 1000000.0
LOG2E = 1.4426950408889634
SCALE = HD**-0.5
F32 = jnp.float32
BF16 = jnp.bfloat16
VMEM_LIMIT = 62 * 1024 * 1024

CORE = [(i, i ^ 1) for i in range(4)]
XSIDE = [(i, i ^ 2) for i in range(4)]
Z_XOR = {d: [(i, i ^ d) for i in range(4)] for d in (1, 2, 3)}
CT = ("ctx", "tp")
SCT = ("shard", "ctx", "tp")
COLUMN = [[(2 * x + k) * 4 + z for k in range(2) for z in range(4)] for x in range(2)]

COST = pl.CostEstimate(flops=1 << 20, bytes_accessed=1 << 16, transcendentals=0)
LONG = pl.CostEstimate(flops=30 << 30, bytes_accessed=16 << 20, transcendentals=0)
HIGHEST = lax.Precision.HIGHEST


def nn(left, right):
    return lax.dot_general(left, right, (((1,), (0,)), ((), ())), preferred_element_type=F32)


def nt(left, right):
    return lax.dot_general(left, right, (((1,), (1,)), ((), ())), preferred_element_type=F32)


def tn(left, right):
    return lax.dot_general(left, right, (((0,), (0,)), ((), ())), preferred_element_type=F32)


def rmsnorm(value, gain):
    return value * lax.rsqrt(jnp.mean(value * value, axis=-1, keepdims=True) + EPS) * gain


def order2(own, other, bit, axis=0):
    return jnp.concatenate(
        [jnp.where(bit == 0, own, other), jnp.where(bit == 0, other, own)], axis=axis
    )


def rows_at(value, block, size, axis=0):
    return lax.dynamic_slice_in_dim(value, block * size, size, axis)


def key_loops(segment, first, key_base, bq, bk, keys, step, acc):
    blocks = keys // bk
    low = jnp.minimum(jnp.maximum(segment[first] - key_base, 0) // bk, blocks)
    high = jnp.clip((first + bq - key_base + bk - 1) // bk, 0, blocks)
    low = jnp.minimum(low, high)
    free_low = (jnp.maximum(segment[first + bq - 1] - key_base, 0) + bk - 1) // bk
    free_low = jnp.clip(free_low, low, high)
    free_high = jnp.clip(jnp.maximum(first + 1 - key_base, 0) // bk, free_low, high)
    ahead = free_low - low

    def masked(t, carry):
        j = jnp.where(t < ahead, low + t, free_high + t - ahead)
        return step(j, carry, True)

    acc = lax.fori_loop(0, ahead + high - free_high, masked, acc)
    return lax.fori_loop(free_low, free_high, lambda j, carry: step(j, carry, False), acc)


def row_sums(weights, value):
    return lax.dot_general(
        weights, value, (((1,), (1,)), ((), ())), precision=HIGHEST, preferred_element_type=F32
    )


def fwd_kernel(bq, bk, back, last, segment, at, q_ref, kv_ref, seg_ref, *rest):
    if last:
        acc_in, mixed_ref, low_ref, lse_ref, vx = rest
    else:
        acc_ref, vx = rest
    i = pl.program_id(0)
    keys = kv_ref.shape[0]

    @pl.when(i == 0)
    def _():
        col = lax.broadcasted_iota(jnp.int32, (keys, 2 * HD), 1)
        kv = kv_ref[...]
        swapped = jnp.concatenate([kv[:, HD:], kv[:, :HD]], axis=1)
        ones = jnp.where(col == HD, 1.0, 0.0).astype(BF16)
        vx[...] = jnp.where(col < HD, swapped, ones)

    q = q_ref[...]
    both = jnp.concatenate([q[:, :HD], q[:, HD:]], axis=0)
    q_base = at[1] * (bq * pl.num_programs(0))
    k_base = q_base - back
    seg_col = jnp.broadcast_to(seg_ref[0].astype(F32), (8, bq))
    seg_col = jnp.transpose(seg_col)[:, :1].astype(jnp.int32)

    def step(j, acc, masked):
        off = pl.multiple_of(j * bk, bk)
        scores = nt(both, kv_ref[pl.ds(off, bk), :HD])
        probs = jnp.exp2(scores * (SCALE * LOG2E))
        if masked:
            qi = q_base + i * bq + lax.broadcasted_iota(jnp.int32, (bq, bk), 0)
            ki = k_base + off + lax.broadcasted_iota(jnp.int32, (bq, bk), 1)
            allowed = (ki <= qi) & (ki >= seg_col)
            probs = jnp.where(jnp.concatenate([allowed, allowed], axis=0), probs, 0.0)
        return acc + nn(probs.astype(BF16), vx[pl.ds(off, bk), :])

    if last:
        acc = jnp.concatenate([acc_in[0], acc_in[1]], axis=0)
    else:
        acc = jnp.zeros((2 * bq, 2 * HD), F32)
    acc = key_loops(segment, q_base + i * bq, k_base, bq, bk, keys, step, acc)
    if last:
        total = acc[:, HD : HD + 1]
        out = acc[:, :HD] / total
        out = jnp.concatenate([out[:bq], out[bq:]], axis=1)
        mixed_ref[...] = out
        low_ref[...] = out.astype(BF16)
        pick = jnp.where(lax.broadcasted_iota(jnp.int32, (8, 2 * HD), 1) == HD, 1.0, 0.0)
        lse_ref[0] = jnp.log2(row_sums(pick, acc)[:1])
    else:
        acc_ref[0] = acc[:bq]
        acc_ref[1] = acc[bq:]


def attention_forward(q, kv, seg, segment, at, back, bq, bk, acc_in=None):
    rows, keys = q.shape[0], kv.shape[0]
    last = acc_in is not None
    row = lambda i, *_: (i, 0)
    everything = lambda i, *_: (0, 0)
    heads = lambda i, *_: (0, i, 0)
    in_specs = [
        pl.BlockSpec((bq, 2 * HD), row),
        pl.BlockSpec((keys, 2 * HD), everything),
        pl.BlockSpec((1, 1, bq), lambda i, g, a: (a[1] * (rows // bq) + i, 0, 0)),
    ]
    args = [q, kv, seg]
    if last:
        in_specs.append(pl.BlockSpec((2, bq, 2 * HD), heads))
        args.append(acc_in)
        out_specs = [
            pl.BlockSpec((bq, 2 * HD), row),
            pl.BlockSpec((bq, 2 * HD), row),
            pl.BlockSpec((1, 1, 2 * bq), lambda i, *_: (i, 0, 0)),
        ]
        out_shape = [
            jax.ShapeDtypeStruct((rows, 2 * HD), F32),
            jax.ShapeDtypeStruct((rows, 2 * HD), BF16),
            jax.ShapeDtypeStruct((rows // bq, 1, 2 * bq), F32),
        ]
    else:
        out_specs = pl.BlockSpec((2, bq, 2 * HD), heads)
        out_shape = jax.ShapeDtypeStruct((2, rows, 2 * HD), F32)
    return pl.pallas_call(
        functools.partial(fwd_kernel, bq, bk, back, last),
        grid_spec=pltpu.PrefetchScalarGridSpec(
            num_scalar_prefetch=2,
            grid=(rows // bq,),
            in_specs=in_specs,
            out_specs=out_specs,
            scratch_shapes=[pltpu.VMEM((keys, 2 * HD), BF16)],
        ),
        out_shape=out_shape,
        compiler_params=pltpu.CompilerParams(vmem_limit_bytes=VMEM_LIMIT),
        cost_estimate=LONG,
        name="attn_fwd_last" if last else "attn_fwd_first",
    )(segment, at, *args)


def bwd_kernel(
    bq, bk, back, first, segment, at, q_ref, kv_ref, seg_ref, do_ref, out_ref, lse_ref, *rest
):
    if first:
        dq_ref, dkv_ref, dk, dv = rest
    else:
        dq_in, dq_ref, dkv_ref, dk, dv = rest
    i = pl.program_id(0)

    @pl.when(i == 0)
    def _():
        dk[...] = jnp.zeros_like(dk)
        dv[...] = jnp.zeros_like(dv)

    q = q_ref[...]
    do = do_ref[...]
    both = jnp.concatenate([q[:, :HD], q[:, HD:]], axis=0)
    both_do = jnp.concatenate([do[:, :HD], do[:, HD:]], axis=0)
    lse = lse_ref[0]
    lane = lax.broadcasted_iota(jnp.int32, (8, 2 * HD), 1)
    row = lax.broadcasted_iota(jnp.int32, (8, 2 * HD), 0)
    pick = jnp.where(lane // HD == row, 1.0, 0.0)
    deltas = row_sums(pick, do.astype(F32) * out_ref[...])
    delta = jnp.concatenate([deltas[:1], deltas[1:2]], axis=1)
    q_base = at[1] * (bq * pl.num_programs(0))
    k_base = q_base - back

    def step(j, acc, masked):
        off = pl.multiple_of(j * bk, bk)
        kv = kv_ref[pl.ds(off, bk), :]
        k, v = kv[:, :HD], kv[:, HD:]
        probs = jnp.exp2(nt(k, both) * (SCALE * LOG2E) - lse)
        if masked:
            ki = k_base + off + lax.broadcasted_iota(jnp.int32, (bk, bq), 0)
            qi = q_base + i * bq + lax.broadcasted_iota(jnp.int32, (bk, bq), 1)
            allowed = (ki <= qi) & (ki >= seg_ref[0])
            probs = jnp.where(jnp.concatenate([allowed, allowed], axis=1), probs, 0.0)
        dscores = (probs * (nt(v, both_do) - delta)).astype(BF16)
        dv[pl.ds(off, bk), :] += nn(probs.astype(BF16), both_do)
        dk[pl.ds(off, bk), :] += nn(dscores, both)
        return acc + tn(k, dscores)

    acc = key_loops(
        segment, q_base + i * bq, k_base, bq, bk, kv_ref.shape[0], step,
        jnp.zeros((HD, 2 * bq), F32),
    )
    acc = jnp.transpose(acc) * SCALE
    acc = jnp.concatenate([acc[:bq], acc[bq:]], axis=1)
    dq_ref[...] = acc if first else dq_in[...] + acc

    @pl.when(i == pl.num_programs(0) - 1)
    def _():
        dkv_ref[...] = jnp.concatenate([dk[...] * SCALE, dv[...]], axis=1).astype(dkv_ref.dtype)


def attention_backward(q, kv, seg, do, out, lse, segment, at, back, bq, bk, dq_in=None):
    rows, keys = q.shape[0], kv.shape[0]
    first = dq_in is None
    row = lambda i, *_: (i, 0)
    everything = lambda i, *_: (0, 0)
    flat = lambda i, *_: (i, 0, 0)
    in_specs = [
        pl.BlockSpec((bq, 2 * HD), row),
        pl.BlockSpec((keys, 2 * HD), everything),
        pl.BlockSpec((1, 1, bq), lambda i, g, a: (a[1] * (rows // bq) + i, 0, 0)),
        pl.BlockSpec((bq, 2 * HD), row),
        pl.BlockSpec((bq, 2 * HD), row),
        pl.BlockSpec((1, 1, 2 * bq), flat),
    ]
    args = [q, kv, seg, do, out, lse]
    if not first:
        in_specs.append(pl.BlockSpec((bq, 2 * HD), row))
        args.append(dq_in)
    return pl.pallas_call(
        functools.partial(bwd_kernel, bq, bk, back, first),
        grid_spec=pltpu.PrefetchScalarGridSpec(
            num_scalar_prefetch=2,
            grid=(rows // bq,),
            in_specs=in_specs,
            out_specs=[pl.BlockSpec((bq, 2 * HD), row), pl.BlockSpec((keys, 2 * HD), everything)],
            scratch_shapes=[pltpu.VMEM((keys, HD), F32), pltpu.VMEM((keys, HD), F32)],
        ),
        out_shape=[
            jax.ShapeDtypeStruct((rows, 2 * HD), F32),
            jax.ShapeDtypeStruct((keys, 2 * HD), BF16 if first else F32),
        ],
        compiler_params=pltpu.CompilerParams(vmem_limit_bytes=VMEM_LIMIT),
        cost_estimate=LONG,
        name="attn_bwd_first" if first else "attn_bwd_last",
    )(segment, at, *args)


def run(kernel, name, grid, scalars, inputs, outputs, scratch=(), cost=COST):
    return pl.pallas_call(
        kernel,
        grid_spec=pltpu.PrefetchScalarGridSpec(
            num_scalar_prefetch=1,
            grid=grid,
            in_specs=[
                pl.BlockSpec(memory_space=pl.ANY) if block is None else pl.BlockSpec(block, index)
                for _, block, index in inputs
            ],
            out_specs=[
                pl.BlockSpec(memory_space=pl.ANY) if block is None else pl.BlockSpec(block, index)
                for _, _, block, index in outputs
            ],
            scratch_shapes=list(scratch),
        ),
        out_shape=[jax.ShapeDtypeStruct(shape, kind) for shape, kind, _, _ in outputs],
        compiler_params=pltpu.CompilerParams(vmem_limit_bytes=VMEM_LIMIT),
        cost_estimate=cost,
        name=name,
    )(scalars, *[array for array, _, _ in inputs])


def fixed(*index):
    return lambda i, s: index


def whole(array):
    return (array, array.shape, fixed(*(0,) * array.ndim))


def out_whole(shape, kind):
    return (shape, kind, shape, fixed(*(0,) * len(shape)))


def place_matrix(back):
    at_row = lax.broadcasted_iota(jnp.int32, (4 * HD, 4 * HD), 0)
    at_col = lax.broadcasted_iota(jnp.int32, (4 * HD, 4 * HD), 1)
    if back:
        at_row, at_col = at_col, at_row
    part = HD // 2
    moved = at_row // part % 2 * (2 * HD) + at_row // HD * part + at_row % part
    return jnp.where(moved == at_col, 1.0, 0.0).astype(BF16)


def head_means(value):
    at_row = lax.broadcasted_iota(jnp.int32, (2 * HD, 2 * HD), 0) // (HD // 2)
    at_col = lax.broadcasted_iota(jnp.int32, (2 * HD, 2 * HD), 1) // (HD // 2)
    same = jnp.where(at_row == at_col, 1.0 / HD, 0.0).astype(BF16)
    high = value.astype(BF16)
    rest = value - high.astype(F32)
    middle = rest.astype(BF16)
    return nn(high, same) + nn(middle, same) + nn((rest - middle.astype(F32)).astype(BF16), same)


def rotation(step, turns, rows, blocks):
    first = turns.shape[1] - blocks
    cos_in, sin_in = turns[0, :rows], turns[1, :rows]
    cos_out, sin_out = turns[0, pl.ds(first + step, 1)], turns[1, pl.ds(first + step, 1)]
    return cos_in * cos_out - sin_in * sin_out, sin_in * cos_out + cos_in * sin_out


def head_root(first, second):
    lane = lax.broadcasted_iota(jnp.int32, first.shape, 1)
    root = lax.rsqrt(head_means(first * first + second * second) + EPS)
    return jnp.where(lane < 3 * (HD // 2), root, 1.0), lane


class Lanes:
    def __init__(self, start, size):
        self.start, self.size = start, size


def down_parts(shape, width):
    rows, cols = shape
    whole = width // cols
    tall = (rows * cols) // width
    parts = [(i * tall, (i + 1) * tall, Lanes(0, cols), 0, i * cols) for i in range(whole)]
    left = rows - whole * tall
    room = width - whole * cols
    for j in range(cols // room if left else 0):
        parts.append((whole * tall, rows, Lanes(j * room, room), j * left, whole * cols))
    return parts


def pieces_kernel(at, gate_up, down, out):
    height, width = gate_up.shape[1:]
    out[:height] = gate_up[0]
    value = down[...]
    for a, b, lanes, at_row, at_lane in down_parts(value.shape, width):
        out[height + at_row : height + at_row + b - a, at_lane : at_lane + lanes.size] = value[
            a:b, lanes.start : lanes.start + lanes.size
        ]


def prepare_kernel(
    at, q, kv, out_w, up_gate_up, lower_down, up_q, up_kv, lower_out,
    rows_o, small_o, upper_o, low_o,
):
    k = at[0]
    value = kv[...].astype(F32)
    value = jnp.where(k == 0, value[:, :, :HD], value[:, :, HD:]).astype(BF16)
    value = jnp.concatenate([q[...], value[0], value[1]], axis=1)
    height = 4 * HD
    rows_o[:height] = nt(place_matrix(True), value).astype(BF16)
    rows_o[height:] = out_w[...]
    small_o[:2] = up_gate_up[0]
    small_o[2] = lower_down[0]
    table = up_kv[0].astype(F32)
    table = jnp.where(k == 0, table[:, :, :HD], table[:, :, HD:]).astype(BF16)
    zero = jnp.zeros_like(table[0])
    wide = jnp.zeros((RANK, 2 * HD), BF16)
    rows = [
        jnp.concatenate([up_q[0], wide], axis=1),
        jnp.concatenate([wide, table[0], zero], axis=1),
        jnp.concatenate([wide, zero, table[1]], axis=1),
    ] + [jnp.concatenate([wide, wide], axis=1)] * 5
    upper_o[...] = nt(place_matrix(True), jnp.concatenate(rows, axis=0)).astype(BF16)
    table = jnp.transpose(lower_out[0].astype(F32))
    low_o[...] = jnp.concatenate(
        [table, jnp.zeros((table.shape[0], 2 * HD - RANK), F32)], axis=1
    ).astype(BF16)


def project_kernel(
    at, own, oth, gain, dense, lower, upper, turns, gains,
    normal_o, narrow_o, q_o, kv_o, raw_o, weights,
):
    width = 4 * HD
    step = pl.program_id(0)
    steps = pl.num_programs(0)

    @pl.when(step == 0)
    def _():
        weights[:width] = dense[...]
        weights[width : width + 3 * RANK] = lower[0]
        weights[width + 3 * RANK :] = jnp.zeros(
            (weights.shape[0] - width - 3 * RANK, weights.shape[1]), BF16
        )

    value = jnp.where(step < steps // 2, own[...].astype(F32), oth[...].astype(F32))
    root = lax.rsqrt(jnp.mean(value * value, axis=1, keepdims=True) + EPS)
    normal = (value * root * gain[...]).astype(BF16)
    normal_o[...] = normal
    raw = nt(normal, weights[...])
    narrow = raw[:, width:].astype(BF16)
    narrow_o[...] = narrow[:, : 3 * RANK]
    raw = raw[:, :width] + ADAPTER_SCALING * nt(narrow, upper[...])
    raw_o[...] = raw
    first, second = raw[:, : 2 * HD], raw[:, 2 * HD :]
    root, _ = head_root(first, second)
    place = jnp.where(step < steps // 2, at[0] * (steps // 2) + step, (1 - at[0]) * (steps // 2) + step - steps // 2)
    cos, sin = rotation(place, turns, normal.shape[0], steps)
    first = first * root * gains[0:1]
    second = second * root * gains[1:2]
    turned = jnp.concatenate([first * cos - second * sin, second * cos + first * sin], axis=1)
    out = nn(turned.astype(BF16), place_matrix(True)).astype(BF16)
    q_o[...] = out[:, : 2 * HD]
    kv_o[...] = out[:, 2 * HD :]


def project_back_kernel(
    at, dq, dkv, dkv_after, raw, turns, gains, narrow, normal, upper,
    out, wide_o, heads_o, wide, heads,
):
    step = pl.program_id(0)

    @pl.when(step == 0)
    def _():
        wide[...] = jnp.zeros_like(wide)
        heads[...] = jnp.zeros_like(heads)

    cos, sin = rotation(2 * step, turns, dq.shape[0], 2 * pl.num_programs(0))
    grad_kv = (dkv[...] + dkv_after[...].astype(F32)).astype(BF16)
    grad = nn(jnp.concatenate([dq[...].astype(BF16), grad_kv], axis=1), place_matrix(False))
    first, second = raw[:, : 2 * HD], raw[:, 2 * HD :]
    root, lane = head_root(first, second)
    first, second = first * root, second * root
    back_first = grad[:, : 2 * HD] * cos + grad[:, 2 * HD :] * sin
    back_second = grad[:, 2 * HD :] * cos - grad[:, : 2 * HD] * sin
    back_first = back_first * gains[0:1]
    back_second = back_second * gains[1:2]
    mean = head_means(back_first * first + back_second * second)
    mean = jnp.where(lane < 3 * (HD // 2), mean, 0.0)
    back_first = (root * (back_first - first * mean)).astype(BF16)
    back_second = (root * (back_second - second * mean)).astype(BF16)
    grad = jnp.concatenate([back_first, back_second], axis=1)
    out[...] = grad
    inside = (ADAPTER_SCALING * nn(grad, upper[...])).astype(BF16)
    wide[...] += tn(inside[:, : 3 * RANK], normal[...])
    heads[...] += tn(narrow[...], grad)

    @pl.when(step == pl.num_programs(0) - 1)
    def _():
        wide_o[...] = wide[...].astype(BF16)
        total = (heads[...] * ADAPTER_SCALING).astype(BF16)
        total = nn(total, place_matrix(True))
        total = jnp.concatenate(
            [
                total[:RANK, : 2 * HD],
                total[RANK : 2 * RANK, 2 * HD : 3 * HD],
                total[2 * RANK :, 3 * HD :],
            ],
            axis=1,
        )
        zero = jnp.zeros_like(total)
        heads_o[:, : 4 * HD] = jnp.where(at[0] == 0, total, zero).astype(BF16)
        heads_o[:, 4 * HD :] = jnp.where(at[0] == 0, zero, total).astype(BF16)


def head_blocks(value, which):
    return jnp.concatenate([value[which * 4 + place] for place in range(4)], axis=1)


def mix_kernel(at, mixed, out_own, out_oth, upper, tokens, gain, hidden_o, normal_o, narrow_o):
    k = at[0]
    width = tokens.shape[2]
    total = nn(head_blocks(mixed, k), out_own[...]) + nn(head_blocks(mixed, 1 - k), out_oth[...])
    narrow = total[:, width : width + RANK].astype(BF16)
    narrow_o[...] = narrow
    total = tokens[0].astype(F32) + total[:, :width] + ADAPTER_SCALING * nn(narrow, upper[0])
    hidden_o[...] = total
    root = lax.rsqrt(jnp.mean(total * total, axis=1, keepdims=True) + EPS)
    normal_o[...] = (total * root * gain[...]).astype(BF16)


def norm_back(value, grad, gain):
    root = lax.rsqrt(jnp.mean(value * value, axis=1, keepdims=True) + EPS)
    unit = value * root
    grad = grad * gain
    return root * (grad - unit * jnp.mean(grad * unit, axis=1, keepdims=True))


def mix_back_kernel(
    at, hidden, cotangent, own, arrived, far, gain, out_own, out_oth, upper,
    grad_o, low_o, mixed_o, narrow_o,
):
    k = at[0]
    rows = hidden.shape[0]
    grad = own[:rows].astype(F32) + arrived[:rows].astype(F32) + far[...].astype(F32)
    grad = cotangent[0].astype(F32) + norm_back(hidden[...], grad, gain[...])
    grad_o[...] = grad
    low = grad.astype(BF16)
    low_o[...] = low
    table = jnp.transpose(upper[0].astype(F32))
    table = jnp.concatenate([table, jnp.zeros((table.shape[0], 2 * HD - RANK), F32)], axis=1)
    narrow = (ADAPTER_SCALING * nn(low, table.astype(BF16))).astype(BF16)
    narrow_o[...] = narrow[:, :RANK]
    low = jnp.concatenate([low, narrow], axis=1)
    for which, source in ((k, out_own), (1 - k, out_oth)):
        value = nt(low, source[...]).astype(BF16)
        for place in range(4):
            mixed_o[which * 4 + place] = value[:, place * 2 * HD : (place + 1) * 2 * HD]


def mix_grads_kernel(at, mixed, low, narrow, narrow_back, out_o):
    out_o[:RANK] = (ADAPTER_SCALING * tn(narrow[...], low[...])).astype(BF16)
    for i in range(8):
        value = tn(narrow_back[...], mixed[i])
        out_o[RANK:, i * 2 * HD : (i + 1) * 2 * HD] = value.astype(BF16)


def last_kernel(at, grads, own, own_x, oth, oth_x, lower, hidden, tokens, gain, out):
    k, x = at[0], at[1]
    width = hidden.shape[1]
    total = 0.0
    for which, side, source in ((k, x, own), (k, 1 - x, own_x), (1 - k, x, oth), (1 - k, 1 - x, oth_x)):
        lanes = pl.ds(pl.multiple_of(side * 2 * HD, 2 * HD), 2 * HD)
        value = [grads[which * 4 + place, :, lanes] for place in range(4)]
        total += nn(jnp.concatenate(value, axis=1), source[...])
    narrow = (ADAPTER_SCALING * total[:, width : width + 3 * RANK]).astype(BF16)
    total = total[:, :width] + nn(narrow, lower[0])
    value = tokens[0].astype(F32)
    out[...] = (hidden[...] + norm_back(value, total, gain[...])).astype(BF16)


def weight_copies(at, sources, dst, sem, down):
    k, x, y = at[0], at[1], at[2]

    def lanes(start, size):
        return pl.ds(pl.multiple_of(start, 2 * HD), size)

    def rows(start, size):
        return pl.ds(pl.multiple_of(start, 16), size)

    if down:
        height, width = dst.shape[0], sources[0].shape[1]
    else:
        height, width = sources[0].shape[1:]
    if len(sources) == 1:
        if down:
            pairs = [(sources[0], dst.at[:, pl.ds(0, width)])]
        else:
            pairs = [
                (sources[0].at[m], dst.at[pl.ds(0, height), pl.ds(m * width, width)])
                for m in range(2)
            ]
        return [
            (None, [pltpu.make_async_copy(a, b, sem.at[i]) for i, (a, b) in enumerate(pairs)])
        ]
    local, mine, *pieces = sources
    zero, one = [], []
    if down:
        part = height // 2
        for j, source in enumerate((local, mine)):
            zero.append((source, dst.at[:, lanes((y + j) % 2 * width, width)]))
        tall = pieces[0].shape[0] - part * width // pieces[0].shape[1]
        for j, source in enumerate(pieces):
            for a, b, cols, at_row, at_lane in down_parts((part, width), source.shape[1]):
                one.append(
                    (
                        source.at[pl.ds(tall + at_row, b - a), pl.ds(at_lane, cols.size)],
                        dst.at[
                            rows((x + j) % 2 * part + a, b - a),
                            lanes((y + j // 2) % 2 * width + cols.start, cols.size),
                        ],
                    )
                )
    else:
        for j, source in enumerate((local, mine)):
            for m in range(2):
                at_row = rows((y + j) % 2 * height, height)
                zero.append((source.at[m], dst.at[at_row, pl.ds(m * width, width)]))
        for j, source in enumerate(pieces):
            at_row = rows((y + j // 2) % 2 * height, height)
            source = source.at[pl.ds(0, height)]
            one.append((source, dst.at[at_row, lanes((x + j) % 2 * width, width)]))
    return [
        (when, [pltpu.make_async_copy(a, b, sem.at[i]) for i, (a, b) in enumerate(pairs)])
        for when, pairs in ((k == 0, zero), (k == 1, one))
    ]


def for_copies(groups, what):
    for when, copies in groups:
        if when is None:
            for copy in copies:
                what(copy)
        else:

            @pl.when(when)
            def _():
                for copy in copies:
                    what(copy)


def put_down_lower(down, small):
    width = 2 * HD
    table = jnp.transpose(small[2].astype(F32))
    table = jnp.concatenate(
        [table, jnp.zeros((table.shape[0], width - table.shape[1]), F32)], axis=1
    )
    down[:, down.shape[1] - width :] = table.astype(BF16)


def both_tokens(step, own, far, own_oth, far_oth):
    here = jnp.concatenate([own[...], far[...]], axis=0).astype(F32)
    there = jnp.concatenate([own_oth[...], far_oth[...]], axis=0).astype(F32)
    return jnp.where(step == 0, here, there).astype(BF16)


def wide_table(table):
    table = jnp.transpose(table.astype(F32))
    return jnp.concatenate(
        [table, jnp.zeros((table.shape[0], 2 * HD - table.shape[1]), F32)], axis=1
    ).astype(BF16)


def ffn_kernel(many, at, own, far, own_oth, far_oth, cot, cot_far, cot_oth, cot_far_oth, *rest):
    lower, small, upper = rest[:3]
    sources, down_sources = rest[3 : 3 + many], rest[3 + many : 3 + 2 * many]
    part_own, part_oth, act_o, grad_o, narrow_o, back_o, weights, down, tables, sem = rest[
        3 + 2 * many :
    ]
    step = pl.program_id(0)
    units = small.shape[2]
    first = weight_copies(at, sources, weights, sem.at[0], False)
    second = weight_copies(at, down_sources, down, sem.at[1], True)

    @pl.when(step == 0)
    def _():
        for_copies(first, lambda copy: copy.start())
        for_copies(second, lambda copy: copy.start())
        put_down_lower(down, small)
        tables[0] = wide_table(lower[0][3 * RANK :])
        tables[1] = wide_table(upper[0])
        for_copies(first, lambda copy: copy.wait())
        for i in range(2):
            term = lower[0][(3 + i) * RANK : (4 + i) * RANK]
            at_lanes = slice(i * units, (i + 1) * units)
            merged = weights[:, at_lanes].astype(F32) + ADAPTER_SCALING * tn(term, small[i])
            weights[:, at_lanes] = merged.astype(BF16)
        for_copies(second, lambda copy: copy.wait())

    value = both_tokens(step, own, far, own_oth, far_oth)
    grad = both_tokens(step, cot.at[0], cot_far.at[0], cot_oth, cot_far_oth)
    narrow_o[0] = nn(value, tables[0]).astype(BF16)[:, : 2 * RANK]
    narrow = (ADAPTER_SCALING * nn(grad, tables[1])).astype(BF16)
    back_o[0] = narrow[:, :RANK]
    grad = jnp.concatenate([grad, narrow], axis=1)
    both = nn(value, weights[...])
    gate, up = both[:, :units], both[:, units:]
    grad_act = nt(grad, down[...])
    sig = 0.5 * jnp.tanh(0.5 * gate) + 0.5
    silu = gate * sig
    act_o[0] = (silu * up).astype(BF16)
    grad_gate = (grad_act * up * (sig + silu * (1.0 - sig))).astype(BF16)
    grad_up = (grad_act * silu).astype(BF16)
    grad_both = jnp.concatenate([grad_gate, grad_up], axis=1)
    grad_o[0] = grad_both
    part = nt(grad_both, weights[...]).astype(BF16)

    @pl.when(step == 0)
    def _():
        part_own[...] = part

    @pl.when(step == 1)
    def _():
        part_oth[...] = part


def ffn_down_kernel(many, at, act, small, upper, *rest):
    sources = rest[:many]
    part_own, part_oth, zd_o, down, sem = rest[many:]
    step = pl.program_id(0)
    width = upper.shape[2]
    copies = weight_copies(at, sources, down, sem.at[0], True)

    @pl.when(step == 0)
    def _():
        for_copies(copies, lambda copy: copy.start())
        put_down_lower(down, small)
        for_copies(copies, lambda copy: copy.wait())

    part = nn(act[0], down[...])
    zd = part[:, width : width + RANK].astype(BF16)
    zd_o[0] = zd
    part = (part[:, :width] + ADAPTER_SCALING * nn(zd, upper[0])).astype(BF16)

    @pl.when(step == 0)
    def _():
        part_own[...] = part

    @pl.when(step == 1)
    def _():
        part_oth[...] = part


def ffn_grads_kernel(at, own, far, own_oth, far_oth, cot, cot_far, cot_oth, cot_far_oth, *rest):
    act, grads, narrow, narrow_back, zd, small, wide_o, quarter_o, lanes, wide, quarter = rest
    step = pl.program_id(0)
    units = small.shape[2]

    @pl.when(step == 0)
    def _():
        wide[...] = jnp.zeros_like(wide)
        quarter[...] = jnp.zeros_like(quarter)
        lanes[...] = jnp.zeros_like(lanes)
        for i in range(2):
            table = jnp.transpose(small[i].astype(F32))
            zero = jnp.zeros_like(table)
            table = jnp.concatenate([table, zero] if i == 0 else [zero, table], axis=1)
            lanes[i * units : (i + 1) * units, : 2 * RANK] = table.astype(BF16)

    value = both_tokens(step, own, far, own_oth, far_oth)
    grad = both_tokens(step, cot.at[0], cot_far.at[0], cot_oth, cot_far_oth)
    inner = (ADAPTER_SCALING * nn(grads[0], lanes[...])).astype(BF16)[:, : 2 * RANK]
    wide[:RANK] += ADAPTER_SCALING * tn(zd[0], grad)
    wide[RANK:] += tn(inner, value)
    both = tn(narrow[0], grads[0])
    quarter[:RANK] += ADAPTER_SCALING * both[:RANK, :units]
    quarter[RANK : 2 * RANK] += ADAPTER_SCALING * both[RANK:, units:]
    quarter[2 * RANK :] += tn(narrow_back[0], act[0])

    @pl.when(step == 1)
    def _():
        wide_o[...] = wide[...].astype(BF16)
        quarter_o[...] = quarter[...].astype(BF16)


def assemble_kernel(at, own, *rest):
    z = at[4]
    up, down, out = rest[:3], rest[3:6], rest[6]
    place = pl.program_id(0)

    @pl.when(place == z)
    def _():
        out[0] = own[...].astype(out.dtype)

    for d in range(3):

        @pl.when(z - place == d + 1)
        def _():
            out[0] = up[d][...].astype(out.dtype)

        @pl.when(place - z == d + 1)
        def _():
            out[0] = down[d][...].astype(out.dtype)


def plus(here, there):
    return (here.astype(F32) + there.astype(F32)).astype(BF16)


def tie(*values):
    return lax.optimization_barrier(values)


def tie_all(values):
    return lax.optimization_barrier(values)


def heads_tokens(value):
    return lax.all_to_all(value, CT, 0, 0, axis_index_groups=COLUMN, tiled=True)


UP = [(i, i + 1) for i in range(3)]
DOWN = [(i + 1, i) for i in range(3)]


def body(
    shards,
    inputs,
    cotangent,
    segments,
    adapter_index,
    query_weight,
    key_value_weight,
    output_weight,
    gate_up_weight,
    down_weight,
    norm_attn,
    norm_ffn,
    q_gain,
    k_gain,
    input_adapter_lower,
    query_adapter_upper,
    key_value_adapter_upper,
    gate_up_adapter_upper,
    output_adapter_lower,
    output_adapter_upper,
    down_adapter_lower,
    down_adapter_upper,
):
    ctx = lax.axis_index("ctx")
    x, k = ctx // 2, ctx % 2
    z = lax.axis_index("tp")
    y = lax.axis_index("shard")
    tok = inputs.shape[1]
    half = 2 * tok
    sub = tok // 4
    width = inputs.shape[2]
    hidden_units = gate_up_weight.shape[2]
    slot = adapter_index[0]
    segment = segments[0]
    pair = shards == 2
    swap_y = [(0, 1), (1, 0)]
    cols = 2 * HD
    at = jnp.stack([k, x, y, slot, z]).astype(jnp.int32)
    K, X, Y, SLOT, Z = range(5)

    def shard_rows(piece, axis):
        if pair:
            return order2(piece, lax.ppermute(piece, "shard", swap_y), y, axis)
        return lax.all_gather(piece, "shard", axis=axis, tiled=True)

    def over_y(cores):
        return [
            ((s * 4 + c) * 4 + t, ((s ^ 1) * 4 + c) * 4 + t)
            for s in range(2)
            for c in cores
            for t in range(4)
        ]

    tokens_other = lax.ppermute(inputs[0], "ctx", CORE)
    by_slot = lambda i, s: (s[SLOT], 0, 0)
    prepared = run(
        prepare_kernel,
        "prepare",
        (1,),
        at,
        [
            (query_weight, (query_weight.shape[0], cols), lambda i, s: (0, s[K])),
            whole(key_value_weight),
            (output_weight, (cols, output_weight.shape[1]), lambda i, s: (s[K], 0)),
            (gate_up_adapter_upper, (1, 2, RANK, hidden_units), lambda i, s: (s[SLOT], 0, 0, 0)),
            (jnp.swapaxes(down_adapter_lower, 1, 2), (1, RANK, hidden_units), by_slot),
            (query_adapter_upper, (1, RANK, cols), lambda i, s: (s[SLOT], 0, s[K])),
            (key_value_adapter_upper, (1, 2, RANK, cols), lambda i, s: (s[SLOT], 0, 0, 0)),
            (
                jnp.swapaxes(output_adapter_lower, 1, 2),
                (1, RANK, cols),
                lambda i, s: (s[SLOT], 0, s[K]),
            ),
        ],
        [
            out_whole((3 * cols, query_weight.shape[0]), BF16),
            out_whole((3, RANK, hidden_units), BF16),
            out_whole((2 * cols, cols), BF16),
            out_whole((cols, cols), BF16),
        ],
    )
    piece_rows, small_ffn, upper_qkv, low_rows = prepared
    dense_rows = shard_rows(piece_rows, 1)
    dense_qkv, rows_here = dense_rows[: 2 * cols], dense_rows[2 * cols :]

    far_z = [(c * 4 + t, c * 4 + (t ^ 2)) for c in (1, 3) for t in range(4)]
    far_x = [(1, 3), (3, 1)]
    if pair:
        (piece,) = run(
            pieces_kernel,
            "pieces",
            (1,),
            at,
            [
                (gate_up_weight, (1,) + gate_up_weight.shape[1:], lambda i, s: (s[X], 0, 0)),
                (down_weight, (hidden_units // 2, down_weight.shape[1]), lambda i, s: (s[X], 0)),
            ],
            [
                out_whole(
                    (
                        gate_up_weight.shape[1] + down_weight.shape[1] // 2,
                        hidden_units,
                    ),
                    BF16,
                )
            ],
        )
        piece = lax.ppermute(piece, CT, far_z)

    block = tok // 4
    blocks = half // block
    half_dim = HD // 2
    first_query = x * half
    inverse = THETA ** (-(jnp.arange(half_dim, dtype=F32) * 2.0 / HD))
    inverse = jnp.concatenate([inverse] * 3 + [jnp.zeros_like(inverse)])
    places = jnp.arange(2 * block + blocks, dtype=jnp.int32)
    places = jnp.where(places < 2 * block, places, first_query + block * (places - 2 * block))
    angles = places.astype(F32)[:, None] * inverse[None, :]
    turns = jnp.stack([jnp.cos(angles), jnp.sin(angles)])

    by_row = lambda i, s: (i, 0)
    by_step = lambda i, s: (i, 0, 0)
    lower_table = jnp.swapaxes(input_adapter_lower, 1, 2)
    lower_spec = (lower_table, (1, 5 * RANK, width), by_slot)
    ones = jnp.ones((half_dim,), F32)
    gains = jnp.stack(
        [
            jnp.concatenate([q_gain[part], q_gain[part], k_gain[part], ones])
            for part in (slice(0, half_dim), slice(half_dim, HD))
        ]
    )
    gain_attn, gain_ffn = norm_attn[None], norm_ffn[None]
    own_row = lambda i, s: (jnp.minimum(i, 3), 0)
    oth_row = lambda i, s: (jnp.maximum(i - 4, 0), 0)
    chip_row = lambda i, s: (jnp.where(i < 4, s[K] * 4 + i, (1 - s[K]) * 4 + i - 4), 0)
    normalized, narrow, queries, keyvals, raw = run(
        project_kernel,
        "project",
        (8,),
        at,
        [
            (inputs[0], (block, width), own_row),
            (tokens_other, (block, width), oth_row),
            whole(gain_attn),
            (dense_rows, (2 * cols, width), fixed(0, 0)),
            (lower_table, (1, 3 * RANK, width), by_slot),
            whole(upper_qkv),
            whole(turns),
            whole(gains),
        ],
        [
            ((half, width), BF16, (block, width), chip_row),
            ((half, 3 * RANK), BF16, (block, 3 * RANK), chip_row),
            ((half, cols), BF16, (block, cols), chip_row),
            ((half, cols), BF16, (block, cols), chip_row),
            ((half, 2 * cols), F32, (block, 2 * cols), chip_row),
        ],
        [pltpu.VMEM((3 * cols, width), BF16)],
    )
    keyvals_before = lax.ppermute(keyvals, "ctx", [(0, 2), (1, 3)])

    size = half // 4
    seg_rows = segment.reshape(-1, 1, size)
    keyvals, small_from = tie(keyvals, small_ffn)
    small_far = lax.ppermute(small_from, "tp", Z_XOR[2])
    if pair:
        keyvals, gate_up_from = tie(keyvals, gate_up_weight)
        mine_g = lax.ppermute(gate_up_from, SCT, over_y((0, 2)))
    acc = attention_forward(queries, keyvals, seg_rows, segment, at, 0, size, size)
    acc, cot_here, out_rows = tie(acc, cotangent[0], jnp.concatenate([rows_here, low_rows], axis=1))
    out_own = lax.all_gather(out_rows, "tp", axis=0, tiled=True)
    cot_oth = lax.ppermute(cot_here, "ctx", CORE)
    mixed, mixed_low, lse = attention_forward(
        queries, keyvals_before, seg_rows, segment, at, half, size, 2 * size, acc
    )
    mixed_low, small_far = tie(mixed_low, small_far)
    small_ffn = jnp.where(k == 0, small_ffn, small_far)
    if pair:
        mixed_low, piece, down_from = tie(mixed_low, piece, down_weight)
        piece_x = lax.ppermute(piece, "ctx", far_x)
        piece_y = lax.ppermute(piece, SCT, over_y((1, 3)))
        mine_d = lax.ppermute(down_from, SCT, over_y((0, 2)))

    mixed_all = heads_tokens(mixed_low.reshape(8, sub, cols))
    qkv_rows = rows_at(jnp.concatenate([dense_qkv, upper_qkv], axis=1), x, cols)
    mixed_all, small_ffn, cot_oth, qkv_rows = tie(mixed_all, small_ffn, cot_oth, qkv_rows)
    out_oth = lax.ppermute(out_own, "ctx", CORE)
    if pair:
        mixed_all, mine_g, piece_x, piece_y, out_own = tie(
            mixed_all, mine_g, piece_x, piece_y, out_own
        )
        piece_xy = lax.ppermute(piece_y, "ctx", far_x)
        pieces = [piece, piece_x, piece_y, piece_xy]
        sources = [gate_up_weight, mine_g] + pieces
        down_sources = [down_weight, mine_d] + pieces
    else:
        full_g = lax.all_gather(gate_up_weight, "shard", axis=1, tiled=True)
        full_d = lax.all_gather(down_weight, "shard", axis=1, tiled=True)
        sources = [jnp.where(k == 0, full_g, lax.ppermute(full_g, "tp", Z_XOR[2]))]
        down_sources = [jnp.where(k == 0, full_d, lax.ppermute(full_d, "tp", Z_XOR[2]))]
    z_block = lambda i, s: (0, s[Z], 0)
    upper_out_spec = (output_adapter_upper, (1, RANK, width), lambda i, s: (s[SLOT], 0, 0))
    hidden_state, normalized_second, narrow_out = run(
        mix_kernel,
        "mix",
        (1,),
        at,
        [
            whole(mixed_all),
            whole(out_own),
            whole(out_oth),
            upper_out_spec,
            (inputs, (1, sub, width), z_block),
            whole(gain_ffn),
        ],
        [
            out_whole((sub, width), F32),
            out_whole((sub, width), BF16),
            out_whole((sub, RANK), BF16),
        ],
    )

    second = normalized_second
    second_oth = lax.ppermute(second, "ctx", CORE)
    second_far = lax.ppermute(second, "tp", Z_XOR[1])
    second_far_oth = lax.ppermute(second_far, "ctx", CORE)
    upper_down_spec = (down_adapter_upper, (1, RANK, width), by_slot)
    z_far = lambda i, s: (0, s[Z] ^ 1, 0)
    ffn_tokens = [
        whole(second),
        whole(second_far),
        whole(second_oth),
        whole(second_far_oth),
        (cotangent, (1, sub, width), z_block),
        (cotangent, (1, sub, width), z_far),
        (cot_oth, (sub, width), lambda i, s: (s[Z], 0)),
        (cot_oth, (sub, width), lambda i, s: (s[Z] ^ 1, 0)),
    ]
    tall = 2 * sub
    qkv_rows, second_far_oth = tie(qkv_rows, second_far_oth)
    qkv_own = lax.all_gather(qkv_rows, "tp", axis=0, tiled=True)
    ffn_tokens[3] = whole(second_far_oth)
    part_own, part_oth, active, grad_both, narrow_second, narrow_back_second = run(
        functools.partial(ffn_kernel, len(sources)),
        "ffn",
        (2,),
        at,
        ffn_tokens
        + [lower_spec, whole(small_ffn), upper_down_spec]
        + [(source, None, None) for source in sources + down_sources],
        [
            out_whole((tall, width), BF16),
            out_whole((tall, width), BF16),
            ((2, tall, hidden_units), BF16, (1, tall, hidden_units), by_step),
            ((2, tall, 2 * hidden_units), BF16, (1, tall, 2 * hidden_units), by_step),
            ((2, tall, 2 * RANK), BF16, (1, tall, 2 * RANK), by_step),
            ((2, tall, RANK), BF16, (1, tall, RANK), by_step),
        ],
        [
            pltpu.VMEM((width, 2 * hidden_units), BF16),
            pltpu.VMEM((hidden_units, width + cols), BF16),
            pltpu.VMEM((2, width, cols), BF16),
            pltpu.SemaphoreType.DMA((2, 24)),
        ],
        LONG,
    )
    part_arrived = lax.ppermute(part_oth, "ctx", CORE)
    part_give = (part_own[sub:].astype(F32) + part_arrived[sub:].astype(F32)).astype(BF16)
    part_give, active, qkv_own = tie(part_give, active, qkv_own)
    part_far = lax.ppermute(part_give, "tp", Z_XOR[1])
    qkv_own_x = lax.ppermute(qkv_own, "ctx", XSIDE)

    down_own, down_oth, zd = run(
        functools.partial(ffn_down_kernel, len(sources)),
        "ffn_down",
        (2,),
        at,
        [
            (active, (1, tall, hidden_units), by_step),
            whole(small_ffn),
            upper_down_spec,
        ]
        + [(source, None, None) for source in down_sources],
        [
            out_whole((tall, width), BF16),
            out_whole((tall, width), BF16),
            ((2, tall, RANK), BF16, (1, tall, RANK), by_step),
        ],
        [pltpu.VMEM((hidden_units, width + cols), BF16), pltpu.SemaphoreType.DMA((1, 24))],
        LONG,
    )
    hidden_back, down_own, down_oth, zd = tie(hidden_state, down_own, down_oth, zd)

    grad_hidden, grad_hidden_low, grad_mixed_all, narrow_back = run(
        mix_back_kernel,
        "mix_back",
        (1,),
        at,
        [
            whole(hidden_back),
            (cotangent, (1, sub, width), z_block),
            whole(part_own),
            whole(part_arrived),
            whole(part_far),
            whole(gain_ffn),
            whole(out_own),
            whole(out_oth),
            upper_out_spec,
        ],
        [
            out_whole((sub, width), F32),
            out_whole((sub, width), BF16),
            out_whole((8, sub, cols), BF16),
            out_whole((sub, RANK), BF16),
        ],
    )
    grad_mixed_all, grad_both, down_oth = tie(grad_mixed_all, grad_both, down_oth)
    grad_mixed = heads_tokens(grad_mixed_all).reshape(half, cols)
    down_arrived = lax.ppermute(down_oth, "ctx", CORE)
    down_give = (down_own[sub:].astype(F32) + down_arrived[sub:].astype(F32)).astype(BF16)
    down_far = lax.ppermute(down_give, "tp", Z_XOR[1])
    final = hidden_state + (
        down_own[:sub].astype(F32) + down_arrived[:sub].astype(F32) + down_far.astype(F32)
    )
    final = final.astype(BF16)
    wide_ffn, quarter_grads = run(
        ffn_grads_kernel,
        "ffn_grads",
        (2,),
        at,
        ffn_tokens
        + [
            (active, (1, tall, hidden_units), by_step),
            (grad_both, (1, tall, 2 * hidden_units), by_step),
            (narrow_second, (1, tall, 2 * RANK), by_step),
            (narrow_back_second, (1, tall, RANK), by_step),
            (zd, (1, tall, RANK), by_step),
            whole(small_ffn),
        ],
        [out_whole((3 * RANK, width), BF16), out_whole((3 * RANK, hidden_units), BF16)],
        [
            pltpu.VMEM((2 * hidden_units, cols), BF16),
            pltpu.VMEM((3 * RANK, width), F32),
            pltpu.VMEM((3 * RANK, hidden_units), F32),
        ],
        LONG,
    )
    (wide_mix,) = run(
        mix_grads_kernel,
        "mix_grads",
        (1,),
        at,
        [whole(mixed_all), whole(grad_hidden_low), whole(narrow_out), whole(narrow_back)],
        [out_whole((2 * RANK, width), BF16)],
    )
    wide_early = jnp.concatenate([wide_mix, wide_ffn], axis=0)
    grad_mixed, wide_early, qkv_own_x = tie(grad_mixed, wide_early, qkv_own_x)
    wide_near = lax.ppermute(wide_early, "tp", Z_XOR[1])
    if pair:
        slot_other = lax.ppermute(adapter_index, "shard", swap_y)[0]

    dq_before, dkv_before = attention_backward(
        queries,
        keyvals_before,
        seg_rows,
        grad_mixed,
        mixed,
        lse,
        segment,
        at,
        half,
        size,
        size,
    )
    dkv_after = lax.ppermute(dkv_before, "ctx", [(2, 0), (3, 1)])
    dq_before, wide_near, quarter_grads, qkv_own, qkv_own_x, final = tie(
        dq_before, wide_near, quarter_grads, qkv_own, qkv_own_x, final
    )
    out_up_1 = lax.ppermute(final, "tp", UP)
    out_down_1 = lax.ppermute(final, "tp", DOWN)
    if pair:
        dq_before, slot_other = tie(dq_before, slot_other)
    qkv_oth = lax.ppermute(qkv_own, "ctx", CORE)
    qkv_oth_x = lax.ppermute(qkv_own_x, "ctx", CORE)
    wide_early = plus(wide_early, wide_near)
    early = jnp.concatenate(
        [jnp.pad(wide_early, ((0, 0), (0, hidden_units - width))), quarter_grads], axis=0
    )
    early_far = lax.ppermute(early, "tp", Z_XOR[2])
    dq, dkv = attention_backward(
        queries,
        keyvals,
        seg_rows,
        grad_mixed,
        mixed,
        lse,
        segment,
        at,
        0,
        size,
        size,
        dq_before,
    )
    dq, early_far, out_up_1, out_down_1 = tie(dq, early_far, out_up_1, out_down_1)
    out_up_2 = lax.ppermute(out_up_1, "tp", UP)
    out_down_2 = lax.ppermute(out_down_1, "tp", DOWN)
    early = jnp.concatenate(
        [
            plus(early[: 5 * RANK], early_far[: 5 * RANK]),
            jnp.where(k == 0, early[5 * RANK :], early_far[5 * RANK :]),
        ],
        axis=0,
    )
    tall_blocks = blocks // 2
    d_projected, wide_attn, head_grads = run(
        project_back_kernel,
        "project_back",
        (tall_blocks,),
        at,
        [
            (dq, (2 * block, cols), by_row),
            (dkv, (2 * block, cols), by_row),
            (dkv_after, (2 * block, cols), by_row),
            (raw, (2 * block, 2 * cols), by_row),
            whole(turns),
            whole(gains),
            (narrow, (2 * block, 3 * RANK), by_row),
            (normalized, (2 * block, width), by_row),
            whole(upper_qkv),
        ],
        [
            ((half, 2 * cols), BF16, (2 * block, 2 * cols), by_row),
            out_whole((3 * RANK, width), BF16),
            out_whole((RANK, 4 * cols), BF16),
        ],
        [pltpu.VMEM((3 * RANK, width), F32), pltpu.VMEM((3 * RANK, 2 * cols), F32)],
        LONG,
    )
    d_projected, out_up_2, out_down_2 = tie(d_projected, out_up_2, out_down_2)
    out_up_3 = lax.ppermute(out_up_2, "tp", UP)
    out_down_3 = lax.ppermute(out_down_2, "tp", DOWN)

    d_all = heads_tokens(d_projected.reshape(8, sub, 2 * cols))
    def lanes_to(value, size):
        return jnp.pad(value, ((0, 0), (0, size - value.shape[1])))

    packed = jnp.concatenate(
        [early, lanes_to(wide_attn, hidden_units), lanes_to(head_grads, hidden_units)], axis=0
    )

    packed = plus(packed, lax.ppermute(packed, "ctx", CORE))
    packed = plus(packed, lax.ppermute(packed, "ctx", XSIDE))
    slots = jnp.arange(ADAPT, dtype=jnp.int32)

    def placed(value, which):
        mask = (slots == which).astype(F32).reshape((ADAPT,) + (1,) * value.ndim)
        return mask * value.astype(F32)[None]

    if pair:
        both = jnp.stack([packed, lax.ppermute(packed, "shard", swap_y)])
    else:
        both = lax.psum(placed(packed, slot), "shard")
    (grad_tokens,) = run(
        last_kernel,
        "last",
        (1,),
        at,
        [
            whole(d_all),
            whole(qkv_own),
            whole(qkv_own_x),
            whole(qkv_oth),
            whole(qkv_oth_x),
            (lower_table, (1, 3 * RANK, width), by_slot),
            whole(grad_hidden),
            (inputs, (1, sub, width), z_block),
            whole(gain_attn),
        ],
        [out_whole((sub, width), BF16)],
    )
    up_1 = lax.ppermute(grad_tokens, "tp", UP)
    down_1 = lax.ppermute(grad_tokens, "tp", DOWN)
    own_width = width // (shards * 4)
    in_attn = rows_at(both[:, 8 * RANK : 11 * RANK, :width], y * 4 + ctx, own_width, 2)
    in_attn = plus(in_attn, lax.ppermute(in_attn, "tp", Z_XOR[1]))
    up_1, down_1, in_attn, both = tie(up_1, down_1, in_attn, both)
    up_2 = lax.ppermute(up_1, "tp", UP)
    down_2 = lax.ppermute(down_1, "tp", DOWN)
    in_far = lax.ppermute(in_attn, "tp", Z_XOR[2])
    wide = both[:, : 5 * RANK, :width]
    in_ffn = rows_at(wide[:, 3 * RANK :], y * 4 + ctx, own_width, 2)
    rest = jnp.concatenate([both[:, 5 * RANK : 8 * RANK], both[:, 11 * RANK :]], axis=1)
    if pair:
        slots_here = (slot, slot_other)
        rest = sum(placed(rest[i], which) for i, which in enumerate(slots_here))
    quarter_sum, heads = rest[:, : 3 * RANK], rest[:, 3 * RANK :, : 4 * cols]
    grad_b_query = jnp.concatenate([heads[..., :cols], heads[..., 2 * cols : 3 * cols]], axis=-1)
    grad_b_keyval = jnp.stack(
        [
            jnp.concatenate(
                [heads[..., core * 2 * cols + c * HD :][..., :HD] for core in range(2)], axis=-1
            )
            for c in (2, 3)
        ],
        axis=1,
    )
    grad_b_gate_up = quarter_sum[:, : 2 * RANK].reshape(ADAPT, 2, RANK, -1)
    grad_a_down = jnp.swapaxes(quarter_sum[:, 2 * RANK :], 1, 2)
    in_all = jnp.concatenate([plus(in_attn, in_far), in_ffn], axis=1)
    if pair:
        wide = sum(placed(wide[i, : 3 * RANK], which) for i, which in enumerate(slots_here))
        in_all = sum(placed(in_all[i], which) for i, which in enumerate(slots_here))
    else:
        wide, in_all = wide.astype(F32), in_all.astype(F32)
    grad_b_out = wide[:, :RANK]
    grad_a_out = wide[:, RANK : 2 * RANK]
    grad_b_down = wide[:, 2 * RANK : 3 * RANK]
    grad_a_out = jnp.concatenate(
        [rows_at(grad_a_out, z, cols, 2), rows_at(grad_a_out, 4 + z, cols, 2)], axis=2
    )
    grad_a_out = jnp.swapaxes(grad_a_out, 1, 2)
    grad_adapt_in = jnp.swapaxes(in_all, 1, 2)
    up_2, down_2, final, grad_b_query, grad_b_keyval, grad_b_gate_up, grad_a_down = tie(
        up_2, down_2, final, grad_b_query, grad_b_keyval, grad_b_gate_up, grad_a_down
    )
    up_3 = lax.ppermute(up_2, "tp", UP)
    down_3 = lax.ppermute(down_2, "tp", DOWN)
    line = [grad_tokens, up_1, up_2, up_3, down_1, down_2, down_3]
    z_row = lambda i, s: (0, i, 0)
    (grad_inputs,) = run(
        assemble_kernel,
        "assemble",
        (4,),
        at,
        [whole(part) for part in line],
        [((1, tok, width), F32, (1, sub, width), z_row)],
    )
    line = [final, out_up_1, out_up_2, out_up_3, out_down_1, out_down_2, out_down_3]
    (result,) = run(
        assemble_kernel,
        "assemble_out",
        (4,),
        at,
        [whole(part) for part in line],
        [((1, tok, width), BF16, (1, sub, width), z_row)],
        cost=LONG,
    )
    return (
        result,
        grad_inputs,
        grad_adapt_in,
        grad_b_query,
        grad_b_keyval,
        grad_b_gate_up,
        grad_a_out,
        grad_b_out,
        grad_a_down,
        grad_b_down,
    )


def solution(mesh):
    return jax.shard_map(
        functools.partial(body, mesh.shape["shard"]),
        mesh=mesh,
        in_specs=(
            P("shard", "ctx", None),
            P("shard", "ctx", None),
            P("shard", None),
            P("shard"),
            P("shard", "tp"),
            P(None, "shard", "tp"),
            P("tp", "shard"),
            P(None, "shard", "tp"),
            P("tp", "shard"),
            P(),
            P(),
            P(),
            P(),
            P(),
            P(None, None, "tp"),
            P(None, None, None, "tp"),
            P(None, None, None, "tp"),
            P(None, "tp", None),
            P(),
            P(None, "tp", None),
            P(),
        ),
        out_specs=(
            P("shard", "ctx", None),
            P("shard", "ctx", None),
            P(None, ("shard", "ctx"), None),
            P(None, None, "tp"),
            P(None, None, None, "tp"),
            P(None, None, None, "tp"),
            P(None, "tp", None),
            P(),
            P(None, "tp", None),
            P(),
        ),
        check_vma=False,
    )
```

```python
import functools

import jax
import jax.numpy as jnp
from jax import lax
from jax.experimental import pallas as pl
from jax.experimental.pallas import tpu as pltpu
from jax.sharding import PartitionSpec as P

HD = 64
RANK = 16
ADAPT = 8
EPS = 1e-05
ADAPTER_SCALING = 2.0
THETA = 1000000.0
LOG2E = 1.4426950408889634
SCALE = HD**-0.5
F32 = jnp.float32
BF16 = jnp.bfloat16
VMEM_LIMIT = 62 * 1024 * 1024

CORE = [(i, i ^ 1) for i in range(4)]
XSIDE = [(i, i ^ 2) for i in range(4)]
Z_XOR = {d: [(i, i ^ d) for i in range(4)] for d in (1, 2, 3)}
CT = ("ctx", "tp")
SCT = ("shard", "ctx", "tp")
COLUMN = [[(2 * x + k) * 4 + z for k in range(2) for z in range(4)] for x in range(2)]

COST = pl.CostEstimate(flops=1 << 20, bytes_accessed=1 << 16, transcendentals=0)
LONG = pl.CostEstimate(flops=30 << 30, bytes_accessed=16 << 20, transcendentals=0)
HIGHEST = lax.Precision.HIGHEST


def nn(left, right):
    return lax.dot_general(left, right, (((1,), (0,)), ((), ())), preferred_element_type=F32)


def nt(left, right):
    return lax.dot_general(left, right, (((1,), (1,)), ((), ())), preferred_element_type=F32)


def tn(left, right):
    return lax.dot_general(left, right, (((0,), (0,)), ((), ())), preferred_element_type=F32)


def rmsnorm(value, gain):
    return value * lax.rsqrt(jnp.mean(value * value, axis=-1, keepdims=True) + EPS) * gain


def order2(own, other, bit, axis=0):
    return jnp.concatenate(
        [jnp.where(bit == 0, own, other), jnp.where(bit == 0, other, own)], axis=axis
    )


def rows_at(value, block, size, axis=0):
    return lax.dynamic_slice_in_dim(value, block * size, size, axis)


def key_loops(segment, first, key_base, bq, bk, keys, step, acc):
    blocks = keys // bk
    low = jnp.minimum(jnp.maximum(segment[first] - key_base, 0) // bk, blocks)
    high = jnp.clip((first + bq - key_base + bk - 1) // bk, 0, blocks)
    low = jnp.minimum(low, high)
    free_low = (jnp.maximum(segment[first + bq - 1] - key_base, 0) + bk - 1) // bk
    free_low = jnp.clip(free_low, low, high)
    free_high = jnp.clip(jnp.maximum(first + 1 - key_base, 0) // bk, free_low, high)
    ahead = free_low - low

    def masked(t, carry):
        j = jnp.where(t < ahead, low + t, free_high + t - ahead)
        return step(j, carry, True)

    acc = lax.fori_loop(0, ahead + high - free_high, masked, acc)
    return lax.fori_loop(free_low, free_high, lambda j, carry: step(j, carry, False), acc)


def row_sums(weights, value):
    return lax.dot_general(
        weights, value, (((1,), (1,)), ((), ())), precision=HIGHEST, preferred_element_type=F32
    )


def fwd_kernel(bq, bk, back, last, segment, at, q_ref, kv_ref, seg_ref, *rest):
    if last:
        acc_in, mixed_ref, low_ref, lse_ref, vx = rest
    else:
        acc_ref, vx = rest
    i = pl.program_id(0)
    keys = kv_ref.shape[0]

    @pl.when(i == 0)
    def _():
        col = lax.broadcasted_iota(jnp.int32, (keys, 2 * HD), 1)
        kv = kv_ref[...]
        swapped = jnp.concatenate([kv[:, HD:], kv[:, :HD]], axis=1)
        ones = jnp.where(col == HD, 1.0, 0.0).astype(BF16)
        vx[...] = jnp.where(col < HD, swapped, ones)

    q = q_ref[...]
    both = jnp.concatenate([q[:, :HD], q[:, HD:]], axis=0)
    q_base = at[1] * (bq * pl.num_programs(0))
    k_base = q_base - back
    seg_col = jnp.broadcast_to(seg_ref[0].astype(F32), (8, bq))
    seg_col = jnp.transpose(seg_col)[:, :1].astype(jnp.int32)

    def step(j, acc, masked):
        off = pl.multiple_of(j * bk, bk)
        scores = nt(both, kv_ref[pl.ds(off, bk), :HD])
        probs = jnp.exp2(scores * (SCALE * LOG2E))
        if masked:
            qi = q_base + i * bq + lax.broadcasted_iota(jnp.int32, (bq, bk), 0)
            ki = k_base + off + lax.broadcasted_iota(jnp.int32, (bq, bk), 1)
            allowed = (ki <= qi) & (ki >= seg_col)
            probs = jnp.where(jnp.concatenate([allowed, allowed], axis=0), probs, 0.0)
        return acc + nn(probs.astype(BF16), vx[pl.ds(off, bk), :])

    if last:
        acc = jnp.concatenate([acc_in[0], acc_in[1]], axis=0)
    else:
        acc = jnp.zeros((2 * bq, 2 * HD), F32)
    acc = key_loops(segment, q_base + i * bq, k_base, bq, bk, keys, step, acc)
    if last:
        total = acc[:, HD : HD + 1]
        out = acc[:, :HD] / total
        out = jnp.concatenate([out[:bq], out[bq:]], axis=1)
        mixed_ref[...] = out
        low_ref[...] = out.astype(BF16)
        pick = jnp.where(lax.broadcasted_iota(jnp.int32, (8, 2 * HD), 1) == HD, 1.0, 0.0)
        lse_ref[0] = jnp.log2(row_sums(pick, acc)[:1])
    else:
        acc_ref[0] = acc[:bq]
        acc_ref[1] = acc[bq:]


def attention_forward(q, kv, seg, segment, at, back, bq, bk, acc_in=None):
    rows, keys = q.shape[0], kv.shape[0]
    last = acc_in is not None
    row = lambda i, *_: (i, 0)
    everything = lambda i, *_: (0, 0)
    heads = lambda i, *_: (0, i, 0)
    in_specs = [
        pl.BlockSpec((bq, 2 * HD), row),
        pl.BlockSpec((keys, 2 * HD), everything),
        pl.BlockSpec((1, 1, bq), lambda i, g, a: (a[1] * (rows // bq) + i, 0, 0)),
    ]
    args = [q, kv, seg]
    if last:
        in_specs.append(pl.BlockSpec((2, bq, 2 * HD), heads))
        args.append(acc_in)
        out_specs = [
            pl.BlockSpec((bq, 2 * HD), row),
            pl.BlockSpec((bq, 2 * HD), row),
            pl.BlockSpec((1, 1, 2 * bq), lambda i, *_: (i, 0, 0)),
        ]
        out_shape = [
            jax.ShapeDtypeStruct((rows, 2 * HD), F32),
            jax.ShapeDtypeStruct((rows, 2 * HD), BF16),
            jax.ShapeDtypeStruct((rows // bq, 1, 2 * bq), F32),
        ]
    else:
        out_specs = pl.BlockSpec((2, bq, 2 * HD), heads)
        out_shape = jax.ShapeDtypeStruct((2, rows, 2 * HD), F32)
    return pl.pallas_call(
        functools.partial(fwd_kernel, bq, bk, back, last),
        grid_spec=pltpu.PrefetchScalarGridSpec(
            num_scalar_prefetch=2,
            grid=(rows // bq,),
            in_specs=in_specs,
            out_specs=out_specs,
            scratch_shapes=[pltpu.VMEM((keys, 2 * HD), BF16)],
        ),
        out_shape=out_shape,
        compiler_params=pltpu.CompilerParams(vmem_limit_bytes=VMEM_LIMIT),
        cost_estimate=LONG,
        name="attn_fwd_last" if last else "attn_fwd_first",
    )(segment, at, *args)


def bwd_kernel(
    bq, bk, back, first, segment, at, q_ref, kv_ref, seg_ref, do_ref, out_ref, lse_ref, *rest
):
    if first:
        dq_ref, dkv_ref, dk, dv = rest
    else:
        dq_in, dq_ref, dkv_ref, dk, dv = rest
    i = pl.program_id(0)

    @pl.when(i == 0)
    def _():
        dk[...] = jnp.zeros_like(dk)
        dv[...] = jnp.zeros_like(dv)

    q = q_ref[...]
    do = do_ref[...]
    both = jnp.concatenate([q[:, :HD], q[:, HD:]], axis=0)
    both_do = jnp.concatenate([do[:, :HD], do[:, HD:]], axis=0)
    lse = lse_ref[0]
    lane = lax.broadcasted_iota(jnp.int32, (8, 2 * HD), 1)
    row = lax.broadcasted_iota(jnp.int32, (8, 2 * HD), 0)
    pick = jnp.where(lane // HD == row, 1.0, 0.0)
    deltas = row_sums(pick, do.astype(F32) * out_ref[...])
    delta = jnp.concatenate([deltas[:1], deltas[1:2]], axis=1)
    q_base = at[1] * (bq * pl.num_programs(0))
    k_base = q_base - back

    def step(j, acc, masked):
        off = pl.multiple_of(j * bk, bk)
        kv = kv_ref[pl.ds(off, bk), :]
        k, v = kv[:, :HD], kv[:, HD:]
        probs = jnp.exp2(nt(k, both) * (SCALE * LOG2E) - lse)
        if masked:
            ki = k_base + off + lax.broadcasted_iota(jnp.int32, (bk, bq), 0)
            qi = q_base + i * bq + lax.broadcasted_iota(jnp.int32, (bk, bq), 1)
            allowed = (ki <= qi) & (ki >= seg_ref[0])
            probs = jnp.where(jnp.concatenate([allowed, allowed], axis=1), probs, 0.0)
        dscores = (probs * (nt(v, both_do) - delta)).astype(BF16)
        dv[pl.ds(off, bk), :] += nn(probs.astype(BF16), both_do)
        dk[pl.ds(off, bk), :] += nn(dscores, both)
        return acc + tn(k, dscores)

    acc = key_loops(
        segment, q_base + i * bq, k_base, bq, bk, kv_ref.shape[0], step,
        jnp.zeros((HD, 2 * bq), F32),
    )
    acc = jnp.transpose(acc) * SCALE
    acc = jnp.concatenate([acc[:bq], acc[bq:]], axis=1)
    dq_ref[...] = acc if first else dq_in[...] + acc

    @pl.when(i == pl.num_programs(0) - 1)
    def _():
        dkv_ref[...] = jnp.concatenate([dk[...] * SCALE, dv[...]], axis=1).astype(dkv_ref.dtype)


def attention_backward(q, kv, seg, do, out, lse, segment, at, back, bq, bk, dq_in=None):
    rows, keys = q.shape[0], kv.shape[0]
    first = dq_in is None
    row = lambda i, *_: (i, 0)
    everything = lambda i, *_: (0, 0)
    flat = lambda i, *_: (i, 0, 0)
    in_specs = [
        pl.BlockSpec((bq, 2 * HD), row),
        pl.BlockSpec((keys, 2 * HD), everything),
        pl.BlockSpec((1, 1, bq), lambda i, g, a: (a[1] * (rows // bq) + i, 0, 0)),
        pl.BlockSpec((bq, 2 * HD), row),
        pl.BlockSpec((bq, 2 * HD), row),
        pl.BlockSpec((1, 1, 2 * bq), flat),
    ]
    args = [q, kv, seg, do, out, lse]
    if not first:
        in_specs.append(pl.BlockSpec((bq, 2 * HD), row))
        args.append(dq_in)
    return pl.pallas_call(
        functools.partial(bwd_kernel, bq, bk, back, first),
        grid_spec=pltpu.PrefetchScalarGridSpec(
            num_scalar_prefetch=2,
            grid=(rows // bq,),
            in_specs=in_specs,
            out_specs=[pl.BlockSpec((bq, 2 * HD), row), pl.BlockSpec((keys, 2 * HD), everything)],
            scratch_shapes=[pltpu.VMEM((keys, HD), F32), pltpu.VMEM((keys, HD), F32)],
        ),
        out_shape=[
            jax.ShapeDtypeStruct((rows, 2 * HD), F32),
            jax.ShapeDtypeStruct((keys, 2 * HD), BF16 if first else F32),
        ],
        compiler_params=pltpu.CompilerParams(vmem_limit_bytes=VMEM_LIMIT),
        cost_estimate=LONG,
        name="attn_bwd_first" if first else "attn_bwd_last",
    )(segment, at, *args)


def run(kernel, name, grid, scalars, inputs, outputs, scratch=(), cost=COST):
    return pl.pallas_call(
        kernel,
        grid_spec=pltpu.PrefetchScalarGridSpec(
            num_scalar_prefetch=1,
            grid=grid,
            in_specs=[
                pl.BlockSpec(memory_space=pl.ANY) if block is None else pl.BlockSpec(block, index)
                for _, block, index in inputs
            ],
            out_specs=[
                pl.BlockSpec(memory_space=pl.ANY) if block is None else pl.BlockSpec(block, index)
                for _, _, block, index in outputs
            ],
            scratch_shapes=list(scratch),
        ),
        out_shape=[jax.ShapeDtypeStruct(shape, kind) for shape, kind, _, _ in outputs],
        compiler_params=pltpu.CompilerParams(vmem_limit_bytes=VMEM_LIMIT),
        cost_estimate=cost,
        name=name,
    )(scalars, *[array for array, _, _ in inputs])


def fixed(*index):
    return lambda i, s: index


def whole(array):
    return (array, array.shape, fixed(*(0,) * array.ndim))


def out_whole(shape, kind):
    return (shape, kind, shape, fixed(*(0,) * len(shape)))


def place_matrix(back):
    at_row = lax.broadcasted_iota(jnp.int32, (4 * HD, 4 * HD), 0)
    at_col = lax.broadcasted_iota(jnp.int32, (4 * HD, 4 * HD), 1)
    if back:
        at_row, at_col = at_col, at_row
    part = HD // 2
    moved = at_row // part % 2 * (2 * HD) + at_row // HD * part + at_row % part
    return jnp.where(moved == at_col, 1.0, 0.0).astype(BF16)


def head_means(value):
    at_row = lax.broadcasted_iota(jnp.int32, (2 * HD, 2 * HD), 0) // (HD // 2)
    at_col = lax.broadcasted_iota(jnp.int32, (2 * HD, 2 * HD), 1) // (HD // 2)
    same = jnp.where(at_row == at_col, 1.0 / HD, 0.0).astype(BF16)
    high = value.astype(BF16)
    rest = (value - high.astype(F32)).astype(BF16)
    return nn(jnp.concatenate([high, rest], axis=1), jnp.concatenate([same, same], axis=0))


def rotation(step, turns, rows, blocks):
    first = turns.shape[1] - blocks
    cos_in, sin_in = turns[0, :rows], turns[1, :rows]
    cos_out, sin_out = turns[0, pl.ds(first + step, 1)], turns[1, pl.ds(first + step, 1)]
    return cos_in * cos_out - sin_in * sin_out, sin_in * cos_out + cos_in * sin_out


def head_root(first, second):
    lane = lax.broadcasted_iota(jnp.int32, first.shape, 1)
    root = lax.rsqrt(head_means(first * first + second * second) + EPS)
    return jnp.where(lane < 3 * (HD // 2), root, 1.0), lane


class Lanes:
    def __init__(self, start, size):
        self.start, self.size = start, size


def down_parts(shape, width):
    rows, cols = shape
    whole = width // cols
    tall = (rows * cols) // width
    parts = [(i * tall, (i + 1) * tall, Lanes(0, cols), 0, i * cols) for i in range(whole)]
    left = rows - whole * tall
    room = width - whole * cols
    for j in range(cols // room if left else 0):
        parts.append((whole * tall, rows, Lanes(j * room, room), j * left, whole * cols))
    return parts


def pieces_kernel(at, gate_up, down, out):
    height, width = gate_up.shape[1:]
    out[:height] = gate_up[0]
    value = down[...]
    for a, b, lanes, at_row, at_lane in down_parts(value.shape, width):
        out[height + at_row : height + at_row + b - a, at_lane : at_lane + lanes.size] = value[
            a:b, lanes.start : lanes.start + lanes.size
        ]


def prepare_kernel(
    at, q, kv, out_w, up_gate_up, lower_down, up_q, up_kv, lower_out,
    rows_o, small_o, upper_o, low_o,
):
    k = at[0]
    value = kv[...].astype(F32)
    value = jnp.where(k == 0, value[:, :, :HD], value[:, :, HD:]).astype(BF16)
    value = jnp.concatenate([q[...], value[0], value[1]], axis=1)
    height = 4 * HD
    rows_o[:height] = nt(place_matrix(True), value).astype(BF16)
    rows_o[height:] = out_w[...]
    small_o[:2] = up_gate_up[0]
    small_o[2] = lower_down[0]
    table = up_kv[0].astype(F32)
    table = jnp.where(k == 0, table[:, :, :HD], table[:, :, HD:]).astype(BF16)
    zero = jnp.zeros_like(table[0])
    wide = jnp.zeros((RANK, 2 * HD), BF16)
    rows = [
        jnp.concatenate([up_q[0], wide], axis=1),
        jnp.concatenate([wide, table[0], zero], axis=1),
        jnp.concatenate([wide, zero, table[1]], axis=1),
    ] + [jnp.concatenate([wide, wide], axis=1)] * 5
    upper_o[...] = nt(place_matrix(True), jnp.concatenate(rows, axis=0)).astype(BF16)
    table = jnp.transpose(lower_out[0].astype(F32))
    low_o[...] = jnp.concatenate(
        [table, jnp.zeros((table.shape[0], 2 * HD - RANK), F32)], axis=1
    ).astype(BF16)


def project_kernel(
    at, own, oth, gain, dense, lower, upper, turns, gains,
    normal_o, narrow_o, q_o, kv_o, raw_o, weights,
):
    width = 4 * HD
    step = pl.program_id(0)
    steps = pl.num_programs(0)

    @pl.when(step == 0)
    def _():
        weights[:width] = dense[...]
        weights[width : width + 3 * RANK] = lower[0]
        weights[width + 3 * RANK :] = jnp.zeros(
            (weights.shape[0] - width - 3 * RANK, weights.shape[1]), BF16
        )

    value = jnp.where(step < steps // 2, own[...].astype(F32), oth[...].astype(F32))
    root = lax.rsqrt(jnp.mean(value * value, axis=1, keepdims=True) + EPS)
    normal = (value * root * gain[...]).astype(BF16)
    normal_o[...] = normal
    raw = nt(normal, weights[...])
    narrow = raw[:, width:].astype(BF16)
    narrow_o[...] = narrow[:, : 3 * RANK]
    raw = raw[:, :width] + ADAPTER_SCALING * nt(narrow, upper[...])
    raw_o[...] = raw
    first, second = raw[:, : 2 * HD], raw[:, 2 * HD :]
    root, _ = head_root(first, second)
    place = jnp.where(step < steps // 2, at[0] * (steps // 2) + step, (1 - at[0]) * (steps // 2) + step - steps // 2)
    cos, sin = rotation(place, turns, normal.shape[0], steps)
    first = first * root * gains[0:1]
    second = second * root * gains[1:2]
    turned = jnp.concatenate([first * cos - second * sin, second * cos + first * sin], axis=1)
    out = nn(turned.astype(BF16), place_matrix(True)).astype(BF16)
    q_o[...] = out[:, : 2 * HD]
    kv_o[...] = out[:, 2 * HD :]


def project_back_kernel(
    at, dq, dkv, dkv_after, raw, turns, gains, narrow, normal, upper,
    out, wide_o, heads_o, wide, heads,
):
    step = pl.program_id(0)

    @pl.when(step == 0)
    def _():
        wide[...] = jnp.zeros_like(wide)
        heads[...] = jnp.zeros_like(heads)

    cos, sin = rotation(2 * step, turns, dq.shape[0], 2 * pl.num_programs(0))
    grad_kv = (dkv[...] + dkv_after[...].astype(F32)).astype(BF16)
    grad = nn(jnp.concatenate([dq[...].astype(BF16), grad_kv], axis=1), place_matrix(False))
    first, second = raw[:, : 2 * HD], raw[:, 2 * HD :]
    root, lane = head_root(first, second)
    first, second = first * root, second * root
    back_first = grad[:, : 2 * HD] * cos + grad[:, 2 * HD :] * sin
    back_second = grad[:, 2 * HD :] * cos - grad[:, : 2 * HD] * sin
    back_first = back_first * gains[0:1]
    back_second = back_second * gains[1:2]
    mean = head_means(back_first * first + back_second * second)
    mean = jnp.where(lane < 3 * (HD // 2), mean, 0.0)
    back_first = (root * (back_first - first * mean)).astype(BF16)
    back_second = (root * (back_second - second * mean)).astype(BF16)
    grad = jnp.concatenate([back_first, back_second], axis=1)
    out[...] = grad
    inside = (ADAPTER_SCALING * nn(grad, upper[...])).astype(BF16)
    wide[...] += tn(inside[:, : 3 * RANK], normal[...])
    heads[...] += tn(narrow[...], grad)

    @pl.when(step == pl.num_programs(0) - 1)
    def _():
        wide_o[...] = wide[...].astype(BF16)
        total = (heads[...] * ADAPTER_SCALING).astype(BF16)
        total = nn(total, place_matrix(True))
        total = jnp.concatenate(
            [
                total[:RANK, : 2 * HD],
                total[RANK : 2 * RANK, 2 * HD : 3 * HD],
                total[2 * RANK :, 3 * HD :],
            ],
            axis=1,
        )
        zero = jnp.zeros_like(total)
        heads_o[:, : 4 * HD] = jnp.where(at[0] == 0, total, zero).astype(BF16)
        heads_o[:, 4 * HD :] = jnp.where(at[0] == 0, zero, total).astype(BF16)


def head_blocks(value, which):
    return jnp.concatenate([value[which * 4 + place] for place in range(4)], axis=1)


def mix_kernel(at, mixed, out_own, out_oth, upper, tokens, gain, hidden_o, normal_o, narrow_o):
    k = at[0]
    width = tokens.shape[2]
    total = nn(head_blocks(mixed, k), out_own[...]) + nn(head_blocks(mixed, 1 - k), out_oth[...])
    narrow = total[:, width : width + RANK].astype(BF16)
    narrow_o[...] = narrow
    total = tokens[0].astype(F32) + total[:, :width] + ADAPTER_SCALING * nn(narrow, upper[0])
    hidden_o[...] = total
    root = lax.rsqrt(jnp.mean(total * total, axis=1, keepdims=True) + EPS)
    normal_o[...] = (total * root * gain[...]).astype(BF16)


def norm_back(value, grad, gain):
    root = lax.rsqrt(jnp.mean(value * value, axis=1, keepdims=True) + EPS)
    unit = value * root
    grad = grad * gain
    return root * (grad - unit * jnp.mean(grad * unit, axis=1, keepdims=True))


def mix_back_kernel(
    at, hidden, cotangent, own, arrived, far, gain, out_own, out_oth, upper,
    grad_o, low_o, mixed_o, narrow_o,
):
    k = at[0]
    rows = hidden.shape[0]
    grad = own[:rows].astype(F32) + arrived[:rows].astype(F32) + far[...].astype(F32)
    grad = cotangent[0].astype(F32) + norm_back(hidden[...], grad, gain[...])
    grad_o[...] = grad
    low = grad.astype(BF16)
    low_o[...] = low
    table = jnp.transpose(upper[0].astype(F32))
    table = jnp.concatenate([table, jnp.zeros((table.shape[0], 2 * HD - RANK), F32)], axis=1)
    narrow = (ADAPTER_SCALING * nn(low, table.astype(BF16))).astype(BF16)
    narrow_o[...] = narrow[:, :RANK]
    low = jnp.concatenate([low, narrow], axis=1)
    for which, source in ((k, out_own), (1 - k, out_oth)):
        value = nt(low, source[...]).astype(BF16)
        for place in range(4):
            mixed_o[which * 4 + place] = value[:, place * 2 * HD : (place + 1) * 2 * HD]


def mix_grads_kernel(at, mixed, low, narrow, narrow_back, out_o):
    out_o[:RANK] = (ADAPTER_SCALING * tn(narrow[...], low[...])).astype(BF16)
    for i in range(8):
        value = tn(narrow_back[...], mixed[i])
        out_o[RANK:, i * 2 * HD : (i + 1) * 2 * HD] = value.astype(BF16)


def last_kernel(at, grads, own, own_x, oth, oth_x, lower, hidden, tokens, gain, out):
    k, x = at[0], at[1]
    width = hidden.shape[1]
    total = 0.0
    for which, side, source in ((k, x, own), (k, 1 - x, own_x), (1 - k, x, oth), (1 - k, 1 - x, oth_x)):
        lanes = pl.ds(pl.multiple_of(side * 2 * HD, 2 * HD), 2 * HD)
        value = [grads[which * 4 + place, :, lanes] for place in range(4)]
        total += nn(jnp.concatenate(value, axis=1), source[...])
    narrow = (ADAPTER_SCALING * total[:, width : width + 3 * RANK]).astype(BF16)
    total = total[:, :width] + nn(narrow, lower[0])
    value = tokens[0].astype(F32)
    out[...] = (hidden[...] + norm_back(value, total, gain[...])).astype(BF16)


def weight_copies(at, sources, dst, sem, down):
    k, x, y = at[0], at[1], at[2]

    def lanes(start, size):
        return pl.ds(pl.multiple_of(start, 2 * HD), size)

    def rows(start, size):
        return pl.ds(pl.multiple_of(start, 16), size)

    if down:
        height, width = dst.shape[0], sources[0].shape[1]
    else:
        height, width = sources[0].shape[1:]
    if len(sources) == 1:
        if down:
            pairs = [(sources[0], dst.at[:, pl.ds(0, width)])]
        else:
            pairs = [
                (sources[0].at[m], dst.at[pl.ds(0, height), pl.ds(m * width, width)])
                for m in range(2)
            ]
        return [
            (None, [pltpu.make_async_copy(a, b, sem.at[i]) for i, (a, b) in enumerate(pairs)])
        ]
    local, mine, *pieces = sources
    zero, one = [], []
    if down:
        part = height // 2
        for j, source in enumerate((local, mine)):
            zero.append((source, dst.at[:, lanes((y + j) % 2 * width, width)]))
        tall = pieces[0].shape[0] - part * width // pieces[0].shape[1]
        for j, source in enumerate(pieces):
            for a, b, cols, at_row, at_lane in down_parts((part, width), source.shape[1]):
                one.append(
                    (
                        source.at[pl.ds(tall + at_row, b - a), pl.ds(at_lane, cols.size)],
                        dst.at[
                            rows((x + j) % 2 * part + a, b - a),
                            lanes((y + j // 2) % 2 * width + cols.start, cols.size),
                        ],
                    )
                )
    else:
        for j, source in enumerate((local, mine)):
            for m in range(2):
                at_row = rows((y + j) % 2 * height, height)
                zero.append((source.at[m], dst.at[at_row, pl.ds(m * width, width)]))
        for j, source in enumerate(pieces):
            at_row = rows((y + j // 2) % 2 * height, height)
            source = source.at[pl.ds(0, height)]
            one.append((source, dst.at[at_row, lanes((x + j) % 2 * width, width)]))
    return [
        (when, [pltpu.make_async_copy(a, b, sem.at[i]) for i, (a, b) in enumerate(pairs)])
        for when, pairs in ((k == 0, zero), (k == 1, one))
    ]


def for_copies(groups, what):
    for when, copies in groups:
        if when is None:
            for copy in copies:
                what(copy)
        else:

            @pl.when(when)
            def _():
                for copy in copies:
                    what(copy)


def put_down_lower(down, small):
    width = 2 * HD
    table = jnp.transpose(small[2].astype(F32))
    table = jnp.concatenate(
        [table, jnp.zeros((table.shape[0], width - table.shape[1]), F32)], axis=1
    )
    down[:, down.shape[1] - width :] = table.astype(BF16)


def both_tokens(step, own, far, own_oth, far_oth):
    here = jnp.concatenate([own[...], far[...]], axis=0).astype(F32)
    there = jnp.concatenate([own_oth[...], far_oth[...]], axis=0).astype(F32)
    return jnp.where(step == 0, here, there).astype(BF16)


def wide_table(table):
    table = jnp.transpose(table.astype(F32))
    return jnp.concatenate(
        [table, jnp.zeros((table.shape[0], 2 * HD - table.shape[1]), F32)], axis=1
    ).astype(BF16)


def ffn_kernel(many, at, own, far, own_oth, far_oth, cot, cot_far, cot_oth, cot_far_oth, *rest):
    lower, small, upper = rest[:3]
    sources, down_sources = rest[3 : 3 + many], rest[3 + many : 3 + 2 * many]
    part_own, part_oth, act_o, grad_o, narrow_o, back_o, weights, down, tables, sem = rest[
        3 + 2 * many :
    ]
    step = pl.program_id(0)
    units = small.shape[2]
    first = weight_copies(at, sources, weights, sem.at[0], False)
    second = weight_copies(at, down_sources, down, sem.at[1], True)

    @pl.when(step == 0)
    def _():
        for_copies(second, lambda copy: copy.start())
        for_copies(first, lambda copy: copy.start())
        put_down_lower(down, small)
        tables[0] = wide_table(lower[0][3 * RANK :])
        tables[1] = wide_table(upper[0])
        for_copies(second, lambda copy: copy.wait())

    value = both_tokens(step, own, far, own_oth, far_oth)
    grad = both_tokens(step, cot.at[0], cot_far.at[0], cot_oth, cot_far_oth)
    narrow_o[0] = nn(value, tables[0]).astype(BF16)[:, : 2 * RANK]
    narrow = (ADAPTER_SCALING * nn(grad, tables[1])).astype(BF16)
    back_o[0] = narrow[:, :RANK]
    grad = jnp.concatenate([grad, narrow], axis=1)
    grad_act = nt(grad, down[...])

    @pl.when(step == 0)
    def _():
        for_copies(first, lambda copy: copy.wait())
        for i in range(2):
            term = lower[0][(3 + i) * RANK : (4 + i) * RANK]
            at_lanes = slice(i * units, (i + 1) * units)
            merged = weights[:, at_lanes].astype(F32) + ADAPTER_SCALING * tn(term, small[i])
            weights[:, at_lanes] = merged.astype(BF16)

    both = nn(value, weights[...])
    gate, up = both[:, :units], both[:, units:]
    sig = 0.5 * jnp.tanh(0.5 * gate) + 0.5
    silu = gate * sig
    act_o[0] = (silu * up).astype(BF16)
    grad_gate = (grad_act * up * (sig + silu * (1.0 - sig))).astype(BF16)
    grad_up = (grad_act * silu).astype(BF16)
    grad_both = jnp.concatenate([grad_gate, grad_up], axis=1)
    grad_o[0] = grad_both
    part = nt(grad_both, weights[...]).astype(BF16)

    @pl.when(step == 0)
    def _():
        part_own[...] = part

    @pl.when(step == 1)
    def _():
        part_oth[...] = part


def ffn_down_kernel(many, at, act, small, upper, *rest):
    sources = rest[:many]
    part_own, part_oth, zd_o, down, sem = rest[many:]
    step = pl.program_id(0)
    width = upper.shape[2]
    copies = weight_copies(at, sources, down, sem.at[0], True)

    @pl.when(step == 0)
    def _():
        for_copies(copies, lambda copy: copy.start())
        put_down_lower(down, small)
        for_copies(copies, lambda copy: copy.wait())

    part = nn(act[0], down[...])
    zd = part[:, width : width + RANK].astype(BF16)
    zd_o[0] = zd
    part = (part[:, :width] + ADAPTER_SCALING * nn(zd, upper[0])).astype(BF16)

    @pl.when(step == 0)
    def _():
        part_own[...] = part

    @pl.when(step == 1)
    def _():
        part_oth[...] = part


def ffn_grads_kernel(at, own, far, own_oth, far_oth, cot, cot_far, cot_oth, cot_far_oth, *rest):
    act, grads, narrow, narrow_back, zd, small, wide_o, quarter_o, lanes, wide, quarter = rest
    step = pl.program_id(0)
    units = small.shape[2]

    @pl.when(step == 0)
    def _():
        wide[...] = jnp.zeros_like(wide)
        quarter[...] = jnp.zeros_like(quarter)
        lanes[...] = jnp.zeros_like(lanes)
        for i in range(2):
            table = jnp.transpose(small[i].astype(F32))
            zero = jnp.zeros_like(table)
            table = jnp.concatenate([table, zero] if i == 0 else [zero, table], axis=1)
            lanes[i * units : (i + 1) * units, : 2 * RANK] = table.astype(BF16)

    value = both_tokens(step, own, far, own_oth, far_oth)
    grad = both_tokens(step, cot.at[0], cot_far.at[0], cot_oth, cot_far_oth)
    inner = (ADAPTER_SCALING * nn(grads[0], lanes[...])).astype(BF16)[:, : 2 * RANK]
    wide[:RANK] += ADAPTER_SCALING * tn(zd[0], grad)
    wide[RANK:] += tn(inner, value)
    both = tn(narrow[0], grads[0])
    quarter[:RANK] += ADAPTER_SCALING * both[:RANK, :units]
    quarter[RANK : 2 * RANK] += ADAPTER_SCALING * both[RANK:, units:]
    quarter[2 * RANK :] += tn(narrow_back[0], act[0])

    @pl.when(step == 1)
    def _():
        wide_o[...] = wide[...].astype(BF16)
        quarter_o[...] = quarter[...].astype(BF16)


def ring_kernel(at, *rest):
    out = rest[4]
    for d in range(4):

        @pl.when((at[4] + 4 - pl.program_id(0)) % 4 == d)
        def _():
            out[0] = rest[d][...].astype(out.dtype)


def assemble_kernel(at, own, *rest):
    z = at[4]
    up, down, out = rest[:3], rest[3:6], rest[6]
    place = pl.program_id(0)

    @pl.when(place == z)
    def _():
        out[0] = own[...].astype(out.dtype)

    for d in range(3):

        @pl.when(z - place == d + 1)
        def _():
            out[0] = up[d][...].astype(out.dtype)

        @pl.when(place - z == d + 1)
        def _():
            out[0] = down[d][...].astype(out.dtype)


def plus(here, there):
    return (here.astype(F32) + there.astype(F32)).astype(BF16)


def tie(*values):
    return lax.optimization_barrier(values)


def tie_all(values):
    return lax.optimization_barrier(values)


def heads_tokens(value):
    return lax.all_to_all(value, CT, 0, 0, axis_index_groups=COLUMN, tiled=True)


UP = [(i, i + 1) for i in range(3)]
RING = [(i, (i + 1) % 4) for i in range(4)]
DOWN = [(i + 1, i) for i in range(3)]


def body(
    shards,
    inputs,
    cotangent,
    segments,
    adapter_index,
    query_weight,
    key_value_weight,
    output_weight,
    gate_up_weight,
    down_weight,
    norm_attn,
    norm_ffn,
    q_gain,
    k_gain,
    input_adapter_lower,
    query_adapter_upper,
    key_value_adapter_upper,
    gate_up_adapter_upper,
    output_adapter_lower,
    output_adapter_upper,
    down_adapter_lower,
    down_adapter_upper,
):
    ctx = lax.axis_index("ctx")
    x, k = ctx // 2, ctx % 2
    z = lax.axis_index("tp")
    y = lax.axis_index("shard")
    tok = inputs.shape[1]
    half = 2 * tok
    sub = tok // 4
    width = inputs.shape[2]
    hidden_units = gate_up_weight.shape[2]
    slot = adapter_index[0]
    segment = segments[0]
    pair = shards == 2
    swap_y = [(0, 1), (1, 0)]
    cols = 2 * HD
    at = jnp.stack([k, x, y, slot, z]).astype(jnp.int32)
    K, X, Y, SLOT, Z = range(5)

    def shard_rows(piece, axis):
        if pair:
            return order2(piece, lax.ppermute(piece, "shard", swap_y), y, axis)
        return lax.all_gather(piece, "shard", axis=axis, tiled=True)

    def over_y(cores):
        return [
            ((s * 4 + c) * 4 + t, ((s ^ 1) * 4 + c) * 4 + t)
            for s in range(2)
            for c in cores
            for t in range(4)
        ]

    tokens_other = lax.ppermute(inputs[0], "ctx", CORE)
    by_slot = lambda i, s: (s[SLOT], 0, 0)
    prepared = run(
        prepare_kernel,
        "prepare",
        (1,),
        at,
        [
            (query_weight, (query_weight.shape[0], cols), lambda i, s: (0, s[K])),
            whole(key_value_weight),
            (output_weight, (cols, output_weight.shape[1]), lambda i, s: (s[K], 0)),
            (gate_up_adapter_upper, (1, 2, RANK, hidden_units), lambda i, s: (s[SLOT], 0, 0, 0)),
            (jnp.swapaxes(down_adapter_lower, 1, 2), (1, RANK, hidden_units), by_slot),
            (query_adapter_upper, (1, RANK, cols), lambda i, s: (s[SLOT], 0, s[K])),
            (key_value_adapter_upper, (1, 2, RANK, cols), lambda i, s: (s[SLOT], 0, 0, 0)),
            (
                jnp.swapaxes(output_adapter_lower, 1, 2),
                (1, RANK, cols),
                lambda i, s: (s[SLOT], 0, s[K]),
            ),
        ],
        [
            out_whole((3 * cols, query_weight.shape[0]), BF16),
            out_whole((3, RANK, hidden_units), BF16),
            out_whole((2 * cols, cols), BF16),
            out_whole((cols, cols), BF16),
        ],
    )
    piece_rows, small_ffn, upper_qkv, low_rows = prepared
    dense_rows = shard_rows(piece_rows, 1)
    dense_qkv, rows_here = dense_rows[: 2 * cols], dense_rows[2 * cols :]

    far_z = [(c * 4 + t, c * 4 + (t ^ 2)) for c in (1, 3) for t in range(4)]
    far_x = [(1, 3), (3, 1)]
    if pair:
        (piece,) = run(
            pieces_kernel,
            "pieces",
            (1,),
            at,
            [
                (gate_up_weight, (1,) + gate_up_weight.shape[1:], lambda i, s: (s[X], 0, 0)),
                (down_weight, (hidden_units // 2, down_weight.shape[1]), lambda i, s: (s[X], 0)),
            ],
            [
                out_whole(
                    (
                        gate_up_weight.shape[1] + down_weight.shape[1] // 2,
                        hidden_units,
                    ),
                    BF16,
                )
            ],
        )
        piece = lax.ppermute(piece, CT, far_z)

    block = tok // 4
    blocks = half // block
    half_dim = HD // 2
    first_query = x * half
    inverse = THETA ** (-(jnp.arange(half_dim, dtype=F32) * 2.0 / HD))
    inverse = jnp.concatenate([inverse] * 3 + [jnp.zeros_like(inverse)])
    places = jnp.arange(2 * block + blocks, dtype=jnp.int32)
    places = jnp.where(places < 2 * block, places, first_query + block * (places - 2 * block))
    angles = places.astype(F32)[:, None] * inverse[None, :]
    turns = jnp.stack([jnp.cos(angles), jnp.sin(angles)])

    by_row = lambda i, s: (i, 0)
    by_step = lambda i, s: (i, 0, 0)
    lower_table = jnp.swapaxes(input_adapter_lower, 1, 2)
    lower_spec = (lower_table, (1, 5 * RANK, width), by_slot)
    ones = jnp.ones((half_dim,), F32)
    gains = jnp.stack(
        [
            jnp.concatenate([q_gain[part], q_gain[part], k_gain[part], ones])
            for part in (slice(0, half_dim), slice(half_dim, HD))
        ]
    )
    gain_attn, gain_ffn = norm_attn[None], norm_ffn[None]
    own_row = lambda i, s: (jnp.minimum(i, 3), 0)
    oth_row = lambda i, s: (jnp.maximum(i - 4, 0), 0)
    chip_row = lambda i, s: (jnp.where(i < 4, s[K] * 4 + i, (1 - s[K]) * 4 + i - 4), 0)
    normalized, narrow, queries, keyvals, raw = run(
        project_kernel,
        "project",
        (8,),
        at,
        [
            (inputs[0], (block, width), own_row),
            (tokens_other, (block, width), oth_row),
            whole(gain_attn),
            (dense_rows, (2 * cols, width), fixed(0, 0)),
            (lower_table, (1, 3 * RANK, width), by_slot),
            whole(upper_qkv),
            whole(turns),
            whole(gains),
        ],
        [
            ((half, width), BF16, (block, width), chip_row),
            ((half, 3 * RANK), BF16, (block, 3 * RANK), chip_row),
            ((half, cols), BF16, (block, cols), chip_row),
            ((half, cols), BF16, (block, cols), chip_row),
            ((half, 2 * cols), F32, (block, 2 * cols), chip_row),
        ],
        [pltpu.VMEM((3 * cols, width), BF16)],
    )
    keyvals_before = lax.ppermute(keyvals, "ctx", [(0, 2), (1, 3)])

    size = half // 4
    seg_rows = segment.reshape(-1, 1, size)
    keyvals, small_from = tie(keyvals, small_ffn)
    small_far = lax.ppermute(small_from, "tp", Z_XOR[2])
    if pair:
        keyvals, gate_up_from = tie(keyvals, gate_up_weight)
        mine_g = lax.ppermute(gate_up_from, SCT, over_y((0, 2)))
    acc = attention_forward(queries, keyvals, seg_rows, segment, at, 0, size, size)
    acc, cot_here, out_rows = tie(acc, cotangent[0], jnp.concatenate([rows_here, low_rows], axis=1))
    out_own = lax.all_gather(out_rows, "tp", axis=0, tiled=True)
    cot_oth = lax.ppermute(cot_here, "ctx", CORE)
    mixed, mixed_low, lse = attention_forward(
        queries, keyvals_before, seg_rows, segment, at, half, size, 2 * size, acc
    )
    mixed_low, small_far = tie(mixed_low, small_far)
    small_ffn = jnp.where(k == 0, small_ffn, small_far)
    if pair:
        mixed_low, piece, down_from = tie(mixed_low, piece, down_weight)
        piece_x = lax.ppermute(piece, "ctx", far_x)
        piece_y = lax.ppermute(piece, SCT, over_y((1, 3)))
        mine_d = lax.ppermute(down_from, SCT, over_y((0, 2)))

    mixed_all = heads_tokens(mixed_low.reshape(8, sub, cols))
    qkv_rows = rows_at(jnp.concatenate([dense_qkv, upper_qkv], axis=1), x, cols)
    mixed_all, small_ffn, cot_oth, qkv_rows = tie(mixed_all, small_ffn, cot_oth, qkv_rows)
    out_oth = lax.ppermute(out_own, "ctx", CORE)
    if pair:
        mixed_all, mine_g, piece_x, piece_y, out_own = tie(
            mixed_all, mine_g, piece_x, piece_y, out_own
        )
        piece_xy = lax.ppermute(piece_y, "ctx", far_x)
        pieces = [piece, piece_x, piece_y, piece_xy]
        sources = [gate_up_weight, mine_g] + pieces
        down_sources = [down_weight, mine_d] + pieces
    else:
        full_g = lax.all_gather(gate_up_weight, "shard", axis=1, tiled=True)
        full_d = lax.all_gather(down_weight, "shard", axis=1, tiled=True)
        sources = [jnp.where(k == 0, full_g, lax.ppermute(full_g, "tp", Z_XOR[2]))]
        down_sources = [jnp.where(k == 0, full_d, lax.ppermute(full_d, "tp", Z_XOR[2]))]
    z_block = lambda i, s: (0, s[Z], 0)
    upper_out_spec = (output_adapter_upper, (1, RANK, width), lambda i, s: (s[SLOT], 0, 0))
    hidden_state, normalized_second, narrow_out = run(
        mix_kernel,
        "mix",
        (1,),
        at,
        [
            whole(mixed_all),
            whole(out_own),
            whole(out_oth),
            upper_out_spec,
            (inputs, (1, sub, width), z_block),
            whole(gain_ffn),
        ],
        [
            out_whole((sub, width), F32),
            out_whole((sub, width), BF16),
            out_whole((sub, RANK), BF16),
        ],
    )

    second = normalized_second
    second_oth = lax.ppermute(second, "ctx", CORE)
    second_far = lax.ppermute(second, "tp", Z_XOR[1])
    second_far_oth = lax.ppermute(second_far, "ctx", CORE)
    upper_down_spec = (down_adapter_upper, (1, RANK, width), by_slot)
    z_far = lambda i, s: (0, s[Z] ^ 1, 0)
    ffn_tokens = [
        whole(second),
        whole(second_far),
        whole(second_oth),
        whole(second_far_oth),
        (cotangent, (1, sub, width), z_block),
        (cotangent, (1, sub, width), z_far),
        (cot_oth, (sub, width), lambda i, s: (s[Z], 0)),
        (cot_oth, (sub, width), lambda i, s: (s[Z] ^ 1, 0)),
    ]
    tall = 2 * sub
    qkv_rows, second_far_oth = tie(qkv_rows, second_far_oth)
    qkv_own = lax.all_gather(qkv_rows, "tp", axis=0, tiled=True)
    ffn_tokens[3] = whole(second_far_oth)
    part_own, part_oth, active, grad_both, narrow_second, narrow_back_second = run(
        functools.partial(ffn_kernel, len(sources)),
        "ffn",
        (2,),
        at,
        ffn_tokens
        + [lower_spec, whole(small_ffn), upper_down_spec]
        + [(source, None, None) for source in sources + down_sources],
        [
            out_whole((tall, width), BF16),
            out_whole((tall, width), BF16),
            ((2, tall, hidden_units), BF16, (1, tall, hidden_units), by_step),
            ((2, tall, 2 * hidden_units), BF16, (1, tall, 2 * hidden_units), by_step),
            ((2, tall, 2 * RANK), BF16, (1, tall, 2 * RANK), by_step),
            ((2, tall, RANK), BF16, (1, tall, RANK), by_step),
        ],
        [
            pltpu.VMEM((width, 2 * hidden_units), BF16),
            pltpu.VMEM((hidden_units, width + cols), BF16),
            pltpu.VMEM((2, width, cols), BF16),
            pltpu.SemaphoreType.DMA((2, 24)),
        ],
        LONG,
    )
    part_arrived = lax.ppermute(part_oth, "ctx", CORE)
    part_give = (part_own[sub:].astype(F32) + part_arrived[sub:].astype(F32)).astype(BF16)
    part_give, active, qkv_own = tie(part_give, active, qkv_own)
    part_far = lax.ppermute(part_give, "tp", Z_XOR[1])
    qkv_own_x = lax.ppermute(qkv_own, "ctx", XSIDE)

    down_own, down_oth, zd = run(
        functools.partial(ffn_down_kernel, len(sources)),
        "ffn_down",
        (2,),
        at,
        [
            (active, (1, tall, hidden_units), by_step),
            whole(small_ffn),
            upper_down_spec,
        ]
        + [(source, None, None) for source in down_sources],
        [
            out_whole((tall, width), BF16),
            out_whole((tall, width), BF16),
            ((2, tall, RANK), BF16, (1, tall, RANK), by_step),
        ],
        [pltpu.VMEM((hidden_units, width + cols), BF16), pltpu.SemaphoreType.DMA((1, 24))],
        LONG,
    )
    hidden_back, down_own, down_oth, zd = tie(hidden_state, down_own, down_oth, zd)

    grad_hidden, grad_hidden_low, grad_mixed_all, narrow_back = run(
        mix_back_kernel,
        "mix_back",
        (1,),
        at,
        [
            whole(hidden_back),
            (cotangent, (1, sub, width), z_block),
            whole(part_own),
            whole(part_arrived),
            whole(part_far),
            whole(gain_ffn),
            whole(out_own),
            whole(out_oth),
            upper_out_spec,
        ],
        [
            out_whole((sub, width), F32),
            out_whole((sub, width), BF16),
            out_whole((8, sub, cols), BF16),
            out_whole((sub, RANK), BF16),
        ],
    )
    grad_mixed_all, grad_both, down_oth = tie(grad_mixed_all, grad_both, down_oth)
    grad_mixed = heads_tokens(grad_mixed_all).reshape(half, cols)
    down_arrived = lax.ppermute(down_oth, "ctx", CORE)
    down_give = (down_own[sub:].astype(F32) + down_arrived[sub:].astype(F32)).astype(BF16)
    down_far = lax.ppermute(down_give, "tp", Z_XOR[1])
    final = hidden_state + (
        down_own[:sub].astype(F32) + down_arrived[:sub].astype(F32) + down_far.astype(F32)
    )
    final = final.astype(BF16)
    wide_ffn, quarter_grads = run(
        ffn_grads_kernel,
        "ffn_grads",
        (2,),
        at,
        ffn_tokens
        + [
            (active, (1, tall, hidden_units), by_step),
            (grad_both, (1, tall, 2 * hidden_units), by_step),
            (narrow_second, (1, tall, 2 * RANK), by_step),
            (narrow_back_second, (1, tall, RANK), by_step),
            (zd, (1, tall, RANK), by_step),
            whole(small_ffn),
        ],
        [out_whole((3 * RANK, width), BF16), out_whole((3 * RANK, hidden_units), BF16)],
        [
            pltpu.VMEM((2 * hidden_units, cols), BF16),
            pltpu.VMEM((3 * RANK, width), F32),
            pltpu.VMEM((3 * RANK, hidden_units), F32),
        ],
        LONG,
    )
    (wide_mix,) = run(
        mix_grads_kernel,
        "mix_grads",
        (1,),
        at,
        [whole(mixed_all), whole(grad_hidden_low), whole(narrow_out), whole(narrow_back)],
        [out_whole((2 * RANK, width), BF16)],
    )
    wide_early = jnp.concatenate([wide_mix, wide_ffn], axis=0)
    grad_mixed, wide_early, qkv_own_x = tie(grad_mixed, wide_early, qkv_own_x)
    wide_near = lax.ppermute(wide_early, "tp", Z_XOR[1])
    if pair:
        slot_other = lax.ppermute(adapter_index, "shard", swap_y)[0]

    dq_before, dkv_before = attention_backward(
        queries,
        keyvals_before,
        seg_rows,
        grad_mixed,
        mixed,
        lse,
        segment,
        at,
        half,
        size,
        size,
    )
    dkv_after = lax.ppermute(dkv_before, "ctx", [(2, 0), (3, 1)])
    dq_before, wide_near, quarter_grads, qkv_own, qkv_own_x, final = tie(
        dq_before, wide_near, quarter_grads, qkv_own, qkv_own_x, final
    )
    out_up_1 = lax.ppermute(final, "tp", UP)
    out_down_1 = lax.ppermute(final, "tp", DOWN)
    if pair:
        dq_before, slot_other = tie(dq_before, slot_other)
    qkv_oth = lax.ppermute(qkv_own, "ctx", CORE)
    qkv_oth_x = lax.ppermute(qkv_own_x, "ctx", CORE)
    wide_early = plus(wide_early, wide_near)
    early = jnp.concatenate(
        [jnp.pad(wide_early, ((0, 0), (0, hidden_units - width))), quarter_grads], axis=0
    )
    early_far = lax.ppermute(early, "tp", Z_XOR[2])
    dq, dkv = attention_backward(
        queries,
        keyvals,
        seg_rows,
        grad_mixed,
        mixed,
        lse,
        segment,
        at,
        0,
        size,
        size,
        dq_before,
    )
    dq, early_far, out_up_1, out_down_1 = tie(dq, early_far, out_up_1, out_down_1)
    out_up_2 = lax.ppermute(out_up_1, "tp", UP[1:])
    out_down_2 = lax.ppermute(out_down_1, "tp", DOWN[:2])
    early = jnp.concatenate(
        [
            plus(early[: 5 * RANK], early_far[: 5 * RANK]),
            jnp.where(k == 0, early[5 * RANK :], early_far[5 * RANK :]),
        ],
        axis=0,
    )
    tall_blocks = blocks // 2
    d_projected, wide_attn, head_grads = run(
        project_back_kernel,
        "project_back",
        (tall_blocks,),
        at,
        [
            (dq, (2 * block, cols), by_row),
            (dkv, (2 * block, cols), by_row),
            (dkv_after, (2 * block, cols), by_row),
            (raw, (2 * block, 2 * cols), by_row),
            whole(turns),
            whole(gains),
            (narrow, (2 * block, 3 * RANK), by_row),
            (normalized, (2 * block, width), by_row),
            whole(upper_qkv),
        ],
        [
            ((half, 2 * cols), BF16, (2 * block, 2 * cols), by_row),
            out_whole((3 * RANK, width), BF16),
            out_whole((RANK, 4 * cols), BF16),
        ],
        [pltpu.VMEM((3 * RANK, width), F32), pltpu.VMEM((3 * RANK, 2 * cols), F32)],
        LONG,
    )
    d_projected, out_up_2, out_down_2 = tie(d_projected, out_up_2, out_down_2)
    out_up_3 = lax.ppermute(out_up_2, "tp", UP[2:])
    out_down_3 = lax.ppermute(out_down_2, "tp", DOWN[:1])

    d_all = heads_tokens(d_projected.reshape(8, sub, 2 * cols))
    def lanes_to(value, size):
        return jnp.pad(value, ((0, 0), (0, size - value.shape[1])))

    packed = jnp.concatenate(
        [early, lanes_to(wide_attn, hidden_units), lanes_to(head_grads, hidden_units)], axis=0
    )

    packed = plus(packed, lax.ppermute(packed, "ctx", CORE))
    packed = plus(packed, lax.ppermute(packed, "ctx", XSIDE))
    slots = jnp.arange(ADAPT, dtype=jnp.int32)

    def placed(value, which):
        mask = (slots == which).astype(F32).reshape((ADAPT,) + (1,) * value.ndim)
        return mask * value.astype(F32)[None]

    if pair:
        both = jnp.stack([packed, lax.ppermute(packed, "shard", swap_y)])
    else:
        both = lax.psum(placed(packed, slot), "shard")
    (grad_tokens,) = run(
        last_kernel,
        "last",
        (1,),
        at,
        [
            whole(d_all),
            whole(qkv_own),
            whole(qkv_own_x),
            whole(qkv_oth),
            whole(qkv_oth_x),
            (lower_table, (1, 3 * RANK, width), by_slot),
            whole(grad_hidden),
            (inputs, (1, sub, width), z_block),
            whole(gain_attn),
        ],
        [out_whole((sub, width), BF16)],
    )
    up_1 = lax.ppermute(grad_tokens, "tp", RING)
    own_width = width // (shards * 4)
    in_attn = rows_at(both[:, 8 * RANK : 11 * RANK, :width], y * 4 + ctx, own_width, 2)
    in_attn = plus(in_attn, lax.ppermute(in_attn, "tp", Z_XOR[1]))
    up_1, in_attn, both = tie(up_1, in_attn, both)
    up_2 = lax.ppermute(up_1, "tp", RING)
    in_far = lax.ppermute(in_attn, "tp", Z_XOR[2])
    wide = both[:, : 5 * RANK, :width]
    in_ffn = rows_at(wide[:, 3 * RANK :], y * 4 + ctx, own_width, 2)
    rest = jnp.concatenate([both[:, 5 * RANK : 8 * RANK], both[:, 11 * RANK :]], axis=1)
    if pair:
        slots_here = (slot, slot_other)
        rest = sum(placed(rest[i], which) for i, which in enumerate(slots_here))
    quarter_sum, heads = rest[:, : 3 * RANK], rest[:, 3 * RANK :, : 4 * cols]
    grad_b_query = jnp.concatenate([heads[..., :cols], heads[..., 2 * cols : 3 * cols]], axis=-1)
    grad_b_keyval = jnp.stack(
        [
            jnp.concatenate(
                [heads[..., core * 2 * cols + c * HD :][..., :HD] for core in range(2)], axis=-1
            )
            for c in (2, 3)
        ],
        axis=1,
    )
    grad_b_gate_up = quarter_sum[:, : 2 * RANK].reshape(ADAPT, 2, RANK, -1)
    grad_a_down = jnp.swapaxes(quarter_sum[:, 2 * RANK :], 1, 2)
    in_all = jnp.concatenate([plus(in_attn, in_far), in_ffn], axis=1)
    if pair:
        wide = sum(placed(wide[i, : 3 * RANK], which) for i, which in enumerate(slots_here))
        in_all = sum(placed(in_all[i], which) for i, which in enumerate(slots_here))
    else:
        wide, in_all = wide.astype(F32), in_all.astype(F32)
    grad_b_out = wide[:, :RANK]
    grad_a_out = wide[:, RANK : 2 * RANK]
    grad_b_down = wide[:, 2 * RANK : 3 * RANK]
    grad_a_out = jnp.concatenate(
        [rows_at(grad_a_out, z, cols, 2), rows_at(grad_a_out, 4 + z, cols, 2)], axis=2
    )
    grad_a_out = jnp.swapaxes(grad_a_out, 1, 2)
    grad_adapt_in = jnp.swapaxes(in_all, 1, 2)
    up_2, final, grad_b_query, grad_b_keyval, grad_b_gate_up, grad_a_down = tie(
        up_2, final, grad_b_query, grad_b_keyval, grad_b_gate_up, grad_a_down
    )
    up_3 = lax.ppermute(up_2, "tp", RING)
    line = [grad_tokens, up_1, up_2, up_3]
    z_row = lambda i, s: (0, i, 0)
    (grad_inputs,) = run(
        ring_kernel,
        "assemble",
        (4,),
        at,
        [whole(part) for part in line],
        [((1, tok, width), F32, (1, sub, width), z_row)],
    )
    line = [final, out_up_1, out_up_2, out_up_3, out_down_1, out_down_2, out_down_3]
    (result,) = run(
        assemble_kernel,
        "assemble_out",
        (4,),
        at,
        [whole(part) for part in line],
        [((1, tok, width), BF16, (1, sub, width), z_row)],
        cost=LONG,
    )
    return (
        result,
        grad_inputs,
        grad_adapt_in,
        grad_b_query,
        grad_b_keyval,
        grad_b_gate_up,
        grad_a_out,
        grad_b_out,
        grad_a_down,
        grad_b_down,
    )


def solution(mesh):
    return jax.shard_map(
        functools.partial(body, mesh.shape["shard"]),
        mesh=mesh,
        in_specs=(
            P("shard", "ctx", None),
            P("shard", "ctx", None),
            P("shard", None),
            P("shard"),
            P("shard", "tp"),
            P(None, "shard", "tp"),
            P("tp", "shard"),
            P(None, "shard", "tp"),
            P("tp", "shard"),
            P(),
            P(),
            P(),
            P(),
            P(),
            P(None, None, "tp"),
            P(None, None, None, "tp"),
            P(None, None, None, "tp"),
            P(None, "tp", None),
            P(),
            P(None, "tp", None),
            P(),
        ),
        out_specs=(
            P("shard", "ctx", None),
            P("shard", "ctx", None),
            P(None, ("shard", "ctx"), None),
            P(None, None, "tp"),
            P(None, None, None, "tp"),
            P(None, None, None, "tp"),
            P(None, "tp", None),
            P(),
            P(None, "tp", None),
            P(),
        ),
        check_vma=False,
    )
```

```python
import functools

import jax
import jax.numpy as jnp
from jax import lax
from jax.experimental import pallas as pl
from jax.experimental.pallas import tpu as pltpu
from jax.sharding import PartitionSpec as P

HD = 64
RANK = 16
ADAPT = 8
EPS = 1e-05
ADAPTER_SCALING = 2.0
THETA = 1000000.0
LOG2E = 1.4426950408889634
SCALE = HD**-0.5
F32 = jnp.float32
BF16 = jnp.bfloat16
VMEM_LIMIT = 62 * 1024 * 1024

CORE = [(i, i ^ 1) for i in range(4)]
XSIDE = [(i, i ^ 2) for i in range(4)]
Z_XOR = {d: [(i, i ^ d) for i in range(4)] for d in (1, 2, 3)}
CT = ("ctx", "tp")
SCT = ("shard", "ctx", "tp")
COLUMN = [[(2 * x + k) * 4 + z for k in range(2) for z in range(4)] for x in range(2)]

COST = pl.CostEstimate(flops=1 << 20, bytes_accessed=1 << 16, transcendentals=0)
LONG = pl.CostEstimate(flops=30 << 30, bytes_accessed=16 << 20, transcendentals=0)
HIGHEST = lax.Precision.HIGHEST


def nn(left, right):
    return lax.dot_general(left, right, (((1,), (0,)), ((), ())), preferred_element_type=F32)


def nt(left, right):
    return lax.dot_general(left, right, (((1,), (1,)), ((), ())), preferred_element_type=F32)


def tn(left, right):
    return lax.dot_general(left, right, (((0,), (0,)), ((), ())), preferred_element_type=F32)


def rmsnorm(value, gain):
    return value * lax.rsqrt(jnp.mean(value * value, axis=-1, keepdims=True) + EPS) * gain


def order2(own, other, bit, axis=0):
    return jnp.concatenate(
        [jnp.where(bit == 0, own, other), jnp.where(bit == 0, other, own)], axis=axis
    )


def rows_at(value, block, size, axis=0):
    return lax.dynamic_slice_in_dim(value, block * size, size, axis)


def key_loops(segment, first, key_base, bq, bk, keys, step, acc):
    blocks = keys // bk
    low = jnp.minimum(jnp.maximum(segment[first] - key_base, 0) // bk, blocks)
    high = jnp.clip((first + bq - key_base + bk - 1) // bk, 0, blocks)
    low = jnp.minimum(low, high)
    free_low = (jnp.maximum(segment[first + bq - 1] - key_base, 0) + bk - 1) // bk
    free_low = jnp.clip(free_low, low, high)
    free_high = jnp.clip(jnp.maximum(first + 1 - key_base, 0) // bk, free_low, high)
    ahead = free_low - low

    def masked(t, carry):
        j = jnp.where(t < ahead, low + t, free_high + t - ahead)
        return step(j, carry, True)

    acc = lax.fori_loop(0, ahead + high - free_high, masked, acc)
    return lax.fori_loop(free_low, free_high, lambda j, carry: step(j, carry, False), acc)


def row_sums(weights, value):
    return lax.dot_general(
        weights, value, (((1,), (1,)), ((), ())), precision=HIGHEST, preferred_element_type=F32
    )


def fwd_kernel(bq, bk, back, last, segment, at, q_ref, kv_ref, seg_ref, *rest):
    if last:
        acc_in, mixed_ref, low_ref, lse_ref, vx = rest
    else:
        acc_ref, vx = rest
    i = pl.program_id(0)
    keys = kv_ref.shape[0]

    @pl.when(i == 0)
    def _():
        col = lax.broadcasted_iota(jnp.int32, (keys, 2 * HD), 1)
        kv = kv_ref[...]
        swapped = jnp.concatenate([kv[:, HD:], kv[:, :HD]], axis=1)
        ones = jnp.where(col == HD, 1.0, 0.0).astype(BF16)
        vx[...] = jnp.where(col < HD, swapped, ones)

    q = q_ref[...]
    both = jnp.concatenate([q[:, :HD], q[:, HD:]], axis=0)
    q_base = at[1] * (bq * pl.num_programs(0))
    k_base = q_base - back
    seg_col = jnp.broadcast_to(seg_ref[0].astype(F32), (8, bq))
    seg_col = jnp.transpose(seg_col)[:, :1].astype(jnp.int32)

    def step(j, acc, masked):
        off = pl.multiple_of(j * bk, bk)
        scores = nt(both, kv_ref[pl.ds(off, bk), :HD])
        probs = jnp.exp2(scores * (SCALE * LOG2E))
        if masked:
            qi = q_base + i * bq + lax.broadcasted_iota(jnp.int32, (bq, bk), 0)
            ki = k_base + off + lax.broadcasted_iota(jnp.int32, (bq, bk), 1)
            allowed = (ki <= qi) & (ki >= seg_col)
            probs = jnp.where(jnp.concatenate([allowed, allowed], axis=0), probs, 0.0)
        return acc + nn(probs.astype(BF16), vx[pl.ds(off, bk), :])

    if last:
        acc = jnp.concatenate([acc_in[0], acc_in[1]], axis=0)
    else:
        acc = jnp.zeros((2 * bq, 2 * HD), F32)
    acc = key_loops(segment, q_base + i * bq, k_base, bq, bk, keys, step, acc)
    if last:
        total = acc[:, HD : HD + 1]
        out = acc[:, :HD] / total
        out = jnp.concatenate([out[:bq], out[bq:]], axis=1)
        mixed_ref[...] = out
        low_ref[...] = out.astype(BF16)
        pick = jnp.where(lax.broadcasted_iota(jnp.int32, (8, 2 * HD), 1) == HD, 1.0, 0.0)
        lse_ref[0] = jnp.log2(row_sums(pick, acc)[:1])
    else:
        acc_ref[0] = acc[:bq]
        acc_ref[1] = acc[bq:]


def attention_forward(q, kv, seg, segment, at, back, bq, bk, acc_in=None):
    rows, keys = q.shape[0], kv.shape[0]
    last = acc_in is not None
    row = lambda i, *_: (i, 0)
    everything = lambda i, *_: (0, 0)
    heads = lambda i, *_: (0, i, 0)
    in_specs = [
        pl.BlockSpec((bq, 2 * HD), row),
        pl.BlockSpec((keys, 2 * HD), everything),
        pl.BlockSpec((1, 1, bq), lambda i, g, a: (a[1] * (rows // bq) + i, 0, 0)),
    ]
    args = [q, kv, seg]
    if last:
        in_specs.append(pl.BlockSpec((2, bq, 2 * HD), heads))
        args.append(acc_in)
        out_specs = [
            pl.BlockSpec((bq, 2 * HD), row),
            pl.BlockSpec((bq, 2 * HD), row),
            pl.BlockSpec((1, 1, 2 * bq), lambda i, *_: (i, 0, 0)),
        ]
        out_shape = [
            jax.ShapeDtypeStruct((rows, 2 * HD), F32),
            jax.ShapeDtypeStruct((rows, 2 * HD), BF16),
            jax.ShapeDtypeStruct((rows // bq, 1, 2 * bq), F32),
        ]
    else:
        out_specs = pl.BlockSpec((2, bq, 2 * HD), heads)
        out_shape = jax.ShapeDtypeStruct((2, rows, 2 * HD), F32)
    return pl.pallas_call(
        functools.partial(fwd_kernel, bq, bk, back, last),
        grid_spec=pltpu.PrefetchScalarGridSpec(
            num_scalar_prefetch=2,
            grid=(rows // bq,),
            in_specs=in_specs,
            out_specs=out_specs,
            scratch_shapes=[pltpu.VMEM((keys, 2 * HD), BF16)],
        ),
        out_shape=out_shape,
        compiler_params=pltpu.CompilerParams(vmem_limit_bytes=VMEM_LIMIT),
        cost_estimate=LONG,
        name="attn_fwd_last" if last else "attn_fwd_first",
    )(segment, at, *args)


def bwd_kernel(
    bq, bk, back, first, segment, at, q_ref, kv_ref, seg_ref, do_ref, out_ref, lse_ref, *rest
):
    if first:
        dq_ref, dkv_ref, dk, dv = rest
    else:
        dq_in, dq_ref, dkv_ref, dk, dv = rest
    i = pl.program_id(0)

    @pl.when(i == 0)
    def _():
        dk[...] = jnp.zeros_like(dk)
        dv[...] = jnp.zeros_like(dv)

    q = q_ref[...]
    do = do_ref[...]
    both = jnp.concatenate([q[:, :HD], q[:, HD:]], axis=0)
    both_do = jnp.concatenate([do[:, :HD], do[:, HD:]], axis=0)
    lse = lse_ref[0]
    lane = lax.broadcasted_iota(jnp.int32, (8, 2 * HD), 1)
    row = lax.broadcasted_iota(jnp.int32, (8, 2 * HD), 0)
    pick = jnp.where(lane // HD == row, 1.0, 0.0)
    deltas = row_sums(pick, do.astype(F32) * out_ref[...])
    delta = jnp.concatenate([deltas[:1], deltas[1:2]], axis=1)
    q_base = at[1] * (bq * pl.num_programs(0))
    k_base = q_base - back

    def step(j, acc, masked):
        off = pl.multiple_of(j * bk, bk)
        kv = kv_ref[pl.ds(off, bk), :]
        k, v = kv[:, :HD], kv[:, HD:]
        probs = jnp.exp2(nt(k, both) * (SCALE * LOG2E) - lse)
        if masked:
            ki = k_base + off + lax.broadcasted_iota(jnp.int32, (bk, bq), 0)
            qi = q_base + i * bq + lax.broadcasted_iota(jnp.int32, (bk, bq), 1)
            allowed = (ki <= qi) & (ki >= seg_ref[0])
            probs = jnp.where(jnp.concatenate([allowed, allowed], axis=1), probs, 0.0)
        dscores = (probs * (nt(v, both_do) - delta)).astype(BF16)
        dv[pl.ds(off, bk), :] += nn(probs.astype(BF16), both_do)
        dk[pl.ds(off, bk), :] += nn(dscores, both)
        return acc + tn(k, dscores)

    acc = key_loops(
        segment, q_base + i * bq, k_base, bq, bk, kv_ref.shape[0], step,
        jnp.zeros((HD, 2 * bq), F32),
    )
    acc = jnp.transpose(acc) * SCALE
    acc = jnp.concatenate([acc[:bq], acc[bq:]], axis=1)
    dq_ref[...] = acc if first else dq_in[...] + acc

    @pl.when(i == pl.num_programs(0) - 1)
    def _():
        dkv_ref[...] = jnp.concatenate([dk[...] * SCALE, dv[...]], axis=1).astype(dkv_ref.dtype)


def attention_backward(q, kv, seg, do, out, lse, segment, at, back, bq, bk, dq_in=None):
    rows, keys = q.shape[0], kv.shape[0]
    first = dq_in is None
    row = lambda i, *_: (i, 0)
    everything = lambda i, *_: (0, 0)
    flat = lambda i, *_: (i, 0, 0)
    in_specs = [
        pl.BlockSpec((bq, 2 * HD), row),
        pl.BlockSpec((keys, 2 * HD), everything),
        pl.BlockSpec((1, 1, bq), lambda i, g, a: (a[1] * (rows // bq) + i, 0, 0)),
        pl.BlockSpec((bq, 2 * HD), row),
        pl.BlockSpec((bq, 2 * HD), row),
        pl.BlockSpec((1, 1, 2 * bq), flat),
    ]
    args = [q, kv, seg, do, out, lse]
    if not first:
        in_specs.append(pl.BlockSpec((bq, 2 * HD), row))
        args.append(dq_in)
    return pl.pallas_call(
        functools.partial(bwd_kernel, bq, bk, back, first),
        grid_spec=pltpu.PrefetchScalarGridSpec(
            num_scalar_prefetch=2,
            grid=(rows // bq,),
            in_specs=in_specs,
            out_specs=[pl.BlockSpec((bq, 2 * HD), row), pl.BlockSpec((keys, 2 * HD), everything)],
            scratch_shapes=[pltpu.VMEM((keys, HD), F32), pltpu.VMEM((keys, HD), F32)],
        ),
        out_shape=[
            jax.ShapeDtypeStruct((rows, 2 * HD), F32),
            jax.ShapeDtypeStruct((keys, 2 * HD), BF16 if first else F32),
        ],
        compiler_params=pltpu.CompilerParams(vmem_limit_bytes=VMEM_LIMIT),
        cost_estimate=LONG,
        name="attn_bwd_first" if first else "attn_bwd_last",
    )(segment, at, *args)


def run(kernel, name, grid, scalars, inputs, outputs, scratch=(), cost=COST):
    return pl.pallas_call(
        kernel,
        grid_spec=pltpu.PrefetchScalarGridSpec(
            num_scalar_prefetch=1,
            grid=grid,
            in_specs=[
                pl.BlockSpec(memory_space=pl.ANY) if block is None else pl.BlockSpec(block, index)
                for _, block, index in inputs
            ],
            out_specs=[
                pl.BlockSpec(memory_space=pl.ANY) if block is None else pl.BlockSpec(block, index)
                for _, _, block, index in outputs
            ],
            scratch_shapes=list(scratch),
        ),
        out_shape=[jax.ShapeDtypeStruct(shape, kind) for shape, kind, _, _ in outputs],
        compiler_params=pltpu.CompilerParams(vmem_limit_bytes=VMEM_LIMIT),
        cost_estimate=cost,
        name=name,
    )(scalars, *[array for array, _, _ in inputs])


def fixed(*index):
    return lambda i, s: index


def whole(array):
    return (array, array.shape, fixed(*(0,) * array.ndim))


def out_whole(shape, kind):
    return (shape, kind, shape, fixed(*(0,) * len(shape)))


def place_matrix(back):
    at_row = lax.broadcasted_iota(jnp.int32, (4 * HD, 4 * HD), 0)
    at_col = lax.broadcasted_iota(jnp.int32, (4 * HD, 4 * HD), 1)
    if back:
        at_row, at_col = at_col, at_row
    part = HD // 2
    moved = at_row // part % 2 * (2 * HD) + at_row // HD * part + at_row % part
    return jnp.where(moved == at_col, 1.0, 0.0).astype(BF16)


def head_means(value):
    at_row = lax.broadcasted_iota(jnp.int32, (2 * HD, 2 * HD), 0) // (HD // 2)
    at_col = lax.broadcasted_iota(jnp.int32, (2 * HD, 2 * HD), 1) // (HD // 2)
    same = jnp.where(at_row == at_col, 1.0 / HD, 0.0).astype(BF16)
    high = value.astype(BF16)
    rest = (value - high.astype(F32)).astype(BF16)
    return nn(jnp.concatenate([high, rest], axis=1), jnp.concatenate([same, same], axis=0))


def rotation(step, turns, rows, blocks):
    first = turns.shape[1] - blocks
    cos_in, sin_in = turns[0, :rows], turns[1, :rows]
    cos_out, sin_out = turns[0, pl.ds(first + step, 1)], turns[1, pl.ds(first + step, 1)]
    return cos_in * cos_out - sin_in * sin_out, sin_in * cos_out + cos_in * sin_out


def head_root(first, second):
    lane = lax.broadcasted_iota(jnp.int32, first.shape, 1)
    root = lax.rsqrt(head_means(first * first + second * second) + EPS)
    return jnp.where(lane < 3 * (HD // 2), root, 1.0), lane


class Lanes:
    def __init__(self, start, size):
        self.start, self.size = start, size


def down_parts(shape, width):
    rows, cols = shape
    whole = width // cols
    tall = (rows * cols) // width
    parts = [(i * tall, (i + 1) * tall, Lanes(0, cols), 0, i * cols) for i in range(whole)]
    left = rows - whole * tall
    room = width - whole * cols
    for j in range(cols // room if left else 0):
        parts.append((whole * tall, rows, Lanes(j * room, room), j * left, whole * cols))
    return parts


def pieces_kernel(at, gate_up, down, out):
    height, width = gate_up.shape[1:]
    out[:height] = gate_up[0]
    value = down[...]
    for a, b, lanes, at_row, at_lane in down_parts(value.shape, width):
        out[height + at_row : height + at_row + b - a, at_lane : at_lane + lanes.size] = value[
            a:b, lanes.start : lanes.start + lanes.size
        ]


def prepare_kernel(
    at, q, kv, out_w, up_gate_up, lower_down, up_q, up_kv, lower_out,
    rows_o, small_o, upper_o, low_o,
):
    k = at[0]
    value = kv[...].astype(F32)
    value = jnp.where(k == 0, value[:, :, :HD], value[:, :, HD:]).astype(BF16)
    value = jnp.concatenate([q[...], value[0], value[1]], axis=1)
    height = 4 * HD
    rows_o[:height] = nt(place_matrix(True), value).astype(BF16)
    rows_o[height:] = out_w[...]
    small_o[:2] = up_gate_up[0]
    small_o[2] = lower_down[0]
    table = up_kv[0].astype(F32)
    table = jnp.where(k == 0, table[:, :, :HD], table[:, :, HD:]).astype(BF16)
    zero = jnp.zeros_like(table[0])
    wide = jnp.zeros((RANK, 2 * HD), BF16)
    rows = [
        jnp.concatenate([up_q[0], wide], axis=1),
        jnp.concatenate([wide, table[0], zero], axis=1),
        jnp.concatenate([wide, zero, table[1]], axis=1),
    ] + [jnp.concatenate([wide, wide], axis=1)] * 5
    upper_o[...] = nt(place_matrix(True), jnp.concatenate(rows, axis=0)).astype(BF16)
    table = jnp.transpose(lower_out[0].astype(F32))
    low_o[...] = jnp.concatenate(
        [table, jnp.zeros((table.shape[0], 2 * HD - RANK), F32)], axis=1
    ).astype(BF16)


def project_kernel(
    at, own, oth, gain, dense, lower, upper, turns, gains,
    normal_o, narrow_o, q_o, kv_o, raw_o, weights,
):
    width = 4 * HD
    step = pl.program_id(0)
    steps = pl.num_programs(0)

    @pl.when(step == 0)
    def _():
        weights[:width] = dense[...]
        weights[width : width + 3 * RANK] = lower[0]
        weights[width + 3 * RANK :] = jnp.zeros(
            (weights.shape[0] - width - 3 * RANK, weights.shape[1]), BF16
        )

    value = jnp.where(step < steps // 2, own[...].astype(F32), oth[...].astype(F32))
    root = lax.rsqrt(jnp.mean(value * value, axis=1, keepdims=True) + EPS)
    normal = (value * root * gain[...]).astype(BF16)
    normal_o[...] = normal
    raw = nt(normal, weights[...])
    narrow = raw[:, width:].astype(BF16)
    narrow_o[...] = narrow[:, : 3 * RANK]
    raw = raw[:, :width] + ADAPTER_SCALING * nt(narrow, upper[...])
    raw_o[...] = raw
    first, second = raw[:, : 2 * HD], raw[:, 2 * HD :]
    root, _ = head_root(first, second)
    place = jnp.where(step < steps // 2, at[0] * (steps // 2) + step, (1 - at[0]) * (steps // 2) + step - steps // 2)
    cos, sin = rotation(place, turns, normal.shape[0], steps)
    first = first * root * gains[0:1]
    second = second * root * gains[1:2]
    turned = jnp.concatenate([first * cos - second * sin, second * cos + first * sin], axis=1)
    out = nn(turned.astype(BF16), place_matrix(True)).astype(BF16)
    q_o[...] = out[:, : 2 * HD]
    kv_o[...] = out[:, 2 * HD :]


def project_back_kernel(
    at, dq, dkv, dkv_after, raw, turns, gains, narrow, normal, upper,
    out, wide_o, heads_o, wide, heads,
):
    step = pl.program_id(0)

    @pl.when(step == 0)
    def _():
        wide[...] = jnp.zeros_like(wide)
        heads[...] = jnp.zeros_like(heads)

    cos, sin = rotation(2 * step, turns, dq.shape[0], 2 * pl.num_programs(0))
    grad_kv = (dkv[...] + dkv_after[...].astype(F32)).astype(BF16)
    grad = nn(jnp.concatenate([dq[...].astype(BF16), grad_kv], axis=1), place_matrix(False))
    first, second = raw[:, : 2 * HD], raw[:, 2 * HD :]
    root, lane = head_root(first, second)
    first, second = first * root, second * root
    back_first = grad[:, : 2 * HD] * cos + grad[:, 2 * HD :] * sin
    back_second = grad[:, 2 * HD :] * cos - grad[:, : 2 * HD] * sin
    back_first = back_first * gains[0:1]
    back_second = back_second * gains[1:2]
    mean = head_means(back_first * first + back_second * second)
    mean = jnp.where(lane < 3 * (HD // 2), mean, 0.0)
    back_first = (root * (back_first - first * mean)).astype(BF16)
    back_second = (root * (back_second - second * mean)).astype(BF16)
    grad = jnp.concatenate([back_first, back_second], axis=1)
    out[...] = grad
    inside = (ADAPTER_SCALING * nn(grad, upper[...])).astype(BF16)
    wide[...] += tn(inside[:, : 3 * RANK], normal[...])
    heads[...] += tn(narrow[...], grad)

    @pl.when(step == pl.num_programs(0) - 1)
    def _():
        wide_o[...] = wide[...].astype(BF16)
        total = (heads[...] * ADAPTER_SCALING).astype(BF16)
        total = nn(total, place_matrix(True))
        total = jnp.concatenate(
            [
                total[:RANK, : 2 * HD],
                total[RANK : 2 * RANK, 2 * HD : 3 * HD],
                total[2 * RANK :, 3 * HD :],
            ],
            axis=1,
        )
        zero = jnp.zeros_like(total)
        heads_o[:, : 4 * HD] = jnp.where(at[0] == 0, total, zero).astype(BF16)
        heads_o[:, 4 * HD :] = jnp.where(at[0] == 0, zero, total).astype(BF16)


def head_blocks(value, which):
    return jnp.concatenate([value[which * 4 + place] for place in range(4)], axis=1)


def mix_kernel(at, mixed, out_own, out_oth, upper, tokens, gain, hidden_o, normal_o, narrow_o):
    k = at[0]
    width = tokens.shape[2]
    total = nn(head_blocks(mixed, k), out_own[...]) + nn(head_blocks(mixed, 1 - k), out_oth[...])
    narrow = total[:, width : width + RANK].astype(BF16)
    narrow_o[...] = narrow
    total = tokens[0].astype(F32) + total[:, :width] + ADAPTER_SCALING * nn(narrow, upper[0])
    hidden_o[...] = total
    root = lax.rsqrt(jnp.mean(total * total, axis=1, keepdims=True) + EPS)
    normal_o[...] = (total * root * gain[...]).astype(BF16)


def norm_back(value, grad, gain):
    root = lax.rsqrt(jnp.mean(value * value, axis=1, keepdims=True) + EPS)
    unit = value * root
    grad = grad * gain
    return root * (grad - unit * jnp.mean(grad * unit, axis=1, keepdims=True))


def mix_back_kernel(
    at, hidden, cotangent, own, arrived, far, gain, out_own, out_oth, upper,
    grad_o, low_o, mixed_o, narrow_o,
):
    k = at[0]
    rows = hidden.shape[0]
    grad = own[:rows].astype(F32) + arrived[:rows].astype(F32) + far[...].astype(F32)
    grad = cotangent[0].astype(F32) + norm_back(hidden[...], grad, gain[...])
    grad_o[...] = grad
    low = grad.astype(BF16)
    low_o[...] = low
    table = jnp.transpose(upper[0].astype(F32))
    table = jnp.concatenate([table, jnp.zeros((table.shape[0], 2 * HD - RANK), F32)], axis=1)
    narrow = (ADAPTER_SCALING * nn(low, table.astype(BF16))).astype(BF16)
    narrow_o[...] = narrow[:, :RANK]
    low = jnp.concatenate([low, narrow], axis=1)
    for which, source in ((k, out_own), (1 - k, out_oth)):
        value = nt(low, source[...]).astype(BF16)
        for place in range(4):
            mixed_o[which * 4 + place] = value[:, place * 2 * HD : (place + 1) * 2 * HD]


def mix_grads_kernel(at, mixed, low, narrow, narrow_back, out_o):
    out_o[:RANK] = (ADAPTER_SCALING * tn(narrow[...], low[...])).astype(BF16)
    for i in range(8):
        value = tn(narrow_back[...], mixed[i])
        out_o[RANK:, i * 2 * HD : (i + 1) * 2 * HD] = value.astype(BF16)


def last_kernel(at, grads, own, own_x, oth, oth_x, lower, hidden, tokens, gain, out):
    k, x = at[0], at[1]
    width = hidden.shape[1]
    total = 0.0
    for which, side, source in ((k, x, own), (k, 1 - x, own_x), (1 - k, x, oth), (1 - k, 1 - x, oth_x)):
        lanes = pl.ds(pl.multiple_of(side * 2 * HD, 2 * HD), 2 * HD)
        value = [grads[which * 4 + place, :, lanes] for place in range(4)]
        total += nn(jnp.concatenate(value, axis=1), source[...])
    narrow = (ADAPTER_SCALING * total[:, width : width + 3 * RANK]).astype(BF16)
    total = total[:, :width] + nn(narrow, lower[0])
    value = tokens[0].astype(F32)
    out[...] = (hidden[...] + norm_back(value, total, gain[...])).astype(BF16)


def weight_copies(at, sources, dst, sem, down):
    k, x, y = at[0], at[1], at[2]

    def lanes(start, size):
        return pl.ds(pl.multiple_of(start, 2 * HD), size)

    def rows(start, size):
        return pl.ds(pl.multiple_of(start, 16), size)

    if down:
        height, width = dst.shape[0], sources[0].shape[1]
    else:
        height, width = sources[0].shape[1:]
    if len(sources) == 1:
        if down:
            pairs = [(sources[0], dst.at[:, pl.ds(0, width)])]
        else:
            pairs = [
                (sources[0].at[m], dst.at[pl.ds(0, height), pl.ds(m * width, width)])
                for m in range(2)
            ]
        return [
            (None, [pltpu.make_async_copy(a, b, sem.at[i]) for i, (a, b) in enumerate(pairs)])
        ]
    local, mine, *pieces = sources
    zero, one = [], []
    if down:
        part = height // 2
        for j, source in enumerate((local, mine)):
            zero.append((source, dst.at[:, lanes((y + j) % 2 * width, width)]))
        tall = pieces[0].shape[0] - part * width // pieces[0].shape[1]
        for j, source in enumerate(pieces):
            for a, b, cols, at_row, at_lane in down_parts((part, width), source.shape[1]):
                one.append(
                    (
                        source.at[pl.ds(tall + at_row, b - a), pl.ds(at_lane, cols.size)],
                        dst.at[
                            rows((x + j) % 2 * part + a, b - a),
                            lanes((y + j // 2) % 2 * width + cols.start, cols.size),
                        ],
                    )
                )
    else:
        for j, source in enumerate((local, mine)):
            for m in range(2):
                at_row = rows((y + j) % 2 * height, height)
                zero.append((source.at[m], dst.at[at_row, pl.ds(m * width, width)]))
        for j, source in enumerate(pieces):
            at_row = rows((y + j // 2) % 2 * height, height)
            source = source.at[pl.ds(0, height)]
            one.append((source, dst.at[at_row, lanes((x + j) % 2 * width, width)]))
    return [
        (when, [pltpu.make_async_copy(a, b, sem.at[i]) for i, (a, b) in enumerate(pairs)])
        for when, pairs in ((k == 0, zero), (k == 1, one))
    ]


def for_copies(groups, what):
    for when, copies in groups:
        if when is None:
            for copy in copies:
                what(copy)
        else:

            @pl.when(when)
            def _():
                for copy in copies:
                    what(copy)


def put_down_lower(down, small):
    width = 2 * HD
    table = jnp.transpose(small[2].astype(F32))
    table = jnp.concatenate(
        [table, jnp.zeros((table.shape[0], width - table.shape[1]), F32)], axis=1
    )
    down[:, down.shape[1] - width :] = table.astype(BF16)


def both_tokens(step, own, far, own_oth, far_oth):
    here = jnp.concatenate([own[...], far[...]], axis=0).astype(F32)
    there = jnp.concatenate([own_oth[...], far_oth[...]], axis=0).astype(F32)
    return jnp.where(step == 0, here, there).astype(BF16)


def wide_table(table):
    table = jnp.transpose(table.astype(F32))
    return jnp.concatenate(
        [table, jnp.zeros((table.shape[0], 2 * HD - table.shape[1]), F32)], axis=1
    ).astype(BF16)


def ffn_kernel(many, at, own, far, own_oth, far_oth, cot, cot_far, cot_oth, cot_far_oth, *rest):
    lower, small, upper = rest[:3]
    sources, down_sources = rest[3 : 3 + many], rest[3 + many : 3 + 2 * many]
    part_own, part_oth, act_o, grad_o, narrow_o, back_o, weights, down, tables, sem = rest[
        3 + 2 * many :
    ]
    step = pl.program_id(0)
    units = small.shape[2]
    first = weight_copies(at, sources, weights, sem.at[0], False)
    second = weight_copies(at, down_sources, down, sem.at[1], True)

    @pl.when(step == 0)
    def _():
        for_copies(second, lambda copy: copy.start())
        for_copies(first, lambda copy: copy.start())
        put_down_lower(down, small)
        tables[0] = wide_table(lower[0][3 * RANK :])
        tables[1] = wide_table(upper[0])
        for_copies(second, lambda copy: copy.wait())

    value = both_tokens(step, own, far, own_oth, far_oth)
    grad = both_tokens(step, cot.at[0], cot_far.at[0], cot_oth, cot_far_oth)
    narrow_o[0] = nn(value, tables[0]).astype(BF16)[:, : 2 * RANK]
    narrow = (ADAPTER_SCALING * nn(grad, tables[1])).astype(BF16)
    back_o[0] = narrow[:, :RANK]
    grad = jnp.concatenate([grad, narrow], axis=1)
    grad_act = nt(grad, down[...])

    @pl.when(step == 0)
    def _():
        for_copies(first, lambda copy: copy.wait())
        for i in range(2):
            term = lower[0][(3 + i) * RANK : (4 + i) * RANK]
            at_lanes = slice(i * units, (i + 1) * units)
            merged = weights[:, at_lanes].astype(F32) + ADAPTER_SCALING * tn(term, small[i])
            weights[:, at_lanes] = merged.astype(BF16)

    both = nn(value, weights[...])
    gate, up = both[:, :units], both[:, units:]
    sig = 0.5 * jnp.tanh(0.5 * gate) + 0.5
    silu = gate * sig
    act_o[0] = (silu * up).astype(BF16)
    grad_gate = (grad_act * up * (sig + silu * (1.0 - sig))).astype(BF16)
    grad_up = (grad_act * silu).astype(BF16)
    grad_both = jnp.concatenate([grad_gate, grad_up], axis=1)
    grad_o[0] = grad_both
    part = nt(grad_both, weights[...]).astype(BF16)

    @pl.when(step == 0)
    def _():
        part_own[...] = part

    @pl.when(step == 1)
    def _():
        part_oth[...] = part


def ffn_down_kernel(many, at, act, small, upper, *rest):
    sources = rest[:many]
    part_own, part_oth, zd_o, down, sem = rest[many:]
    step = pl.program_id(0)
    width = upper.shape[2]
    copies = weight_copies(at, sources, down, sem.at[0], True)

    @pl.when(step == 0)
    def _():
        for_copies(copies, lambda copy: copy.start())
        put_down_lower(down, small)
        for_copies(copies, lambda copy: copy.wait())

    part = nn(act[0], down[...])
    zd = part[:, width : width + RANK].astype(BF16)
    zd_o[0] = zd
    part = (part[:, :width] + ADAPTER_SCALING * nn(zd, upper[0])).astype(BF16)

    @pl.when(step == 0)
    def _():
        part_own[...] = part

    @pl.when(step == 1)
    def _():
        part_oth[...] = part


def ffn_grads_kernel(at, own, far, own_oth, far_oth, cot, cot_far, cot_oth, cot_far_oth, *rest):
    act, grads, narrow, narrow_back, zd, small, wide_o, quarter_o, lanes, wide, quarter = rest
    step = pl.program_id(0)
    units = small.shape[2]

    @pl.when(step == 0)
    def _():
        wide[...] = jnp.zeros_like(wide)
        quarter[...] = jnp.zeros_like(quarter)
        lanes[...] = jnp.zeros_like(lanes)
        for i in range(2):
            table = jnp.transpose(small[i].astype(F32))
            zero = jnp.zeros_like(table)
            table = jnp.concatenate([table, zero] if i == 0 else [zero, table], axis=1)
            lanes[i * units : (i + 1) * units, : 2 * RANK] = table.astype(BF16)

    value = both_tokens(step, own, far, own_oth, far_oth)
    grad = both_tokens(step, cot.at[0], cot_far.at[0], cot_oth, cot_far_oth)
    inner = (ADAPTER_SCALING * nn(grads[0], lanes[...])).astype(BF16)[:, : 2 * RANK]
    wide[:RANK] += ADAPTER_SCALING * tn(zd[0], grad)
    wide[RANK:] += tn(inner, value)
    both = tn(narrow[0], grads[0])
    quarter[:RANK] += ADAPTER_SCALING * both[:RANK, :units]
    quarter[RANK : 2 * RANK] += ADAPTER_SCALING * both[RANK:, units:]
    quarter[2 * RANK :] += tn(narrow_back[0], act[0])

    @pl.when(step == 1)
    def _():
        wide_o[...] = wide[...].astype(BF16)
        quarter_o[...] = quarter[...].astype(BF16)


def ring_kernel(at, *rest):
    out = rest[4]
    for d in range(4):

        @pl.when((at[4] + 4 - pl.program_id(0)) % 4 == d)
        def _():
            out[0] = rest[d][...].astype(out.dtype)


def assemble_kernel(at, own, *rest):
    z = at[4]
    up, down, out = rest[:3], rest[3:6], rest[6]
    place = pl.program_id(0)

    @pl.when(place == z)
    def _():
        out[0] = own[...].astype(out.dtype)

    for d in range(3):

        @pl.when(z - place == d + 1)
        def _():
            out[0] = up[d][...].astype(out.dtype)

        @pl.when(place - z == d + 1)
        def _():
            out[0] = down[d][...].astype(out.dtype)


def plus(here, there):
    return (here.astype(F32) + there.astype(F32)).astype(BF16)


def tie(*values):
    return lax.optimization_barrier(values)


def tie_all(values):
    return lax.optimization_barrier(values)


def heads_tokens(value):
    return lax.all_to_all(value, CT, 0, 0, axis_index_groups=COLUMN, tiled=True)


UP = [(i, i + 1) for i in range(3)]
RING = [(i, (i + 1) % 4) for i in range(4)]
DOWN = [(i + 1, i) for i in range(3)]


def body(
    shards,
    inputs,
    cotangent,
    segments,
    adapter_index,
    query_weight,
    key_value_weight,
    output_weight,
    gate_up_weight,
    down_weight,
    norm_attn,
    norm_ffn,
    q_gain,
    k_gain,
    input_adapter_lower,
    query_adapter_upper,
    key_value_adapter_upper,
    gate_up_adapter_upper,
    output_adapter_lower,
    output_adapter_upper,
    down_adapter_lower,
    down_adapter_upper,
):
    ctx = lax.axis_index("ctx")
    x, k = ctx // 2, ctx % 2
    z = lax.axis_index("tp")
    y = lax.axis_index("shard")
    tok = inputs.shape[1]
    half = 2 * tok
    sub = tok // 4
    width = inputs.shape[2]
    hidden_units = gate_up_weight.shape[2]
    slot = adapter_index[0]
    segment = segments[0]
    pair = shards == 2
    swap_y = [(0, 1), (1, 0)]
    cols = 2 * HD
    at = jnp.stack([k, x, y, slot, z]).astype(jnp.int32)
    K, X, Y, SLOT, Z = range(5)

    def shard_rows(piece, axis):
        if pair:
            return order2(piece, lax.ppermute(piece, "shard", swap_y), y, axis)
        return lax.all_gather(piece, "shard", axis=axis, tiled=True)

    def over_y(cores):
        return [
            ((s * 4 + c) * 4 + t, ((s ^ 1) * 4 + c) * 4 + t)
            for s in range(2)
            for c in cores
            for t in range(4)
        ]

    tokens_other = lax.ppermute(inputs[0], "ctx", CORE)
    by_slot = lambda i, s: (s[SLOT], 0, 0)
    prepared = run(
        prepare_kernel,
        "prepare",
        (1,),
        at,
        [
            (query_weight, (query_weight.shape[0], cols), lambda i, s: (0, s[K])),
            whole(key_value_weight),
            (output_weight, (cols, output_weight.shape[1]), lambda i, s: (s[K], 0)),
            (gate_up_adapter_upper, (1, 2, RANK, hidden_units), lambda i, s: (s[SLOT], 0, 0, 0)),
            (jnp.swapaxes(down_adapter_lower, 1, 2), (1, RANK, hidden_units), by_slot),
            (query_adapter_upper, (1, RANK, cols), lambda i, s: (s[SLOT], 0, s[K])),
            (key_value_adapter_upper, (1, 2, RANK, cols), lambda i, s: (s[SLOT], 0, 0, 0)),
            (
                jnp.swapaxes(output_adapter_lower, 1, 2),
                (1, RANK, cols),
                lambda i, s: (s[SLOT], 0, s[K]),
            ),
        ],
        [
            out_whole((3 * cols, query_weight.shape[0]), BF16),
            out_whole((3, RANK, hidden_units), BF16),
            out_whole((2 * cols, cols), BF16),
            out_whole((cols, cols), BF16),
        ],
    )
    piece_rows, small_ffn, upper_qkv, low_rows = prepared
    dense_rows = shard_rows(piece_rows, 1)
    dense_qkv, rows_here = dense_rows[: 2 * cols], dense_rows[2 * cols :]

    far_z = [(c * 4 + t, c * 4 + (t ^ 2)) for c in (1, 3) for t in range(4)]
    far_x = [(1, 3), (3, 1)]
    if pair:
        (piece,) = run(
            pieces_kernel,
            "pieces",
            (1,),
            at,
            [
                (gate_up_weight, (1,) + gate_up_weight.shape[1:], lambda i, s: (s[X], 0, 0)),
                (down_weight, (hidden_units // 2, down_weight.shape[1]), lambda i, s: (s[X], 0)),
            ],
            [
                out_whole(
                    (
                        gate_up_weight.shape[1] + down_weight.shape[1] // 2,
                        hidden_units,
                    ),
                    BF16,
                )
            ],
        )
        piece = lax.ppermute(piece, CT, far_z)

    block = tok // 4
    blocks = half // block
    half_dim = HD // 2
    first_query = x * half
    inverse = THETA ** (-(jnp.arange(half_dim, dtype=F32) * 2.0 / HD))
    inverse = jnp.concatenate([inverse] * 3 + [jnp.zeros_like(inverse)])
    places = jnp.arange(2 * block + blocks, dtype=jnp.int32)
    places = jnp.where(places < 2 * block, places, first_query + block * (places - 2 * block))
    angles = places.astype(F32)[:, None] * inverse[None, :]
    turns = jnp.stack([jnp.cos(angles), jnp.sin(angles)])

    by_row = lambda i, s: (i, 0)
    by_step = lambda i, s: (i, 0, 0)
    lower_table = jnp.swapaxes(input_adapter_lower, 1, 2)
    lower_spec = (lower_table, (1, 5 * RANK, width), by_slot)
    ones = jnp.ones((half_dim,), F32)
    gains = jnp.stack(
        [
            jnp.concatenate([q_gain[part], q_gain[part], k_gain[part], ones])
            for part in (slice(0, half_dim), slice(half_dim, HD))
        ]
    )
    gain_attn, gain_ffn = norm_attn[None], norm_ffn[None]
    own_row = lambda i, s: (jnp.minimum(i, 3), 0)
    oth_row = lambda i, s: (jnp.maximum(i - 4, 0), 0)
    chip_row = lambda i, s: (jnp.where(i < 4, s[K] * 4 + i, (1 - s[K]) * 4 + i - 4), 0)
    normalized, narrow, queries, keyvals, raw = run(
        project_kernel,
        "project",
        (8,),
        at,
        [
            (inputs[0], (block, width), own_row),
            (tokens_other, (block, width), oth_row),
            whole(gain_attn),
            (dense_rows, (2 * cols, width), fixed(0, 0)),
            (lower_table, (1, 3 * RANK, width), by_slot),
            whole(upper_qkv),
            whole(turns),
            whole(gains),
        ],
        [
            ((half, width), BF16, (block, width), chip_row),
            ((half, 3 * RANK), BF16, (block, 3 * RANK), chip_row),
            ((half, cols), BF16, (block, cols), chip_row),
            ((half, cols), BF16, (block, cols), chip_row),
            ((half, 2 * cols), F32, (block, 2 * cols), chip_row),
        ],
        [pltpu.VMEM((3 * cols, width), BF16)],
    )
    keyvals_before = lax.ppermute(keyvals, "ctx", [(0, 2), (1, 3)])

    size = half // 4
    seg_rows = segment.reshape(-1, 1, size)
    keyvals, small_from = tie(keyvals, small_ffn)
    small_far = lax.ppermute(small_from, "tp", Z_XOR[2])
    if pair:
        keyvals, gate_up_from = tie(keyvals, gate_up_weight)
        mine_g = lax.ppermute(gate_up_from, SCT, over_y((0, 2)))
    acc = attention_forward(queries, keyvals, seg_rows, segment, at, 0, size, size)
    acc, cot_here, out_rows = tie(acc, cotangent[0], jnp.concatenate([rows_here, low_rows], axis=1))
    out_own = lax.all_gather(out_rows, "tp", axis=0, tiled=True)
    cot_oth = lax.ppermute(cot_here, "ctx", CORE)
    mixed, mixed_low, lse = attention_forward(
        queries, keyvals_before, seg_rows, segment, at, half, size, 2 * size, acc
    )
    mixed_low, small_far = tie(mixed_low, small_far)
    small_ffn = jnp.where(k == 0, small_ffn, small_far)
    if pair:
        mixed_low, piece, down_from = tie(mixed_low, piece, down_weight)
        piece_x = lax.ppermute(piece, "ctx", far_x)
        piece_y = lax.ppermute(piece, SCT, over_y((1, 3)))
        mine_d = lax.ppermute(down_from, SCT, over_y((0, 2)))

    mixed_all = heads_tokens(mixed_low.reshape(8, sub, cols))
    qkv_rows = rows_at(jnp.concatenate([dense_qkv, upper_qkv], axis=1), x, cols)
    mixed_all, small_ffn, cot_oth, qkv_rows = tie(mixed_all, small_ffn, cot_oth, qkv_rows)
    out_oth = lax.ppermute(out_own, "ctx", CORE)
    if pair:
        mixed_all, mine_g, piece_x, piece_y, out_own = tie(
            mixed_all, mine_g, piece_x, piece_y, out_own
        )
        piece_xy = lax.ppermute(piece_y, "ctx", far_x)
        pieces = [piece, piece_x, piece_y, piece_xy]
        sources = [gate_up_weight, mine_g] + pieces
        down_sources = [down_weight, mine_d] + pieces
    else:
        full_g = lax.all_gather(gate_up_weight, "shard", axis=1, tiled=True)
        full_d = lax.all_gather(down_weight, "shard", axis=1, tiled=True)
        sources = [jnp.where(k == 0, full_g, lax.ppermute(full_g, "tp", Z_XOR[2]))]
        down_sources = [jnp.where(k == 0, full_d, lax.ppermute(full_d, "tp", Z_XOR[2]))]
    z_block = lambda i, s: (0, s[Z], 0)
    upper_out_spec = (output_adapter_upper, (1, RANK, width), lambda i, s: (s[SLOT], 0, 0))
    hidden_state, normalized_second, narrow_out = run(
        mix_kernel,
        "mix",
        (1,),
        at,
        [
            whole(mixed_all),
            whole(out_own),
            whole(out_oth),
            upper_out_spec,
            (inputs, (1, sub, width), z_block),
            whole(gain_ffn),
        ],
        [
            out_whole((sub, width), F32),
            out_whole((sub, width), BF16),
            out_whole((sub, RANK), BF16),
        ],
    )

    second = normalized_second
    second_oth = lax.ppermute(second, "ctx", CORE)
    second_far = lax.ppermute(second, "tp", Z_XOR[1])
    second_far_oth = lax.ppermute(second_far, "ctx", CORE)
    upper_down_spec = (down_adapter_upper, (1, RANK, width), by_slot)
    z_far = lambda i, s: (0, s[Z] ^ 1, 0)
    ffn_tokens = [
        whole(second),
        whole(second_far),
        whole(second_oth),
        whole(second_far_oth),
        (cotangent, (1, sub, width), z_block),
        (cotangent, (1, sub, width), z_far),
        (cot_oth, (sub, width), lambda i, s: (s[Z], 0)),
        (cot_oth, (sub, width), lambda i, s: (s[Z] ^ 1, 0)),
    ]
    tall = 2 * sub
    qkv_rows, second_far_oth = tie(qkv_rows, second_far_oth)
    qkv_own = lax.all_gather(qkv_rows, "tp", axis=0, tiled=True)
    ffn_tokens[3] = whole(second_far_oth)
    part_own, part_oth, active, grad_both, narrow_second, narrow_back_second = run(
        functools.partial(ffn_kernel, len(sources)),
        "ffn",
        (2,),
        at,
        ffn_tokens
        + [lower_spec, whole(small_ffn), upper_down_spec]
        + [(source, None, None) for source in sources + down_sources],
        [
            out_whole((tall, width), BF16),
            out_whole((tall, width), BF16),
            ((2, tall, hidden_units), BF16, (1, tall, hidden_units), by_step),
            ((2, tall, 2 * hidden_units), BF16, (1, tall, 2 * hidden_units), by_step),
            ((2, tall, 2 * RANK), BF16, (1, tall, 2 * RANK), by_step),
            ((2, tall, RANK), BF16, (1, tall, RANK), by_step),
        ],
        [
            pltpu.VMEM((width, 2 * hidden_units), BF16),
            pltpu.VMEM((hidden_units, width + cols), BF16),
            pltpu.VMEM((2, width, cols), BF16),
            pltpu.SemaphoreType.DMA((2, 24)),
        ],
        LONG,
    )
    part_arrived = lax.ppermute(part_oth, "ctx", CORE)
    part_give = (part_own[sub:].astype(F32) + part_arrived[sub:].astype(F32)).astype(BF16)
    part_give, active, qkv_own = tie(part_give, active, qkv_own)
    part_far = lax.ppermute(part_give, "tp", Z_XOR[1])
    qkv_own_x = lax.ppermute(qkv_own, "ctx", XSIDE)

    down_own, down_oth, zd = run(
        functools.partial(ffn_down_kernel, len(sources)),
        "ffn_down",
        (2,),
        at,
        [
            (active, (1, tall, hidden_units), by_step),
            whole(small_ffn),
            upper_down_spec,
        ]
        + [(source, None, None) for source in down_sources],
        [
            out_whole((tall, width), BF16),
            out_whole((tall, width), BF16),
            ((2, tall, RANK), BF16, (1, tall, RANK), by_step),
        ],
        [pltpu.VMEM((hidden_units, width + cols), BF16), pltpu.SemaphoreType.DMA((1, 24))],
        LONG,
    )
    hidden_back, down_own, down_oth, zd = tie(hidden_state, down_own, down_oth, zd)

    grad_hidden, grad_hidden_low, grad_mixed_all, narrow_back = run(
        mix_back_kernel,
        "mix_back",
        (1,),
        at,
        [
            whole(hidden_back),
            (cotangent, (1, sub, width), z_block),
            whole(part_own),
            whole(part_arrived),
            whole(part_far),
            whole(gain_ffn),
            whole(out_own),
            whole(out_oth),
            upper_out_spec,
        ],
        [
            out_whole((sub, width), F32),
            out_whole((sub, width), BF16),
            out_whole((8, sub, cols), BF16),
            out_whole((sub, RANK), BF16),
        ],
    )
    grad_mixed_all, grad_both, down_oth = tie(grad_mixed_all, grad_both, down_oth)
    grad_mixed = heads_tokens(grad_mixed_all).reshape(half, cols)
    down_arrived = lax.ppermute(down_oth, "ctx", CORE)
    down_give = (down_own[sub:].astype(F32) + down_arrived[sub:].astype(F32)).astype(BF16)
    down_far = lax.ppermute(down_give, "tp", Z_XOR[1])
    final = hidden_state + (
        down_own[:sub].astype(F32) + down_arrived[:sub].astype(F32) + down_far.astype(F32)
    )
    final = final.astype(BF16)
    wide_ffn, quarter_grads = run(
        ffn_grads_kernel,
        "ffn_grads",
        (2,),
        at,
        ffn_tokens
        + [
            (active, (1, tall, hidden_units), by_step),
            (grad_both, (1, tall, 2 * hidden_units), by_step),
            (narrow_second, (1, tall, 2 * RANK), by_step),
            (narrow_back_second, (1, tall, RANK), by_step),
            (zd, (1, tall, RANK), by_step),
            whole(small_ffn),
        ],
        [out_whole((3 * RANK, width), BF16), out_whole((3 * RANK, hidden_units), BF16)],
        [
            pltpu.VMEM((2 * hidden_units, cols), BF16),
            pltpu.VMEM((3 * RANK, width), F32),
            pltpu.VMEM((3 * RANK, hidden_units), F32),
        ],
        LONG,
    )
    (wide_mix,) = run(
        mix_grads_kernel,
        "mix_grads",
        (1,),
        at,
        [whole(mixed_all), whole(grad_hidden_low), whole(narrow_out), whole(narrow_back)],
        [out_whole((2 * RANK, width), BF16)],
    )
    wide_early = jnp.concatenate([wide_mix, wide_ffn], axis=0)
    grad_mixed, wide_early, qkv_own_x = tie(grad_mixed, wide_early, qkv_own_x)
    wide_near = lax.ppermute(wide_early, "tp", Z_XOR[1])
    if pair:
        slot_other = lax.ppermute(adapter_index, "shard", swap_y)[0]

    dq_before, dkv_before = attention_backward(
        queries,
        keyvals_before,
        seg_rows,
        grad_mixed,
        mixed,
        lse,
        segment,
        at,
        half,
        size,
        size,
    )
    dkv_after = lax.ppermute(dkv_before, "ctx", [(2, 0), (3, 1)])
    dq_before, wide_near, quarter_grads, qkv_own, qkv_own_x, final = tie(
        dq_before, wide_near, quarter_grads, qkv_own, qkv_own_x, final
    )
    out_up_1 = lax.ppermute(final, "tp", UP)
    out_down_1 = lax.ppermute(final, "tp", DOWN)
    if pair:
        dq_before, slot_other = tie(dq_before, slot_other)
    qkv_oth = lax.ppermute(qkv_own, "ctx", CORE)
    qkv_oth_x = lax.ppermute(qkv_own_x, "ctx", CORE)
    wide_early = plus(wide_early, wide_near)
    early = jnp.concatenate(
        [jnp.pad(wide_early, ((0, 0), (0, hidden_units - width))), quarter_grads], axis=0
    )
    early_far = lax.ppermute(early, "tp", Z_XOR[2])
    dq, dkv = attention_backward(
        queries,
        keyvals,
        seg_rows,
        grad_mixed,
        mixed,
        lse,
        segment,
        at,
        0,
        size,
        size,
        dq_before,
    )
    dq, early_far, out_up_1, out_down_1 = tie(dq, early_far, out_up_1, out_down_1)
    out_up_2 = lax.ppermute(out_up_1, "tp", UP[1:])
    out_down_2 = lax.ppermute(out_down_1, "tp", DOWN[:2])
    early = jnp.concatenate(
        [
            plus(early[: 5 * RANK], early_far[: 5 * RANK]),
            jnp.where(k == 0, early[5 * RANK :], early_far[5 * RANK :]),
        ],
        axis=0,
    )
    tall_blocks = blocks // 2
    d_projected, wide_attn, head_grads = run(
        project_back_kernel,
        "project_back",
        (tall_blocks,),
        at,
        [
            (dq, (2 * block, cols), by_row),
            (dkv, (2 * block, cols), by_row),
            (dkv_after, (2 * block, cols), by_row),
            (raw, (2 * block, 2 * cols), by_row),
            whole(turns),
            whole(gains),
            (narrow, (2 * block, 3 * RANK), by_row),
            (normalized, (2 * block, width), by_row),
            whole(upper_qkv),
        ],
        [
            ((half, 2 * cols), BF16, (2 * block, 2 * cols), by_row),
            out_whole((3 * RANK, width), BF16),
            out_whole((RANK, 4 * cols), BF16),
        ],
        [pltpu.VMEM((3 * RANK, width), F32), pltpu.VMEM((3 * RANK, 2 * cols), F32)],
        LONG,
    )
    d_projected, out_up_2, out_down_2 = tie(d_projected, out_up_2, out_down_2)
    out_3 = lax.ppermute(jnp.where(z == 2, out_up_2, out_down_2), "tp", UP[2:] + DOWN[:1])
    out_up_3 = out_down_3 = out_3

    d_all = heads_tokens(d_projected.reshape(8, sub, 2 * cols))
    def lanes_to(value, size):
        return jnp.pad(value, ((0, 0), (0, size - value.shape[1])))

    packed = jnp.concatenate(
        [early, lanes_to(wide_attn, hidden_units), lanes_to(head_grads, hidden_units)], axis=0
    )

    packed = plus(packed, lax.ppermute(packed, "ctx", CORE))
    packed = plus(packed, lax.ppermute(packed, "ctx", XSIDE))
    slots = jnp.arange(ADAPT, dtype=jnp.int32)

    def placed(value, which):
        mask = (slots == which).astype(F32).reshape((ADAPT,) + (1,) * value.ndim)
        return mask * value.astype(F32)[None]

    if pair:
        both = jnp.stack([packed, lax.ppermute(packed, "shard", swap_y)])
    else:
        both = lax.psum(placed(packed, slot), "shard")
    (grad_tokens,) = run(
        last_kernel,
        "last",
        (1,),
        at,
        [
            whole(d_all),
            whole(qkv_own),
            whole(qkv_own_x),
            whole(qkv_oth),
            whole(qkv_oth_x),
            (lower_table, (1, 3 * RANK, width), by_slot),
            whole(grad_hidden),
            (inputs, (1, sub, width), z_block),
            whole(gain_attn),
        ],
        [out_whole((sub, width), BF16)],
    )
    up_1 = lax.ppermute(grad_tokens, "tp", RING)
    own_width = width // (shards * 4)
    in_attn = rows_at(both[:, 8 * RANK : 11 * RANK, :width], y * 4 + ctx, own_width, 2)
    in_attn = plus(in_attn, lax.ppermute(in_attn, "tp", Z_XOR[1]))
    up_1, in_attn, both = tie(up_1, in_attn, both)
    up_2 = lax.ppermute(up_1, "tp", RING)
    in_far = lax.ppermute(in_attn, "tp", Z_XOR[2])
    wide = both[:, : 5 * RANK, :width]
    in_ffn = rows_at(wide[:, 3 * RANK :], y * 4 + ctx, own_width, 2)
    rest = jnp.concatenate([both[:, 5 * RANK : 8 * RANK], both[:, 11 * RANK :]], axis=1)
    if pair:
        slots_here = (slot, slot_other)
        rest = sum(placed(rest[i], which) for i, which in enumerate(slots_here))
    quarter_sum, heads = rest[:, : 3 * RANK], rest[:, 3 * RANK :, : 4 * cols]
    grad_b_query = jnp.concatenate([heads[..., :cols], heads[..., 2 * cols : 3 * cols]], axis=-1)
    grad_b_keyval = jnp.stack(
        [
            jnp.concatenate(
                [heads[..., core * 2 * cols + c * HD :][..., :HD] for core in range(2)], axis=-1
            )
            for c in (2, 3)
        ],
        axis=1,
    )
    grad_b_gate_up = quarter_sum[:, : 2 * RANK].reshape(ADAPT, 2, RANK, -1)
    grad_a_down = jnp.swapaxes(quarter_sum[:, 2 * RANK :], 1, 2)
    in_all = jnp.concatenate([plus(in_attn, in_far), in_ffn], axis=1)
    if pair:
        wide = sum(placed(wide[i, : 3 * RANK], which) for i, which in enumerate(slots_here))
        in_all = sum(placed(in_all[i], which) for i, which in enumerate(slots_here))
    else:
        wide, in_all = wide.astype(F32), in_all.astype(F32)
    grad_b_out = wide[:, :RANK]
    grad_a_out = wide[:, RANK : 2 * RANK]
    grad_b_down = wide[:, 2 * RANK : 3 * RANK]
    grad_a_out = jnp.concatenate(
        [rows_at(grad_a_out, z, cols, 2), rows_at(grad_a_out, 4 + z, cols, 2)], axis=2
    )
    grad_a_out = jnp.swapaxes(grad_a_out, 1, 2)
    grad_adapt_in = jnp.swapaxes(in_all, 1, 2)
    up_2, final, grad_b_query, grad_b_keyval, grad_b_gate_up, grad_a_down = tie(
        up_2, final, grad_b_query, grad_b_keyval, grad_b_gate_up, grad_a_down
    )
    up_3 = lax.ppermute(up_2, "tp", RING)
    line = [grad_tokens, up_1, up_2, up_3]
    z_row = lambda i, s: (0, i, 0)
    (grad_inputs,) = run(
        ring_kernel,
        "assemble",
        (4,),
        at,
        [whole(part) for part in line],
        [((1, tok, width), F32, (1, sub, width), z_row)],
    )
    line = [final, out_up_1, out_up_2, out_up_3, out_down_1, out_down_2, out_down_3]
    (result,) = run(
        assemble_kernel,
        "assemble_out",
        (4,),
        at,
        [whole(part) for part in line],
        [((1, tok, width), BF16, (1, sub, width), z_row)],
        cost=LONG,
    )
    return (
        result,
        grad_inputs,
        grad_adapt_in,
        grad_b_query,
        grad_b_keyval,
        grad_b_gate_up,
        grad_a_out,
        grad_b_out,
        grad_a_down,
        grad_b_down,
    )


def solution(mesh):
    return jax.shard_map(
        functools.partial(body, mesh.shape["shard"]),
        mesh=mesh,
        in_specs=(
            P("shard", "ctx", None),
            P("shard", "ctx", None),
            P("shard", None),
            P("shard"),
            P("shard", "tp"),
            P(None, "shard", "tp"),
            P("tp", "shard"),
            P(None, "shard", "tp"),
            P("tp", "shard"),
            P(),
            P(),
            P(),
            P(),
            P(),
            P(None, None, "tp"),
            P(None, None, None, "tp"),
            P(None, None, None, "tp"),
            P(None, "tp", None),
            P(),
            P(None, "tp", None),
            P(),
        ),
        out_specs=(
            P("shard", "ctx", None),
            P("shard", "ctx", None),
            P(None, ("shard", "ctx"), None),
            P(None, None, "tp"),
            P(None, None, None, "tp"),
            P(None, None, None, "tp"),
            P(None, "tp", None),
            P(),
            P(None, "tp", None),
            P(),
        ),
        check_vma=False,
    )
```

```python
import functools

import jax
import jax.numpy as jnp
from jax import lax
from jax.experimental import pallas as pl
from jax.experimental.pallas import tpu as pltpu
from jax.sharding import PartitionSpec as P

HD = 64
RANK = 16
ADAPT = 8
EPS = 1e-05
ADAPTER_SCALING = 2.0
THETA = 1000000.0
LOG2E = 1.4426950408889634
SCALE = HD**-0.5
F32 = jnp.float32
BF16 = jnp.bfloat16
VMEM_LIMIT = 62 * 1024 * 1024

CORE = [(i, i ^ 1) for i in range(4)]
XSIDE = [(i, i ^ 2) for i in range(4)]
Z_XOR = {d: [(i, i ^ d) for i in range(4)] for d in (1, 2, 3)}
CT = ("ctx", "tp")
SCT = ("shard", "ctx", "tp")
COLUMN = [[(2 * x + k) * 4 + z for k in range(2) for z in range(4)] for x in range(2)]

COST = pl.CostEstimate(flops=1 << 20, bytes_accessed=1 << 16, transcendentals=0)
LONG = pl.CostEstimate(flops=30 << 30, bytes_accessed=16 << 20, transcendentals=0)
HIGHEST = lax.Precision.HIGHEST


def nn(left, right):
    return lax.dot_general(left, right, (((1,), (0,)), ((), ())), preferred_element_type=F32)


def nt(left, right):
    return lax.dot_general(left, right, (((1,), (1,)), ((), ())), preferred_element_type=F32)


def tn(left, right):
    return lax.dot_general(left, right, (((0,), (0,)), ((), ())), preferred_element_type=F32)


def rmsnorm(value, gain):
    return value * lax.rsqrt(jnp.mean(value * value, axis=-1, keepdims=True) + EPS) * gain


def order2(own, other, bit, axis=0):
    return jnp.concatenate(
        [jnp.where(bit == 0, own, other), jnp.where(bit == 0, other, own)], axis=axis
    )


def rows_at(value, block, size, axis=0):
    return lax.dynamic_slice_in_dim(value, block * size, size, axis)


def key_loops(segment, first, key_base, bq, bk, keys, step, acc):
    blocks = keys // bk
    low = jnp.minimum(jnp.maximum(segment[first] - key_base, 0) // bk, blocks)
    high = jnp.clip((first + bq - key_base + bk - 1) // bk, 0, blocks)
    low = jnp.minimum(low, high)
    free_low = (jnp.maximum(segment[first + bq - 1] - key_base, 0) + bk - 1) // bk
    free_low = jnp.clip(free_low, low, high)
    free_high = jnp.clip(jnp.maximum(first + 1 - key_base, 0) // bk, free_low, high)
    ahead = free_low - low

    def masked(t, carry):
        j = jnp.where(t < ahead, low + t, free_high + t - ahead)
        return step(j, carry, True)

    acc = lax.fori_loop(0, ahead + high - free_high, masked, acc)
    return lax.fori_loop(free_low, free_high, lambda j, carry: step(j, carry, False), acc)


def row_sums(weights, value):
    return lax.dot_general(
        weights, value, (((1,), (1,)), ((), ())), precision=HIGHEST, preferred_element_type=F32
    )


def fwd_kernel(bq, bk, back, last, segment, at, q_ref, kv_ref, seg_ref, *rest):
    if last:
        acc_in, mixed_ref, low_ref, lse_ref, vx = rest
    else:
        acc_ref, vx = rest
    i = pl.program_id(0)
    keys = kv_ref.shape[0]

    @pl.when(i == 0)
    def _():
        col = lax.broadcasted_iota(jnp.int32, (keys, 2 * HD), 1)
        kv = kv_ref[...]
        swapped = jnp.concatenate([kv[:, HD:], kv[:, :HD]], axis=1)
        ones = jnp.where(col == HD, 1.0, 0.0).astype(BF16)
        vx[...] = jnp.where(col < HD, swapped, ones)

    q = q_ref[...]
    both = jnp.concatenate([q[:, :HD], q[:, HD:]], axis=0)
    q_base = at[1] * (bq * pl.num_programs(0))
    k_base = q_base - back
    seg_col = jnp.broadcast_to(seg_ref[0].astype(F32), (8, bq))
    seg_col = jnp.transpose(seg_col)[:, :1].astype(jnp.int32)

    def step(j, acc, masked):
        off = pl.multiple_of(j * bk, bk)
        scores = nt(both, kv_ref[pl.ds(off, bk), :HD])
        probs = jnp.exp2(scores * (SCALE * LOG2E))
        if masked:
            qi = q_base + i * bq + lax.broadcasted_iota(jnp.int32, (bq, bk), 0)
            ki = k_base + off + lax.broadcasted_iota(jnp.int32, (bq, bk), 1)
            allowed = (ki <= qi) & (ki >= seg_col)
            probs = jnp.where(jnp.concatenate([allowed, allowed], axis=0), probs, 0.0)
        return acc + nn(probs.astype(BF16), vx[pl.ds(off, bk), :])

    if last:
        acc = jnp.concatenate([acc_in[0], acc_in[1]], axis=0)
    else:
        acc = jnp.zeros((2 * bq, 2 * HD), F32)
    acc = key_loops(segment, q_base + i * bq, k_base, bq, bk, keys, step, acc)
    if last:
        total = acc[:, HD : HD + 1]
        out = acc[:, :HD] / total
        out = jnp.concatenate([out[:bq], out[bq:]], axis=1)
        mixed_ref[...] = out
        low_ref[...] = out.astype(BF16)
        pick = jnp.where(lax.broadcasted_iota(jnp.int32, (8, 2 * HD), 1) == HD, 1.0, 0.0)
        lse_ref[0] = jnp.log2(row_sums(pick, acc)[:1])
    else:
        acc_ref[0] = acc[:bq]
        acc_ref[1] = acc[bq:]


def attention_forward(q, kv, seg, segment, at, back, bq, bk, acc_in=None):
    rows, keys = q.shape[0], kv.shape[0]
    last = acc_in is not None
    row = lambda i, *_: (i, 0)
    everything = lambda i, *_: (0, 0)
    heads = lambda i, *_: (0, i, 0)
    in_specs = [
        pl.BlockSpec((bq, 2 * HD), row),
        pl.BlockSpec((keys, 2 * HD), everything),
        pl.BlockSpec((1, 1, bq), lambda i, g, a: (a[1] * (rows // bq) + i, 0, 0)),
    ]
    args = [q, kv, seg]
    if last:
        in_specs.append(pl.BlockSpec((2, bq, 2 * HD), heads))
        args.append(acc_in)
        out_specs = [
            pl.BlockSpec((bq, 2 * HD), row),
            pl.BlockSpec((bq, 2 * HD), row),
            pl.BlockSpec((1, 1, 2 * bq), lambda i, *_: (i, 0, 0)),
        ]
        out_shape = [
            jax.ShapeDtypeStruct((rows, 2 * HD), F32),
            jax.ShapeDtypeStruct((rows, 2 * HD), BF16),
            jax.ShapeDtypeStruct((rows // bq, 1, 2 * bq), F32),
        ]
    else:
        out_specs = pl.BlockSpec((2, bq, 2 * HD), heads)
        out_shape = jax.ShapeDtypeStruct((2, rows, 2 * HD), F32)
    return pl.pallas_call(
        functools.partial(fwd_kernel, bq, bk, back, last),
        grid_spec=pltpu.PrefetchScalarGridSpec(
            num_scalar_prefetch=2,
            grid=(rows // bq,),
            in_specs=in_specs,
            out_specs=out_specs,
            scratch_shapes=[pltpu.VMEM((keys, 2 * HD), BF16)],
        ),
        out_shape=out_shape,
        compiler_params=pltpu.CompilerParams(vmem_limit_bytes=VMEM_LIMIT),
        cost_estimate=LONG,
        name="attn_fwd_last" if last else "attn_fwd_first",
    )(segment, at, *args)


def bwd_kernel(
    bq, bk, back, first, segment, at, q_ref, kv_ref, seg_ref, do_ref, out_ref, lse_ref, *rest
):
    if first:
        dq_ref, dkv_ref, dk, dv = rest
    else:
        dq_in, dq_ref, dkv_ref, dk, dv = rest
    i = pl.program_id(0)

    @pl.when(i == 0)
    def _():
        dk[...] = jnp.zeros_like(dk)
        dv[...] = jnp.zeros_like(dv)

    q = q_ref[...]
    do = do_ref[...]
    both = jnp.concatenate([q[:, :HD], q[:, HD:]], axis=0)
    both_do = jnp.concatenate([do[:, :HD], do[:, HD:]], axis=0)
    lse = lse_ref[0]
    lane = lax.broadcasted_iota(jnp.int32, (8, 2 * HD), 1)
    row = lax.broadcasted_iota(jnp.int32, (8, 2 * HD), 0)
    pick = jnp.where(lane // HD == row, 1.0, 0.0)
    deltas = row_sums(pick, do.astype(F32) * out_ref[...])
    delta = jnp.concatenate([deltas[:1], deltas[1:2]], axis=1)
    q_base = at[1] * (bq * pl.num_programs(0))
    k_base = q_base - back

    def step(j, acc, masked):
        off = pl.multiple_of(j * bk, bk)
        kv = kv_ref[pl.ds(off, bk), :]
        k, v = kv[:, :HD], kv[:, HD:]
        probs = jnp.exp2(nt(k, both) * (SCALE * LOG2E) - lse)
        if masked:
            ki = k_base + off + lax.broadcasted_iota(jnp.int32, (bk, bq), 0)
            qi = q_base + i * bq + lax.broadcasted_iota(jnp.int32, (bk, bq), 1)
            allowed = (ki <= qi) & (ki >= seg_ref[0])
            probs = jnp.where(jnp.concatenate([allowed, allowed], axis=1), probs, 0.0)
        dscores = (probs * (nt(v, both_do) - delta)).astype(BF16)
        dv[pl.ds(off, bk), :] += nn(probs.astype(BF16), both_do)
        dk[pl.ds(off, bk), :] += nn(dscores, both)
        return acc + tn(k, dscores)

    acc = key_loops(
        segment, q_base + i * bq, k_base, bq, bk, kv_ref.shape[0], step,
        jnp.zeros((HD, 2 * bq), F32),
    )
    acc = jnp.transpose(acc) * SCALE
    acc = jnp.concatenate([acc[:bq], acc[bq:]], axis=1)
    dq_ref[...] = acc if first else dq_in[...] + acc

    @pl.when(i == pl.num_programs(0) - 1)
    def _():
        dkv_ref[...] = jnp.concatenate([dk[...] * SCALE, dv[...]], axis=1).astype(dkv_ref.dtype)


def attention_backward(q, kv, seg, do, out, lse, segment, at, back, bq, bk, dq_in=None):
    rows, keys = q.shape[0], kv.shape[0]
    first = dq_in is None
    row = lambda i, *_: (i, 0)
    everything = lambda i, *_: (0, 0)
    flat = lambda i, *_: (i, 0, 0)
    in_specs = [
        pl.BlockSpec((bq, 2 * HD), row),
        pl.BlockSpec((keys, 2 * HD), everything),
        pl.BlockSpec((1, 1, bq), lambda i, g, a: (a[1] * (rows // bq) + i, 0, 0)),
        pl.BlockSpec((bq, 2 * HD), row),
        pl.BlockSpec((bq, 2 * HD), row),
        pl.BlockSpec((1, 1, 2 * bq), flat),
    ]
    args = [q, kv, seg, do, out, lse]
    if not first:
        in_specs.append(pl.BlockSpec((bq, 2 * HD), row))
        args.append(dq_in)
    return pl.pallas_call(
        functools.partial(bwd_kernel, bq, bk, back, first),
        grid_spec=pltpu.PrefetchScalarGridSpec(
            num_scalar_prefetch=2,
            grid=(rows // bq,),
            in_specs=in_specs,
            out_specs=[pl.BlockSpec((bq, 2 * HD), row), pl.BlockSpec((keys, 2 * HD), everything)],
            scratch_shapes=[pltpu.VMEM((keys, HD), F32), pltpu.VMEM((keys, HD), F32)],
        ),
        out_shape=[
            jax.ShapeDtypeStruct((rows, 2 * HD), F32),
            jax.ShapeDtypeStruct((keys, 2 * HD), BF16 if first else F32),
        ],
        compiler_params=pltpu.CompilerParams(vmem_limit_bytes=VMEM_LIMIT),
        cost_estimate=LONG,
        name="attn_bwd_first" if first else "attn_bwd_last",
    )(segment, at, *args)


def run(kernel, name, grid, scalars, inputs, outputs, scratch=(), cost=COST):
    return pl.pallas_call(
        kernel,
        grid_spec=pltpu.PrefetchScalarGridSpec(
            num_scalar_prefetch=1,
            grid=grid,
            in_specs=[
                pl.BlockSpec(memory_space=pl.ANY) if block is None else pl.BlockSpec(block, index)
                for _, block, index in inputs
            ],
            out_specs=[
                pl.BlockSpec(memory_space=pl.ANY) if block is None else pl.BlockSpec(block, index)
                for _, _, block, index in outputs
            ],
            scratch_shapes=list(scratch),
        ),
        out_shape=[jax.ShapeDtypeStruct(shape, kind) for shape, kind, _, _ in outputs],
        compiler_params=pltpu.CompilerParams(vmem_limit_bytes=VMEM_LIMIT),
        cost_estimate=cost,
        name=name,
    )(scalars, *[array for array, _, _ in inputs])


def fixed(*index):
    return lambda i, s: index


def whole(array):
    return (array, array.shape, fixed(*(0,) * array.ndim))


def out_whole(shape, kind):
    return (shape, kind, shape, fixed(*(0,) * len(shape)))


def place_matrix(back):
    at_row = lax.broadcasted_iota(jnp.int32, (4 * HD, 4 * HD), 0)
    at_col = lax.broadcasted_iota(jnp.int32, (4 * HD, 4 * HD), 1)
    if back:
        at_row, at_col = at_col, at_row
    part = HD // 2
    moved = at_row // part % 2 * (2 * HD) + at_row // HD * part + at_row % part
    return jnp.where(moved == at_col, 1.0, 0.0).astype(BF16)


def head_means(value):
    at_row = lax.broadcasted_iota(jnp.int32, (2 * HD, 2 * HD), 0) // (HD // 2)
    at_col = lax.broadcasted_iota(jnp.int32, (2 * HD, 2 * HD), 1) // (HD // 2)
    same = jnp.where(at_row == at_col, 1.0 / HD, 0.0).astype(BF16)
    high = value.astype(BF16)
    rest = (value - high.astype(F32)).astype(BF16)
    return nn(jnp.concatenate([high, rest], axis=1), jnp.concatenate([same, same], axis=0))


def rotation(step, turns, rows, blocks):
    first = turns.shape[1] - blocks
    cos_in, sin_in = turns[0, :rows], turns[1, :rows]
    cos_out, sin_out = turns[0, pl.ds(first + step, 1)], turns[1, pl.ds(first + step, 1)]
    return cos_in * cos_out - sin_in * sin_out, sin_in * cos_out + cos_in * sin_out


def head_root(first, second):
    lane = lax.broadcasted_iota(jnp.int32, first.shape, 1)
    root = lax.rsqrt(head_means(first * first + second * second) + EPS)
    return jnp.where(lane < 3 * (HD // 2), root, 1.0), lane


class Lanes:
    def __init__(self, start, size):
        self.start, self.size = start, size


def down_parts(shape, width):
    rows, cols = shape
    whole = width // cols
    tall = (rows * cols) // width
    parts = [(i * tall, (i + 1) * tall, Lanes(0, cols), 0, i * cols) for i in range(whole)]
    left = rows - whole * tall
    room = width - whole * cols
    for j in range(cols // room if left else 0):
        parts.append((whole * tall, rows, Lanes(j * room, room), j * left, whole * cols))
    return parts


def pieces_kernel(at, gate_up, down, out):
    height, width = gate_up.shape[1:]
    out[:height] = gate_up[0]
    value = down[...]
    for a, b, lanes, at_row, at_lane in down_parts(value.shape, width):
        out[height + at_row : height + at_row + b - a, at_lane : at_lane + lanes.size] = value[
            a:b, lanes.start : lanes.start + lanes.size
        ]


def prepare_kernel(
    at, q, kv, out_w, up_gate_up, lower_down, up_q, up_kv, lower_out,
    rows_o, small_o, upper_o, low_o,
):
    k = at[0]
    value = kv[...].astype(F32)
    value = jnp.where(k == 0, value[:, :, :HD], value[:, :, HD:]).astype(BF16)
    value = jnp.concatenate([q[...], value[0], value[1]], axis=1)
    height = 4 * HD
    rows_o[:height] = nt(place_matrix(True), value).astype(BF16)
    rows_o[height:] = out_w[...]
    small_o[:2] = up_gate_up[0]
    small_o[2] = lower_down[0]
    table = up_kv[0].astype(F32)
    table = jnp.where(k == 0, table[:, :, :HD], table[:, :, HD:]).astype(BF16)
    zero = jnp.zeros_like(table[0])
    wide = jnp.zeros((RANK, 2 * HD), BF16)
    rows = [
        jnp.concatenate([up_q[0], wide], axis=1),
        jnp.concatenate([wide, table[0], zero], axis=1),
        jnp.concatenate([wide, zero, table[1]], axis=1),
    ] + [jnp.concatenate([wide, wide], axis=1)] * 5
    upper_o[...] = nt(place_matrix(True), jnp.concatenate(rows, axis=0)).astype(BF16)
    table = jnp.transpose(lower_out[0].astype(F32))
    low_o[...] = jnp.concatenate(
        [table, jnp.zeros((table.shape[0], 2 * HD - RANK), F32)], axis=1
    ).astype(BF16)


def project_kernel(
    at, own, oth, gain, dense, lower, upper, turns, gains,
    normal_o, narrow_o, q_o, kv_o, raw_o, weights,
):
    width = 4 * HD
    step = pl.program_id(0)
    steps = pl.num_programs(0)

    @pl.when(step == 0)
    def _():
        weights[:width] = dense[...]
        weights[width : width + 3 * RANK] = lower[0]
        weights[width + 3 * RANK :] = jnp.zeros(
            (weights.shape[0] - width - 3 * RANK, weights.shape[1]), BF16
        )

    value = jnp.where(step < steps // 2, own[...].astype(F32), oth[...].astype(F32))
    root = lax.rsqrt(jnp.mean(value * value, axis=1, keepdims=True) + EPS)
    normal = (value * root * gain[...]).astype(BF16)
    normal_o[...] = normal
    raw = nt(normal, weights[...])
    narrow = raw[:, width:].astype(BF16)
    narrow_o[...] = narrow[:, : 3 * RANK]
    raw = raw[:, :width] + ADAPTER_SCALING * nt(narrow, upper[...])
    raw_o[...] = raw
    first, second = raw[:, : 2 * HD], raw[:, 2 * HD :]
    root, _ = head_root(first, second)
    place = jnp.where(step < steps // 2, at[0] * (steps // 2) + step, (1 - at[0]) * (steps // 2) + step - steps // 2)
    cos, sin = rotation(place, turns, normal.shape[0], steps)
    first = first * root * gains[0:1]
    second = second * root * gains[1:2]
    turned = jnp.concatenate([first * cos - second * sin, second * cos + first * sin], axis=1)
    out = nn(turned.astype(BF16), place_matrix(True)).astype(BF16)
    q_o[...] = out[:, : 2 * HD]
    kv_o[...] = out[:, 2 * HD :]


def project_back_kernel(
    at, dq, dkv, dkv_after, raw, turns, gains, narrow, normal, upper,
    out, wide_o, heads_o, wide, heads,
):
    step = pl.program_id(0)

    @pl.when(step == 0)
    def _():
        wide[...] = jnp.zeros_like(wide)
        heads[...] = jnp.zeros_like(heads)

    cos, sin = rotation(2 * step, turns, dq.shape[0], 2 * pl.num_programs(0))
    grad_kv = (dkv[...] + dkv_after[...].astype(F32)).astype(BF16)
    grad = nn(jnp.concatenate([dq[...].astype(BF16), grad_kv], axis=1), place_matrix(False))
    first, second = raw[:, : 2 * HD], raw[:, 2 * HD :]
    root, lane = head_root(first, second)
    first, second = first * root, second * root
    back_first = grad[:, : 2 * HD] * cos + grad[:, 2 * HD :] * sin
    back_second = grad[:, 2 * HD :] * cos - grad[:, : 2 * HD] * sin
    back_first = back_first * gains[0:1]
    back_second = back_second * gains[1:2]
    mean = head_means(back_first * first + back_second * second)
    mean = jnp.where(lane < 3 * (HD // 2), mean, 0.0)
    back_first = (root * (back_first - first * mean)).astype(BF16)
    back_second = (root * (back_second - second * mean)).astype(BF16)
    grad = jnp.concatenate([back_first, back_second], axis=1)
    out[...] = grad
    inside = (ADAPTER_SCALING * nn(grad, upper[...])).astype(BF16)
    wide[...] += tn(inside[:, : 3 * RANK], normal[...])
    heads[...] += tn(narrow[...], grad)

    @pl.when(step == pl.num_programs(0) - 1)
    def _():
        wide_o[...] = wide[...].astype(BF16)
        total = (heads[...] * ADAPTER_SCALING).astype(BF16)
        total = nn(total, place_matrix(True))
        total = jnp.concatenate(
            [
                total[:RANK, : 2 * HD],
                total[RANK : 2 * RANK, 2 * HD : 3 * HD],
                total[2 * RANK :, 3 * HD :],
            ],
            axis=1,
        )
        zero = jnp.zeros_like(total)
        heads_o[:, : 4 * HD] = jnp.where(at[0] == 0, total, zero).astype(BF16)
        heads_o[:, 4 * HD :] = jnp.where(at[0] == 0, zero, total).astype(BF16)


def head_blocks(value, which):
    return jnp.concatenate([value[which * 4 + place] for place in range(4)], axis=1)


def mix_kernel(at, mixed, out_own, out_oth, upper, tokens, gain, hidden_o, normal_o, narrow_o):
    k = at[0]
    width = tokens.shape[2]
    total = nn(head_blocks(mixed, k), out_own[...]) + nn(head_blocks(mixed, 1 - k), out_oth[...])
    narrow = total[:, width : width + RANK].astype(BF16)
    narrow_o[...] = narrow
    total = tokens[0].astype(F32) + total[:, :width] + ADAPTER_SCALING * nn(narrow, upper[0])
    hidden_o[...] = total
    root = lax.rsqrt(jnp.mean(total * total, axis=1, keepdims=True) + EPS)
    normal_o[...] = (total * root * gain[...]).astype(BF16)


def norm_back(value, grad, gain):
    root = lax.rsqrt(jnp.mean(value * value, axis=1, keepdims=True) + EPS)
    unit = value * root
    grad = grad * gain
    return root * (grad - unit * jnp.mean(grad * unit, axis=1, keepdims=True))


def mix_back_kernel(
    at, hidden, cotangent, own, arrived, far, gain, out_own, out_oth, upper,
    grad_o, low_o, mixed_o, narrow_o,
):
    k = at[0]
    rows = hidden.shape[0]
    grad = own[:rows].astype(F32) + arrived[:rows].astype(F32) + far[...].astype(F32)
    grad = cotangent[0].astype(F32) + norm_back(hidden[...], grad, gain[...])
    grad_o[...] = grad
    low = grad.astype(BF16)
    low_o[...] = low
    table = jnp.transpose(upper[0].astype(F32))
    table = jnp.concatenate([table, jnp.zeros((table.shape[0], 2 * HD - RANK), F32)], axis=1)
    narrow = (ADAPTER_SCALING * nn(low, table.astype(BF16))).astype(BF16)
    narrow_o[...] = narrow[:, :RANK]
    low = jnp.concatenate([low, narrow], axis=1)
    for which, source in ((k, out_own), (1 - k, out_oth)):
        value = nt(low, source[...]).astype(BF16)
        for place in range(4):
            mixed_o[which * 4 + place] = value[:, place * 2 * HD : (place + 1) * 2 * HD]


def mix_grads_kernel(at, mixed, low, narrow, narrow_back, out_o):
    out_o[:RANK] = (ADAPTER_SCALING * tn(narrow[...], low[...])).astype(BF16)
    for i in range(8):
        value = tn(narrow_back[...], mixed[i])
        out_o[RANK:, i * 2 * HD : (i + 1) * 2 * HD] = value.astype(BF16)


def last_kernel(at, grads, own, own_x, oth, oth_x, lower, hidden, tokens, gain, out):
    k, x = at[0], at[1]
    width = hidden.shape[1]
    total = 0.0
    for which, side, source in ((k, x, own), (k, 1 - x, own_x), (1 - k, x, oth), (1 - k, 1 - x, oth_x)):
        lanes = pl.ds(pl.multiple_of(side * 2 * HD, 2 * HD), 2 * HD)
        value = [grads[which * 4 + place, :, lanes] for place in range(4)]
        total += nn(jnp.concatenate(value, axis=1), source[...])
    narrow = (ADAPTER_SCALING * total[:, width : width + 3 * RANK]).astype(BF16)
    total = total[:, :width] + nn(narrow, lower[0])
    value = tokens[0].astype(F32)
    out[...] = (hidden[...] + norm_back(value, total, gain[...])).astype(BF16)


def weight_copies(at, sources, dst, sem, down):
    k, x, y = at[0], at[1], at[2]

    def lanes(start, size):
        return pl.ds(pl.multiple_of(start, 2 * HD), size)

    def rows(start, size):
        return pl.ds(pl.multiple_of(start, 16), size)

    if down:
        height, width = dst.shape[0], sources[0].shape[1]
    else:
        height, width = sources[0].shape[1:]
    if len(sources) == 1:
        if down:
            pairs = [(sources[0], dst.at[:, pl.ds(0, width)])]
        else:
            pairs = [
                (sources[0].at[m], dst.at[pl.ds(0, height), pl.ds(m * width, width)])
                for m in range(2)
            ]
        return [
            (None, [pltpu.make_async_copy(a, b, sem.at[i]) for i, (a, b) in enumerate(pairs)])
        ]
    local, mine, *pieces = sources
    zero, one = [], []
    if down:
        part = height // 2
        for j, source in enumerate((local, mine)):
            zero.append((source, dst.at[:, lanes((y + j) % 2 * width, width)]))
        tall = pieces[0].shape[0] - part * width // pieces[0].shape[1]
        for j, source in enumerate(pieces):
            for a, b, cols, at_row, at_lane in down_parts((part, width), source.shape[1]):
                one.append(
                    (
                        source.at[pl.ds(tall + at_row, b - a), pl.ds(at_lane, cols.size)],
                        dst.at[
                            rows((x + j) % 2 * part + a, b - a),
                            lanes((y + j // 2) % 2 * width + cols.start, cols.size),
                        ],
                    )
                )
    else:
        for j, source in enumerate((local, mine)):
            for m in range(2):
                at_row = rows((y + j) % 2 * height, height)
                zero.append((source.at[m], dst.at[at_row, pl.ds(m * width, width)]))
        for j, source in enumerate(pieces):
            at_row = rows((y + j // 2) % 2 * height, height)
            source = source.at[pl.ds(0, height)]
            one.append((source, dst.at[at_row, lanes((x + j) % 2 * width, width)]))
    return [
        (when, [pltpu.make_async_copy(a, b, sem.at[i]) for i, (a, b) in enumerate(pairs)])
        for when, pairs in ((k == 0, zero), (k == 1, one))
    ]


def for_copies(groups, what):
    for when, copies in groups:
        if when is None:
            for copy in copies:
                what(copy)
        else:

            @pl.when(when)
            def _():
                for copy in copies:
                    what(copy)


def put_down_lower(down, small):
    width = 2 * HD
    table = jnp.transpose(small[2].astype(F32))
    table = jnp.concatenate(
        [table, jnp.zeros((table.shape[0], width - table.shape[1]), F32)], axis=1
    )
    down[:, down.shape[1] - width :] = table.astype(BF16)


def both_tokens(step, own, far, own_oth, far_oth):
    here = jnp.concatenate([own[...], far[...]], axis=0).astype(F32)
    there = jnp.concatenate([own_oth[...], far_oth[...]], axis=0).astype(F32)
    return jnp.where(step == 0, here, there).astype(BF16)


def wide_table(table):
    table = jnp.transpose(table.astype(F32))
    return jnp.concatenate(
        [table, jnp.zeros((table.shape[0], 2 * HD - table.shape[1]), F32)], axis=1
    ).astype(BF16)


def ffn_kernel(many, at, own, far, own_oth, far_oth, cot, cot_far, cot_oth, cot_far_oth, *rest):
    lower, small, upper = rest[:3]
    sources, down_sources = rest[3 : 3 + many], rest[3 + many : 3 + 2 * many]
    part_own, part_oth, act_o, grad_o, narrow_o, back_o, weights, down, tables, sem = rest[
        3 + 2 * many :
    ]
    step = pl.program_id(0)
    units = small.shape[2]
    first = weight_copies(at, sources, weights, sem.at[0], False)
    second = weight_copies(at, down_sources, down, sem.at[1], True)

    @pl.when(step == 0)
    def _():
        for_copies(second, lambda copy: copy.start())
        for_copies(first, lambda copy: copy.start())
        put_down_lower(down, small)
        tables[0] = wide_table(lower[0][3 * RANK :])
        tables[1] = wide_table(upper[0])
        for_copies(second, lambda copy: copy.wait())

    value = both_tokens(step, own, far, own_oth, far_oth)
    grad = both_tokens(step, cot.at[0], cot_far.at[0], cot_oth, cot_far_oth)
    narrow_o[0] = nn(value, tables[0]).astype(BF16)[:, : 2 * RANK]
    narrow = (ADAPTER_SCALING * nn(grad, tables[1])).astype(BF16)
    back_o[0] = narrow[:, :RANK]
    grad = jnp.concatenate([grad, narrow], axis=1)
    grad_act = nt(grad, down[...])

    @pl.when(step == 0)
    def _():
        for_copies(first, lambda copy: copy.wait())
        for i in range(2):
            term = lower[0][(3 + i) * RANK : (4 + i) * RANK]
            at_lanes = slice(i * units, (i + 1) * units)
            merged = weights[:, at_lanes].astype(F32) + ADAPTER_SCALING * tn(term, small[i])
            weights[:, at_lanes] = merged.astype(BF16)

    both = nn(value, weights[...])
    gate, up = both[:, :units], both[:, units:]
    sig = 0.5 * jnp.tanh(0.5 * gate) + 0.5
    silu = gate * sig
    act_o[0] = (silu * up).astype(BF16)
    grad_gate = (grad_act * up * (sig + silu * (1.0 - sig))).astype(BF16)
    grad_up = (grad_act * silu).astype(BF16)
    grad_both = jnp.concatenate([grad_gate, grad_up], axis=1)
    grad_o[0] = grad_both
    part = nt(grad_both, weights[...]).astype(BF16)

    @pl.when(step == 0)
    def _():
        part_own[...] = part

    @pl.when(step == 1)
    def _():
        part_oth[...] = part


def ffn_down_kernel(many, at, act, small, upper, *rest):
    sources = rest[:many]
    part_own, part_oth, zd_o, down, sem = rest[many:]
    step = pl.program_id(0)
    width = upper.shape[2]
    copies = weight_copies(at, sources, down, sem.at[0], True)

    @pl.when(step == 0)
    def _():
        for_copies(copies, lambda copy: copy.start())
        put_down_lower(down, small)
        for_copies(copies, lambda copy: copy.wait())

    part = nn(act[0], down[...])
    zd = part[:, width : width + RANK].astype(BF16)
    zd_o[0] = zd
    part = (part[:, :width] + ADAPTER_SCALING * nn(zd, upper[0])).astype(BF16)

    @pl.when(step == 0)
    def _():
        part_own[...] = part

    @pl.when(step == 1)
    def _():
        part_oth[...] = part


def ffn_grads_kernel(at, own, far, own_oth, far_oth, cot, cot_far, cot_oth, cot_far_oth, *rest):
    act, grads, narrow, narrow_back, zd, small, wide_o, quarter_o, lanes, wide, quarter = rest
    step = pl.program_id(0)
    units = small.shape[2]

    @pl.when(step == 0)
    def _():
        wide[...] = jnp.zeros_like(wide)
        quarter[...] = jnp.zeros_like(quarter)
        lanes[...] = jnp.zeros_like(lanes)
        for i in range(2):
            table = jnp.transpose(small[i].astype(F32))
            zero = jnp.zeros_like(table)
            table = jnp.concatenate([table, zero] if i == 0 else [zero, table], axis=1)
            lanes[i * units : (i + 1) * units, : 2 * RANK] = table.astype(BF16)

    value = both_tokens(step, own, far, own_oth, far_oth)
    grad = both_tokens(step, cot.at[0], cot_far.at[0], cot_oth, cot_far_oth)
    inner = (ADAPTER_SCALING * nn(grads[0], lanes[...])).astype(BF16)[:, : 2 * RANK]
    wide[:RANK] += ADAPTER_SCALING * tn(zd[0], grad)
    wide[RANK:] += tn(inner, value)
    both = tn(narrow[0], grads[0])
    quarter[:RANK] += ADAPTER_SCALING * both[:RANK, :units]
    quarter[RANK : 2 * RANK] += ADAPTER_SCALING * both[RANK:, units:]
    quarter[2 * RANK :] += tn(narrow_back[0], act[0])

    @pl.when(step == 1)
    def _():
        wide_o[...] = wide[...].astype(BF16)
        quarter_o[...] = quarter[...].astype(BF16)


def ring_kernel(at, *rest):
    out = rest[4]
    for d in range(4):

        @pl.when((at[4] + 4 - pl.program_id(0)) % 4 == d)
        def _():
            out[0] = rest[d][...].astype(out.dtype)


def assemble_kernel(at, own, *rest):
    z = at[4]
    up, down, out = rest[:3], rest[3:6], rest[6]
    place = pl.program_id(0)

    @pl.when(place == z)
    def _():
        out[0] = own[...].astype(out.dtype)

    for d in range(3):

        @pl.when(z - place == d + 1)
        def _():
            out[0] = up[d][...].astype(out.dtype)

        @pl.when(place - z == d + 1)
        def _():
            out[0] = down[d][...].astype(out.dtype)


def plus(here, there):
    return (here.astype(F32) + there.astype(F32)).astype(BF16)


def tie(*values):
    return lax.optimization_barrier(values)


def tie_all(values):
    return lax.optimization_barrier(values)


def heads_tokens(value):
    return lax.all_to_all(value, CT, 0, 0, axis_index_groups=COLUMN, tiled=True)


UP = [(i, i + 1) for i in range(3)]
RING = [(i, (i + 1) % 4) for i in range(4)]
DOWN = [(i + 1, i) for i in range(3)]


def body(
    shards,
    inputs,
    cotangent,
    segments,
    adapter_index,
    query_weight,
    key_value_weight,
    output_weight,
    gate_up_weight,
    down_weight,
    norm_attn,
    norm_ffn,
    q_gain,
    k_gain,
    input_adapter_lower,
    query_adapter_upper,
    key_value_adapter_upper,
    gate_up_adapter_upper,
    output_adapter_lower,
    output_adapter_upper,
    down_adapter_lower,
    down_adapter_upper,
):
    ctx = lax.axis_index("ctx")
    x, k = ctx // 2, ctx % 2
    z = lax.axis_index("tp")
    y = lax.axis_index("shard")
    tok = inputs.shape[1]
    half = 2 * tok
    sub = tok // 4
    width = inputs.shape[2]
    hidden_units = gate_up_weight.shape[2]
    slot = adapter_index[0]
    segment = segments[0]
    pair = shards == 2
    swap_y = [(0, 1), (1, 0)]
    cols = 2 * HD
    at = jnp.stack([k, x, y, slot, z]).astype(jnp.int32)
    K, X, Y, SLOT, Z = range(5)

    def shard_rows(piece, axis):
        if pair:
            return order2(piece, lax.ppermute(piece, "shard", swap_y), y, axis)
        return lax.all_gather(piece, "shard", axis=axis, tiled=True)

    def over_y(cores):
        return [
            ((s * 4 + c) * 4 + t, ((s ^ 1) * 4 + c) * 4 + t)
            for s in range(2)
            for c in cores
            for t in range(4)
        ]

    tokens_other = lax.ppermute(inputs[0], "ctx", CORE)
    by_slot = lambda i, s: (s[SLOT], 0, 0)
    prepared = run(
        prepare_kernel,
        "prepare",
        (1,),
        at,
        [
            (query_weight, (query_weight.shape[0], cols), lambda i, s: (0, s[K])),
            whole(key_value_weight),
            (output_weight, (cols, output_weight.shape[1]), lambda i, s: (s[K], 0)),
            (gate_up_adapter_upper, (1, 2, RANK, hidden_units), lambda i, s: (s[SLOT], 0, 0, 0)),
            (jnp.swapaxes(down_adapter_lower, 1, 2), (1, RANK, hidden_units), by_slot),
            (query_adapter_upper, (1, RANK, cols), lambda i, s: (s[SLOT], 0, s[K])),
            (key_value_adapter_upper, (1, 2, RANK, cols), lambda i, s: (s[SLOT], 0, 0, 0)),
            (
                jnp.swapaxes(output_adapter_lower, 1, 2),
                (1, RANK, cols),
                lambda i, s: (s[SLOT], 0, s[K]),
            ),
        ],
        [
            out_whole((3 * cols, query_weight.shape[0]), BF16),
            out_whole((3, RANK, hidden_units), BF16),
            out_whole((2 * cols, cols), BF16),
            out_whole((cols, cols), BF16),
        ],
    )
    piece_rows, small_ffn, upper_qkv, low_rows = prepared
    dense_rows = shard_rows(piece_rows, 1)
    dense_qkv, rows_here = dense_rows[: 2 * cols], dense_rows[2 * cols :]

    far_z = [(c * 4 + t, c * 4 + (t ^ 2)) for c in (1, 3) for t in range(4)]
    far_x = [(1, 3), (3, 1)]
    if pair:
        (piece,) = run(
            pieces_kernel,
            "pieces",
            (1,),
            at,
            [
                (gate_up_weight, (1,) + gate_up_weight.shape[1:], lambda i, s: (s[X], 0, 0)),
                (down_weight, (hidden_units // 2, down_weight.shape[1]), lambda i, s: (s[X], 0)),
            ],
            [
                out_whole(
                    (
                        gate_up_weight.shape[1] + down_weight.shape[1] // 2,
                        hidden_units,
                    ),
                    BF16,
                )
            ],
        )
        piece = lax.ppermute(piece, CT, far_z)

    block = tok // 4
    blocks = half // block
    half_dim = HD // 2
    first_query = x * half
    inverse = THETA ** (-(jnp.arange(half_dim, dtype=F32) * 2.0 / HD))
    inverse = jnp.concatenate([inverse] * 3 + [jnp.zeros_like(inverse)])
    places = jnp.arange(2 * block + blocks, dtype=jnp.int32)
    places = jnp.where(places < 2 * block, places, first_query + block * (places - 2 * block))
    angles = places.astype(F32)[:, None] * inverse[None, :]
    turns = jnp.stack([jnp.cos(angles), jnp.sin(angles)])

    by_row = lambda i, s: (i, 0)
    by_step = lambda i, s: (i, 0, 0)
    lower_table = jnp.swapaxes(input_adapter_lower, 1, 2)
    lower_spec = (lower_table, (1, 5 * RANK, width), by_slot)
    ones = jnp.ones((half_dim,), F32)
    gains = jnp.stack(
        [
            jnp.concatenate([q_gain[part], q_gain[part], k_gain[part], ones])
            for part in (slice(0, half_dim), slice(half_dim, HD))
        ]
    )
    gain_attn, gain_ffn = norm_attn[None], norm_ffn[None]
    own_row = lambda i, s: (jnp.minimum(i, 3), 0)
    oth_row = lambda i, s: (jnp.maximum(i - 4, 0), 0)
    chip_row = lambda i, s: (jnp.where(i < 4, s[K] * 4 + i, (1 - s[K]) * 4 + i - 4), 0)
    normalized, narrow, queries, keyvals, raw = run(
        project_kernel,
        "project",
        (8,),
        at,
        [
            (inputs[0], (block, width), own_row),
            (tokens_other, (block, width), oth_row),
            whole(gain_attn),
            (dense_rows, (2 * cols, width), fixed(0, 0)),
            (lower_table, (1, 3 * RANK, width), by_slot),
            whole(upper_qkv),
            whole(turns),
            whole(gains),
        ],
        [
            ((half, width), BF16, (block, width), chip_row),
            ((half, 3 * RANK), BF16, (block, 3 * RANK), chip_row),
            ((half, cols), BF16, (block, cols), chip_row),
            ((half, cols), BF16, (block, cols), chip_row),
            ((half, 2 * cols), F32, (block, 2 * cols), chip_row),
        ],
        [pltpu.VMEM((3 * cols, width), BF16)],
    )
    keyvals_before = lax.ppermute(keyvals, "ctx", [(0, 2), (1, 3)])

    size = half // 4
    seg_rows = segment.reshape(-1, 1, size)
    keyvals, small_from = tie(keyvals, small_ffn)
    small_far = lax.ppermute(small_from, "tp", Z_XOR[2])
    if pair:
        keyvals, gate_up_from = tie(keyvals, gate_up_weight)
        mine_g = lax.ppermute(gate_up_from, SCT, over_y((0, 2)))
    acc = attention_forward(queries, keyvals, seg_rows, segment, at, 0, size, size)
    acc, out_rows = tie(acc, jnp.concatenate([rows_here, low_rows], axis=1))
    out_own = lax.all_gather(out_rows, "tp", axis=0, tiled=True)
    cot_oth = lax.ppermute(cotangent[0], "ctx", CORE)
    mixed, mixed_low, lse = attention_forward(
        queries, keyvals_before, seg_rows, segment, at, half, size, 2 * size, acc
    )
    mixed_low, small_far = tie(mixed_low, small_far)
    small_ffn = jnp.where(k == 0, small_ffn, small_far)
    if pair:
        mixed_low, piece, down_from = tie(mixed_low, piece, down_weight)
        piece_x = lax.ppermute(piece, "ctx", far_x)
        piece_y = lax.ppermute(piece, SCT, over_y((1, 3)))
        mine_d = lax.ppermute(down_from, SCT, over_y((0, 2)))

    mixed_all = heads_tokens(mixed_low.reshape(8, sub, cols))
    qkv_rows = rows_at(jnp.concatenate([dense_qkv, upper_qkv], axis=1), x, cols)
    mixed_all, small_ffn, cot_oth, qkv_rows = tie(mixed_all, small_ffn, cot_oth, qkv_rows)
    out_oth = lax.ppermute(out_own, "ctx", CORE)
    if pair:
        mixed_all, mine_g, piece_x, piece_y, out_own = tie(
            mixed_all, mine_g, piece_x, piece_y, out_own
        )
        piece_xy = lax.ppermute(piece_y, "ctx", far_x)
        pieces = [piece, piece_x, piece_y, piece_xy]
        sources = [gate_up_weight, mine_g] + pieces
        down_sources = [down_weight, mine_d] + pieces
    else:
        full_g = lax.all_gather(gate_up_weight, "shard", axis=1, tiled=True)
        full_d = lax.all_gather(down_weight, "shard", axis=1, tiled=True)
        sources = [jnp.where(k == 0, full_g, lax.ppermute(full_g, "tp", Z_XOR[2]))]
        down_sources = [jnp.where(k == 0, full_d, lax.ppermute(full_d, "tp", Z_XOR[2]))]
    z_block = lambda i, s: (0, s[Z], 0)
    upper_out_spec = (output_adapter_upper, (1, RANK, width), lambda i, s: (s[SLOT], 0, 0))
    hidden_state, normalized_second, narrow_out = run(
        mix_kernel,
        "mix",
        (1,),
        at,
        [
            whole(mixed_all),
            whole(out_own),
            whole(out_oth),
            upper_out_spec,
            (inputs, (1, sub, width), z_block),
            whole(gain_ffn),
        ],
        [
            out_whole((sub, width), F32),
            out_whole((sub, width), BF16),
            out_whole((sub, RANK), BF16),
        ],
    )

    second = normalized_second
    second_oth = lax.ppermute(second, "ctx", CORE)
    second_far = lax.ppermute(second, "tp", Z_XOR[1])
    second_far_oth = lax.ppermute(second_far, "ctx", CORE)
    upper_down_spec = (down_adapter_upper, (1, RANK, width), by_slot)
    z_far = lambda i, s: (0, s[Z] ^ 1, 0)
    ffn_tokens = [
        whole(second),
        whole(second_far),
        whole(second_oth),
        whole(second_far_oth),
        (cotangent, (1, sub, width), z_block),
        (cotangent, (1, sub, width), z_far),
        (cot_oth, (sub, width), lambda i, s: (s[Z], 0)),
        (cot_oth, (sub, width), lambda i, s: (s[Z] ^ 1, 0)),
    ]
    tall = 2 * sub
    qkv_rows, second_far_oth = tie(qkv_rows, second_far_oth)
    qkv_own = lax.all_gather(qkv_rows, "tp", axis=0, tiled=True)
    ffn_tokens[3] = whole(second_far_oth)
    part_own, part_oth, active, grad_both, narrow_second, narrow_back_second = run(
        functools.partial(ffn_kernel, len(sources)),
        "ffn",
        (2,),
        at,
        ffn_tokens
        + [lower_spec, whole(small_ffn), upper_down_spec]
        + [(source, None, None) for source in sources + down_sources],
        [
            out_whole((tall, width), BF16),
            out_whole((tall, width), BF16),
            ((2, tall, hidden_units), BF16, (1, tall, hidden_units), by_step),
            ((2, tall, 2 * hidden_units), BF16, (1, tall, 2 * hidden_units), by_step),
            ((2, tall, 2 * RANK), BF16, (1, tall, 2 * RANK), by_step),
            ((2, tall, RANK), BF16, (1, tall, RANK), by_step),
        ],
        [
            pltpu.VMEM((width, 2 * hidden_units), BF16),
            pltpu.VMEM((hidden_units, width + cols), BF16),
            pltpu.VMEM((2, width, cols), BF16),
            pltpu.SemaphoreType.DMA((2, 24)),
        ],
        LONG,
    )
    part_arrived = lax.ppermute(part_oth, "ctx", CORE)
    part_give = (part_own[sub:].astype(F32) + part_arrived[sub:].astype(F32)).astype(BF16)
    part_give, active, qkv_own = tie(part_give, active, qkv_own)
    part_far = lax.ppermute(part_give, "tp", Z_XOR[1])
    qkv_own_x = lax.ppermute(qkv_own, "ctx", XSIDE)

    down_own, down_oth, zd = run(
        functools.partial(ffn_down_kernel, len(sources)),
        "ffn_down",
        (2,),
        at,
        [
            (active, (1, tall, hidden_units), by_step),
            whole(small_ffn),
            upper_down_spec,
        ]
        + [(source, None, None) for source in down_sources],
        [
            out_whole((tall, width), BF16),
            out_whole((tall, width), BF16),
            ((2, tall, RANK), BF16, (1, tall, RANK), by_step),
        ],
        [pltpu.VMEM((hidden_units, width + cols), BF16), pltpu.SemaphoreType.DMA((1, 24))],
        LONG,
    )
    hidden_back, down_own, down_oth, zd = tie(hidden_state, down_own, down_oth, zd)

    grad_hidden, grad_hidden_low, grad_mixed_all, narrow_back = run(
        mix_back_kernel,
        "mix_back",
        (1,),
        at,
        [
            whole(hidden_back),
            (cotangent, (1, sub, width), z_block),
            whole(part_own),
            whole(part_arrived),
            whole(part_far),
            whole(gain_ffn),
            whole(out_own),
            whole(out_oth),
            upper_out_spec,
        ],
        [
            out_whole((sub, width), F32),
            out_whole((sub, width), BF16),
            out_whole((8, sub, cols), BF16),
            out_whole((sub, RANK), BF16),
        ],
    )
    grad_mixed_all, grad_both, down_oth = tie(grad_mixed_all, grad_both, down_oth)
    grad_mixed = heads_tokens(grad_mixed_all).reshape(half, cols)
    down_arrived = lax.ppermute(down_oth, "ctx", CORE)
    down_give = (down_own[sub:].astype(F32) + down_arrived[sub:].astype(F32)).astype(BF16)
    down_far = lax.ppermute(down_give, "tp", Z_XOR[1])
    final = hidden_state + (
        down_own[:sub].astype(F32) + down_arrived[:sub].astype(F32) + down_far.astype(F32)
    )
    final = final.astype(BF16)
    wide_ffn, quarter_grads = run(
        ffn_grads_kernel,
        "ffn_grads",
        (2,),
        at,
        ffn_tokens
        + [
            (active, (1, tall, hidden_units), by_step),
            (grad_both, (1, tall, 2 * hidden_units), by_step),
            (narrow_second, (1, tall, 2 * RANK), by_step),
            (narrow_back_second, (1, tall, RANK), by_step),
            (zd, (1, tall, RANK), by_step),
            whole(small_ffn),
        ],
        [out_whole((3 * RANK, width), BF16), out_whole((3 * RANK, hidden_units), BF16)],
        [
            pltpu.VMEM((2 * hidden_units, cols), BF16),
            pltpu.VMEM((3 * RANK, width), F32),
            pltpu.VMEM((3 * RANK, hidden_units), F32),
        ],
        LONG,
    )
    (wide_mix,) = run(
        mix_grads_kernel,
        "mix_grads",
        (1,),
        at,
        [whole(mixed_all), whole(grad_hidden_low), whole(narrow_out), whole(narrow_back)],
        [out_whole((2 * RANK, width), BF16)],
    )
    wide_early = jnp.concatenate([wide_mix, wide_ffn], axis=0)
    grad_mixed, wide_early, qkv_own_x = tie(grad_mixed, wide_early, qkv_own_x)
    wide_near = lax.ppermute(wide_early, "tp", Z_XOR[1])
    if pair:
        slot_other = lax.ppermute(adapter_index, "shard", swap_y)[0]

    dq_before, dkv_before = attention_backward(
        queries,
        keyvals_before,
        seg_rows,
        grad_mixed,
        mixed,
        lse,
        segment,
        at,
        half,
        size,
        size,
    )
    dkv_after = lax.ppermute(dkv_before, "ctx", [(2, 0), (3, 1)])
    dq_before, wide_near, quarter_grads, qkv_own, qkv_own_x, final = tie(
        dq_before, wide_near, quarter_grads, qkv_own, qkv_own_x, final
    )
    out_up_1 = lax.ppermute(final, "tp", UP)
    out_down_1 = lax.ppermute(final, "tp", DOWN)
    if pair:
        dq_before, slot_other = tie(dq_before, slot_other)
    qkv_oth = lax.ppermute(qkv_own, "ctx", CORE)
    qkv_oth_x = lax.ppermute(qkv_own_x, "ctx", CORE)
    wide_early = plus(wide_early, wide_near)
    early = jnp.concatenate(
        [jnp.pad(wide_early, ((0, 0), (0, hidden_units - width))), quarter_grads], axis=0
    )
    early_far = lax.ppermute(early, "tp", Z_XOR[2])
    dq, dkv = attention_backward(
        queries,
        keyvals,
        seg_rows,
        grad_mixed,
        mixed,
        lse,
        segment,
        at,
        0,
        size,
        size,
        dq_before,
    )
    dq, early_far, out_up_1, out_down_1 = tie(dq, early_far, out_up_1, out_down_1)
    out_up_2 = lax.ppermute(out_up_1, "tp", UP[1:])
    out_down_2 = lax.ppermute(out_down_1, "tp", DOWN[:2])
    early = jnp.concatenate(
        [
            plus(early[: 5 * RANK], early_far[: 5 * RANK]),
            jnp.where(k == 0, early[5 * RANK :], early_far[5 * RANK :]),
        ],
        axis=0,
    )
    tall_blocks = blocks // 2
    d_projected, wide_attn, head_grads = run(
        project_back_kernel,
        "project_back",
        (tall_blocks,),
        at,
        [
            (dq, (2 * block, cols), by_row),
            (dkv, (2 * block, cols), by_row),
            (dkv_after, (2 * block, cols), by_row),
            (raw, (2 * block, 2 * cols), by_row),
            whole(turns),
            whole(gains),
            (narrow, (2 * block, 3 * RANK), by_row),
            (normalized, (2 * block, width), by_row),
            whole(upper_qkv),
        ],
        [
            ((half, 2 * cols), BF16, (2 * block, 2 * cols), by_row),
            out_whole((3 * RANK, width), BF16),
            out_whole((RANK, 4 * cols), BF16),
        ],
        [pltpu.VMEM((3 * RANK, width), F32), pltpu.VMEM((3 * RANK, 2 * cols), F32)],
        LONG,
    )
    d_projected, out_up_2, out_down_2 = tie(d_projected, out_up_2, out_down_2)
    out_3 = lax.ppermute(jnp.where(z == 2, out_up_2, out_down_2), "tp", UP[2:] + DOWN[:1])
    out_up_3 = out_down_3 = out_3

    d_all = heads_tokens(d_projected.reshape(8, sub, 2 * cols))
    def lanes_to(value, size):
        return jnp.pad(value, ((0, 0), (0, size - value.shape[1])))

    packed = jnp.concatenate(
        [early, lanes_to(wide_attn, hidden_units), lanes_to(head_grads, hidden_units)], axis=0
    )

    packed = plus(packed, lax.ppermute(packed, "ctx", CORE))
    packed = plus(packed, lax.ppermute(packed, "ctx", XSIDE))
    slots = jnp.arange(ADAPT, dtype=jnp.int32)

    def placed(value, which):
        mask = (slots == which).astype(F32).reshape((ADAPT,) + (1,) * value.ndim)
        return mask * value.astype(F32)[None]

    if pair:
        both = jnp.stack([packed, lax.ppermute(packed, "shard", swap_y)])
    else:
        both = lax.psum(placed(packed, slot), "shard")
    (grad_tokens,) = run(
        last_kernel,
        "last",
        (1,),
        at,
        [
            whole(d_all),
            whole(qkv_own),
            whole(qkv_own_x),
            whole(qkv_oth),
            whole(qkv_oth_x),
            (lower_table, (1, 3 * RANK, width), by_slot),
            whole(grad_hidden),
            (inputs, (1, sub, width), z_block),
            whole(gain_attn),
        ],
        [out_whole((sub, width), BF16)],
    )
    up_1 = lax.ppermute(grad_tokens, "tp", RING)
    own_width = width // (shards * 4)
    in_attn = rows_at(both[:, 8 * RANK : 11 * RANK, :width], y * 4 + ctx, own_width, 2)
    in_attn = plus(in_attn, lax.ppermute(in_attn, "tp", Z_XOR[1]))
    up_1, in_attn, both = tie(up_1, in_attn, both)
    up_2 = lax.ppermute(up_1, "tp", RING)
    in_far = lax.ppermute(in_attn, "tp", Z_XOR[2])
    wide = both[:, : 5 * RANK, :width]
    in_ffn = rows_at(wide[:, 3 * RANK :], y * 4 + ctx, own_width, 2)
    rest = jnp.concatenate([both[:, 5 * RANK : 8 * RANK], both[:, 11 * RANK :]], axis=1)
    if pair:
        slots_here = (slot, slot_other)
        rest = sum(placed(rest[i], which) for i, which in enumerate(slots_here))
    quarter_sum, heads = rest[:, : 3 * RANK], rest[:, 3 * RANK :, : 4 * cols]
    grad_b_query = jnp.concatenate([heads[..., :cols], heads[..., 2 * cols : 3 * cols]], axis=-1)
    grad_b_keyval = jnp.stack(
        [
            jnp.concatenate(
                [heads[..., core * 2 * cols + c * HD :][..., :HD] for core in range(2)], axis=-1
            )
            for c in (2, 3)
        ],
        axis=1,
    )
    grad_b_gate_up = quarter_sum[:, : 2 * RANK].reshape(ADAPT, 2, RANK, -1)
    grad_a_down = jnp.swapaxes(quarter_sum[:, 2 * RANK :], 1, 2)
    in_all = jnp.concatenate([plus(in_attn, in_far), in_ffn], axis=1)
    if pair:
        wide = sum(placed(wide[i, : 3 * RANK], which) for i, which in enumerate(slots_here))
        in_all = sum(placed(in_all[i], which) for i, which in enumerate(slots_here))
    else:
        wide, in_all = wide.astype(F32), in_all.astype(F32)
    grad_b_out = wide[:, :RANK]
    grad_a_out = wide[:, RANK : 2 * RANK]
    grad_b_down = wide[:, 2 * RANK : 3 * RANK]
    grad_a_out = jnp.concatenate(
        [rows_at(grad_a_out, z, cols, 2), rows_at(grad_a_out, 4 + z, cols, 2)], axis=2
    )
    grad_a_out = jnp.swapaxes(grad_a_out, 1, 2)
    grad_adapt_in = jnp.swapaxes(in_all, 1, 2)
    up_2, final, grad_b_query, grad_b_keyval, grad_b_gate_up, grad_a_down = tie(
        up_2, final, grad_b_query, grad_b_keyval, grad_b_gate_up, grad_a_down
    )
    up_3 = lax.ppermute(up_2, "tp", RING)
    line = [grad_tokens, up_1, up_2, up_3]
    z_row = lambda i, s: (0, i, 0)
    (grad_inputs,) = run(
        ring_kernel,
        "assemble",
        (4,),
        at,
        [whole(part) for part in line],
        [((1, tok, width), F32, (1, sub, width), z_row)],
    )
    line = [final, out_up_1, out_up_2, out_up_3, out_down_1, out_down_2, out_down_3]
    (result,) = run(
        assemble_kernel,
        "assemble_out",
        (4,),
        at,
        [whole(part) for part in line],
        [((1, tok, width), BF16, (1, sub, width), z_row)],
        cost=LONG,
    )
    return (
        result,
        grad_inputs,
        grad_adapt_in,
        grad_b_query,
        grad_b_keyval,
        grad_b_gate_up,
        grad_a_out,
        grad_b_out,
        grad_a_down,
        grad_b_down,
    )


def solution(mesh):
    return jax.shard_map(
        functools.partial(body, mesh.shape["shard"]),
        mesh=mesh,
        in_specs=(
            P("shard", "ctx", None),
            P("shard", "ctx", None),
            P("shard", None),
            P("shard"),
            P("shard", "tp"),
            P(None, "shard", "tp"),
            P("tp", "shard"),
            P(None, "shard", "tp"),
            P("tp", "shard"),
            P(),
            P(),
            P(),
            P(),
            P(),
            P(None, None, "tp"),
            P(None, None, None, "tp"),
            P(None, None, None, "tp"),
            P(None, "tp", None),
            P(),
            P(None, "tp", None),
            P(),
        ),
        out_specs=(
            P("shard", "ctx", None),
            P("shard", "ctx", None),
            P(None, ("shard", "ctx"), None),
            P(None, None, "tp"),
            P(None, None, None, "tp"),
            P(None, None, None, "tp"),
            P(None, "tp", None),
            P(),
            P(None, "tp", None),
            P(),
        ),
        check_vma=False,
    )
```
